256 devices in a mesh: mem: 8 (over x, core), row: 4 (over z_lo), col: 8 (over y, z_hi).
Axes of the slice: x: 4, y: 4, z: 8 (z_hi: 2, z_lo: 4; z = z_hi * 4 + z_lo), core: 2. Of those that a mesh axis runs over, the one named last changes fastest.
Arguments:
- fields: bfloat16 [32, 16, 256, 256], P('mem', 'row', 'col'), may hold values from -6 to 6
- norm_gain: float32 [256], replicated, may hold values from 0.5 to 1.5
- w_query: bfloat16 [256, 256], replicated, may hold values from -11 to 11
- w_key: bfloat16 [256, 256], replicated, may hold values from -6 to 6
- w_value: bfloat16 [256, 256], replicated, may hold values from -0.375 to 0.375
- w_out: bfloat16 [256, 256], replicated, may hold values from -0.375 to 0.375
- mix_kernel: float32 [3, 3, 256], replicated, may hold values from -1.5 to 1.5
- cotangent: bfloat16 [32, 16, 256, 256], P('mem', 'row', 'col'), may hold values from -6 to 6
Outputs:
- grad_fields: bfloat16 [32, 16, 256, 256], P('mem', 'row', 'col')
- grad_gain: float32 [256], replicated
- grad_query: float32 [256, 256], replicated
- grad_key: float32 [256, 256], replicated
- grad_value: float32 [256, 256], replicated
- grad_out: float32 [256, 256], replicated
- grad_kernel: float32 [3, 3, 256], replicated
The draws below stay inside these ranges and needn't reach their ends.
All inputs are finite; a program needn't handle non-finite values.
Results may differ from the reference program's by a relative error of at most 0.015.
The reference program's roundings to bfloat16 on the way count: a program that leaves them out, or rounds other values in their place, can miss the bound.
Values may be sent and summed in bfloat16 or wider, within the bound.
No kernel may reach another device: no remote copies, remote signals or barrier semaphores. Data moves between devices by JAX's collectives and lax.ppermute only.
A program may use at most 64 MiB of HBM per device.

```python
import math
import jax
import jax.numpy as jnp
from jax import lax

D = 256
HEADS = 8
MEM_DEV = 4
MEMBERS = 32
NR = 16
NC = 256


def shared_basis(key):
    return jnp.clip(jax.random.normal(jax.random.fold_in(key, 11), (D, D), jnp.float32), -4.0, 4.0)


def draw_w_query(key, part):
    jitter = jnp.clip(jax.random.normal(jax.random.fold_in(key, 12), (D, D), jnp.float32), -4.0, 4.0)
    mixed = jitter
    return (mixed / math.sqrt(D)).astype(jnp.bfloat16)


def draw_w_key(key, part):
    basis = shared_basis(key)
    mixed = basis
    return (mixed / math.sqrt(D)).astype(jnp.bfloat16)


def block_scale(own_key, shape, pieces, smallest, high):
    def one(position, parts):
        heights = jax.random.uniform(jax.random.fold_in(jax.random.fold_in(own_key, 6), position), (parts,), jnp.float32, smallest / len(pieces), high / len(pieces))
        return jnp.repeat(jnp.exp(heights), shape[position] // parts).reshape((-1,) + (1,) * (len(shape) - position - 1))

    loudness = one(*pieces[0])
    for cut in pieces[1:]:
        loudness = loudness * one(*cut)
    return loudness


def normal_values(own_key, dims, scale, bound, split=(), kind=jnp.bfloat16):
    values = scale * jax.random.normal(own_key, dims, jnp.float32)
    if split:
        values = values * block_scale(own_key, dims, split, -0.22, 0.18)
    return jnp.clip(values, -bound, bound).astype(kind)


def setup_inputs(seed: int = 0) -> dict:
    key_list = jax.random.split(jax.random.key(seed), 9)
    fields = normal_values(key_list[0], (MEMBERS, NR, NC, D), 1.0, 6.0, ((0, 8), (1, 4), (2, 8)))
    norm_gain = jnp.clip(1.0 + 0.1 * jax.random.normal(key_list[1], (D,), jnp.float32), 0.5, 1.5)
    w_query = draw_w_query(jax.random.fold_in(key_list[8], 71), 0)
    w_key = draw_w_key(jax.random.fold_in(key_list[8], 71), 0)
    w_value = normal_values(key_list[4], (D, D), D ** -0.5, 0.375)
    w_out = normal_values(key_list[5], (D, D), D ** -0.5, 0.375)
    mix_kernel = normal_values(key_list[6], (3, 3, D), 0.3, 1.5, (), jnp.float32)
    cotangent = normal_values(key_list[7], (MEMBERS, NR, NC, D), 1.0, 6.0, ((0, 8), (1, 4), (2, 8)))
    return dict(fields=fields, norm_gain=norm_gain, w_query=w_query, w_key=w_key, w_value=w_value, w_out=w_out, mix_kernel=mix_kernel, cotangent=cotangent)


epsilon = 1e-06

def project(values, weight):
    shape = values.shape
    flat_in = values.reshape(-1, shape[-1])
    return jnp.dot(flat_in, weight, preferred_element_type=jnp.float32).reshape(shape[:-1] + (weight.shape[1],))

def reference(fields, norm_gain, w_query, w_key, w_value, w_out, mix_kernel, cotangent):
    members_all, grid_rows, grid_cols, model_width = fields.shape
    head_dim = model_width // HEADS
    score_scale = 1.0 / math.sqrt(head_dim)
    group_count = members_all // MEM_DEV
    padded_cot = jnp.pad(cotangent, ((0, 0), (1, 1), (1, 1), (0, 0)))
    summed = jnp.zeros(fields.shape, jnp.float32)
    for row_off in range(3):
        for col_off in range(3):
            summed = summed + mix_kernel[row_off, col_off] * padded_cot[:, 2 - row_off:2 - row_off + grid_rows, 2 - col_off:2 - col_off + grid_cols, :].astype(jnp.float32)
    grad_mixed_all = summed.astype(jnp.bfloat16)

    def attend_row(running, row_in):
        row_fields, row_grad_mixed, row_cot = row_in
        col_count = row_fields.shape[1]
        flat_in = row_fields.astype(jnp.float32)
        inv_rms = lax.rsqrt(lax.optimization_barrier(jnp.mean(flat_in * flat_in, axis=-1, keepdims=True)) + epsilon)
        normed = flat_in * inv_rms
        inputs = (normed * norm_gain).astype(jnp.bfloat16)
        queries = project(inputs, w_query).astype(jnp.bfloat16)
        key_proj = project(inputs, w_key).astype(jnp.bfloat16)
        value_proj = project(inputs, w_value).astype(jnp.bfloat16)
        head_shape = (members_all, col_count, HEADS, head_dim)
        query_heads = queries.reshape(head_shape).astype(jnp.float32)
        key_heads = key_proj.reshape(head_shape).astype(jnp.float32)
        value_heads = value_proj.reshape(head_shape).astype(jnp.float32)
        scores = jnp.einsum('mche,nche->chmn', query_heads, key_heads) * score_scale
        row_max = lax.optimization_barrier(jnp.max(scores, axis=-1, keepdims=True))
        lifted = jnp.exp(scores - row_max)
        attn_prob = lifted / lax.optimization_barrier(jnp.sum(lifted, axis=-1, keepdims=True))
        prob_b = attn_prob.astype(jnp.bfloat16).astype(jnp.float32)
        attended = jnp.einsum('chmn,nche->mche', prob_b, value_heads).astype(jnp.bfloat16)
        attended = attended.reshape(members_all, col_count, model_width)
        mixed_row = project(attended, w_out).astype(jnp.bfloat16)
        grad_att = project(row_grad_mixed, w_out.T).astype(jnp.bfloat16)
        grad_heads = grad_att.reshape(head_shape).astype(jnp.float32)
        grad_prob = jnp.einsum('mche,nche->chmn', grad_heads, value_heads)
        inner = lax.optimization_barrier(jnp.sum(attn_prob * grad_prob, axis=-1, keepdims=True))
        grad_score = (attn_prob * (grad_prob - inner) * score_scale).astype(jnp.bfloat16).astype(jnp.float32)
        grad_q = jnp.einsum('chmn,nche->mche', grad_score, key_heads).astype(jnp.bfloat16)
        score_groups = grad_score.reshape(col_count, HEADS, group_count, MEM_DEV, members_all)
        prob_groups = prob_b.reshape(col_count, HEADS, group_count, MEM_DEV, members_all)
        query_groups = query_heads.reshape(group_count, MEM_DEV, col_count, HEADS, head_dim)
        grad_groups = grad_heads.reshape(group_count, MEM_DEV, col_count, HEADS, head_dim)
        part_k = lax.optimization_barrier(jnp.einsum('chgmn,gmche->gnche', score_groups, query_groups).astype(jnp.bfloat16))
        part_v = lax.optimization_barrier(jnp.einsum('chgmn,gmche->gnche', prob_groups, grad_groups).astype(jnp.bfloat16))
        grad_k = lax.optimization_barrier(jnp.sum(part_k.astype(jnp.float32), axis=0)).astype(jnp.bfloat16)
        grad_v = lax.optimization_barrier(jnp.sum(part_v.astype(jnp.float32), axis=0)).astype(jnp.bfloat16)
        flat_shape = (members_all * col_count, model_width)
        grad_q2 = grad_q.reshape(flat_shape)
        grad_k2 = grad_k.reshape(flat_shape)
        grad_v2 = grad_v.reshape(flat_shape)
        inputs2 = inputs.reshape(flat_shape)
        grad_in = jnp.dot(grad_q2, w_query.T, preferred_element_type=jnp.float32) + jnp.dot(grad_k2, w_key.T, preferred_element_type=jnp.float32) + jnp.dot(grad_v2, w_value.T, preferred_element_type=jnp.float32)
        normed2 = normed.reshape(flat_shape)
        grad_normed = grad_in * norm_gain
        inv2 = inv_rms.reshape(-1, 1)
        grad_row = row_cot.reshape(flat_shape).astype(jnp.float32) + inv2 * (grad_normed - normed2 * lax.optimization_barrier(jnp.mean(grad_normed * normed2, axis=-1, keepdims=True)))
        acc_q, acc_k, acc_v, acc_out, acc_gain = running
        acc_q = acc_q + jnp.dot(inputs2.T, grad_q2, preferred_element_type=jnp.float32)
        acc_k = acc_k + jnp.dot(inputs2.T, grad_k2, preferred_element_type=jnp.float32)
        acc_v = acc_v + jnp.dot(inputs2.T, grad_v2, preferred_element_type=jnp.float32)
        acc_out = acc_out + jnp.dot(attended.reshape(flat_shape).T, row_grad_mixed.reshape(flat_shape), preferred_element_type=jnp.float32)
        acc_gain = acc_gain + lax.optimization_barrier(jnp.sum(grad_in * normed2, axis=0))
        outputs = (mixed_row, grad_row.astype(jnp.bfloat16).reshape(members_all, col_count, model_width))
        return ((acc_q, acc_k, acc_v, acc_out, acc_gain), outputs)
    square = jnp.zeros((model_width, model_width), jnp.float32)
    start = (square, square, square, square, jnp.zeros((model_width,), jnp.float32))
    row_inputs = (jnp.moveaxis(fields, 1, 0), jnp.moveaxis(grad_mixed_all, 1, 0), jnp.moveaxis(cotangent, 1, 0))
    running, outputs = lax.scan(attend_row, start, row_inputs)
    mixed_all = jnp.moveaxis(outputs[0], 0, 1)
    grad_fields = jnp.moveaxis(outputs[1], 0, 1)
    scale_all = 1.0 / math.sqrt(members_all * grid_rows * grid_cols)
    kernel_terms = []
    padded_mixed = jnp.pad(mixed_all, ((0, 0), (1, 1), (1, 1), (0, 0)))
    for row_off in range(3):
        for col_off in range(3):
            shifted = padded_mixed[:, row_off:row_off + grid_rows, col_off:col_off + grid_cols, :].astype(jnp.float32)
            kernel_terms.append(lax.optimization_barrier(jnp.sum(shifted * cotangent.astype(jnp.float32), axis=(0, 1, 2))))
    grad_kernel = jnp.stack(kernel_terms).reshape(3, 3, model_width) * scale_all
    acc_q, acc_k, acc_v, acc_out, acc_gain = running
    return (grad_fields, acc_gain * scale_all, acc_q * scale_all, acc_k * scale_all, acc_v * scale_all, acc_out * scale_all, grad_kernel)
```

```python
import functools
import math

import jax
import jax.numpy as jnp
import numpy as np
from jax import lax
from jax.experimental import pallas as pl
from jax.experimental.pallas import tpu as pltpu
from jax.sharding import PartitionSpec as P

HEADS = 8
EPS = 1e-06
BF = jnp.bfloat16
F32 = jnp.float32
NT = (((1,), (1,)), ((), ()))
TN = (((0,), (0,)), ((), ()))


def dot(a, b, dims=None):
    if dims is None:
        return jnp.dot(a, b, preferred_element_type=F32)
    return lax.dot_general(a, b, dims, preferred_element_type=F32)


def split_matrix(parts, members, cols):
    per = cols // parts
    out = np.zeros((parts, per, members, members, cols), np.float32)
    for j in range(parts):
        for c in range(per):
            for m in range(members):
                out[j, c, m, m, j * per + c] = 1
    return out.reshape(parts * per * members, members * cols)


def halo_matrices(parts, members, rows, cols, side):
    per = cols // parts
    mats = []
    for pair in range((rows + 2) // 2):
        out = np.zeros((parts, 2, per + 2, members, 2 * members * cols + 2 * side), np.float32)
        for j in range(parts):
            for q in range(2):
                for c in range(per + 2):
                    for m in range(members):
                        col = j * per + c - 1
                        edge = (2 * pair + q) * members + m
                        if col < 0:
                            src = 2 * members * cols + edge
                        elif col >= cols:
                            src = 2 * members * cols + side + edge
                        else:
                            src = (q * members + m) * cols + col
                        out[j, q, c, m, src] = 1
        mats.append(out.reshape(-1, out.shape[-1]))
    return np.stack(mats)


def gather_matrix(parts, cells, members):
    out = np.zeros((cells, parts, members, parts, cells, members), np.float32)
    for s in range(parts):
        for c in range(cells):
            for m in range(members):
                out[c, s, m, s, c, m] = 1
    return out.reshape(cells * parts * members, -1)


def pack_kernel(fields, cot, before, after, left, right, split, halo, send):
    members, rows, cols, width = fields.shape
    parts = send.shape[0]
    per = cols // parts * members
    for r in range(rows):
        tokens = fields[:, r].reshape(members * cols, width)
        moved = dot(split[...], tokens).astype(BF).reshape(parts, per, width)
        send[:, r * per : (r + 1) * per, :] = moved
    base = rows * per
    lines = [before[...]] + [cot[:, r] for r in range(rows)] + [after[...]]
    lines = [x.reshape(members * cols, width) for x in lines]
    step = 2 * (per + 2 * members)
    for pair in range(halo.shape[0]):
        tokens = jnp.concatenate([lines[2 * pair], lines[2 * pair + 1], left[...], right[...]], axis=0)
        moved = dot(halo[pair], tokens).astype(BF).reshape(parts, step, width)
        send[:, base + pair * step : base + (pair + 1) * step, :] = moved


def main_kernel(
    tile_rows,
    tile_cols,
    recv,
    gain,
    mix,
    wq,
    wk,
    wv,
    wo,
    gather8,
    gather4,
    headsum,
    send,
    padded,
    lhs_a,
    lhs_b,
    mat_k,
    mat_v,
):
    parts, _, width = recv.shape
    head_dim = width // HEADS
    scale = 1.0 / math.sqrt(head_dim)
    cells = tile_rows * tile_cols
    mem_dev = 4
    all_members = parts * mem_dev
    tokens = cells * all_members
    pad_cols = tile_cols + 2
    pad_cells = (tile_rows + 2) * pad_cols
    base = cells * mem_dev

    def regroup(start, count, matrix):
        rows = count * mem_dev
        part = recv[:, start : start + rows, :].reshape(parts * rows, width)
        return dot(matrix[...], part)

    x = jnp.concatenate([regroup(g * 32, 8, gather8) for g in range(cells // 8)], axis=0)
    done = 0
    while done < pad_cells:
        count = 8 if pad_cells - done >= 8 else 4
        block = regroup(base + done * mem_dev, count, gather8 if count == 8 else gather4)
        padded[done : done + count] = block.reshape(count, all_members, width)
        done += count

    def shifted(i, j):
        picked = [
            padded[(r + 2 - i) * pad_cols + 2 - j : (r + 2 - i) * pad_cols + 2 - j + tile_cols]
            for r in range(tile_rows)
        ]
        return jnp.concatenate(picked, axis=0).reshape(tokens, width)

    inv = lax.rsqrt(jnp.mean(x * x, axis=-1, keepdims=True) + EPS)
    normed = x * inv
    inputs = (normed * gain[...]).astype(BF)
    queries = dot(inputs, wq[...]).astype(BF)
    keys = dot(inputs, wk[...]).astype(BF)
    values = dot(inputs, wv[...]).astype(BF)

    conv = jnp.zeros((tokens, width), F32)
    for i in range(3):
        for j in range(3):
            conv = conv + mix[3 * i + j : 3 * i + j + 1, :] * shifted(i, j)
    grad_mixed = conv.astype(BF)
    grad_att = dot(grad_mixed, wo[...], NT).astype(BF)

    row_head = lax.broadcasted_iota(jnp.int32, (width, width), 0) // head_dim
    col_head = lax.broadcasted_iota(jnp.int32, (width, width), 1) // head_dim
    same = row_head == col_head
    lane_head = lax.broadcasted_iota(jnp.int32, (all_members, width), 1) // head_dim

    def expand(block):
        tiled = jnp.concatenate([block] * HEADS, axis=0)
        return jnp.where(same, tiled, jnp.zeros_like(tiled))

    for c in range(cells):
        rows = slice(c * all_members, (c + 1) * all_members)
        mat_k[c] = expand(keys[rows])
        mat_v[c] = expand(values[rows])
    for c in range(cells):
        rows = slice(c * all_members, (c + 1) * all_members)
        lhs_a[rows, :] = dot(queries[rows], mat_k[c], NT)
        lhs_b[rows, :] = dot(grad_att[rows], mat_v[c], NT)

    scores = lhs_a[...] * scale
    lane = lax.broadcasted_iota(jnp.int32, (tokens, 128), 1)
    halves = []
    for h in range(width // 128):
        top = scores[:, h * 128 : (h + 1) * 128]
        step = 1
        while step < all_members:
            up = pltpu.roll(top, step, 1)
            down = pltpu.roll(top, 128 - step, 1)
            top = jnp.maximum(top, jnp.where((lane & step) != 0, up, down))
            step *= 2
        halves.append(top)
    lifted = jnp.exp(scores - jnp.concatenate(halves, axis=1))

    def head_sums(v):
        hi = v.astype(BF)
        lo = (v - hi.astype(F32)).astype(BF)
        return dot(hi, headsum[...]) + dot(lo, headsum[...])

    prob = lifted / head_sums(lifted)
    prob_b = prob.astype(BF)
    grad_prob = lhs_b[...]
    inner = head_sums(prob * grad_prob)
    grad_score = (prob * (grad_prob - inner) * scale).astype(BF)

    att_l, gq_l, gk_l, gv_l = [], [], [], []

    def diagonal(full):
        out = jnp.zeros((all_members, width), F32)
        for h in range(HEADS):
            out = jnp.where(lane_head == h, full[h * all_members : (h + 1) * all_members], out)
        return out

    for c in range(cells):
        rows = slice(c * all_members, (c + 1) * all_members)
        att_l.append(dot(prob_b[rows], mat_v[c]).astype(BF))
        gq_l.append(dot(grad_score[rows], mat_k[c]).astype(BF))
        gk_l.append(diagonal(dot(grad_score[rows], queries[rows], TN)).astype(BF))
        gv_l.append(diagonal(dot(prob_b[rows], grad_att[rows], TN)).astype(BF))
    attended = jnp.concatenate(att_l, axis=0)
    grad_q = jnp.concatenate(gq_l, axis=0)
    grad_k = jnp.concatenate(gk_l, axis=0)
    grad_v = jnp.concatenate(gv_l, axis=0)

    mixed = dot(attended, wo[...]).astype(BF).astype(F32)
    extra = []
    for i in range(3):
        for j in range(3):
            extra.append(jnp.sum(mixed * shifted(i, j), axis=0, keepdims=True))

    grad_in = dot(grad_q, wq[...], NT) + dot(grad_k, wk[...], NT) + dot(grad_v, wv[...], NT)
    extra.append(jnp.sum(grad_in * normed, axis=0, keepdims=True))
    grad_normed = grad_in * gain[...]
    mean = jnp.mean(grad_normed * normed, axis=-1, keepdims=True)
    grad = (shifted(1, 1) + inv * (grad_normed - normed * mean)).astype(BF)
    for g in range(cells // 8):
        back = dot(gather8[...], grad[g * 256 : (g + 1) * 256], TN).astype(BF)
        send[:, g * 32 : (g + 1) * 32, :] = back.reshape(parts, 32, width)

    weights = [
        dot(inputs, grad_q, TN),
        dot(inputs, grad_k, TN),
        dot(inputs, grad_v, TN),
        dot(attended, grad_mixed, TN),
    ]
    shard = 4 * width // parts
    for j in range(parts):
        which, start = divmod(j * shard, width)
        send[j, base : base + shard, :] = weights[which][start : start + shard].astype(BF)
    extras = jnp.concatenate(extra + [jnp.zeros((16 - len(extra), width), F32)], axis=0).astype(BF)
    for j in range(parts):
        send[j, base + shard : base + shard + 16, :] = extras


def unpack_kernel(base, shard, recv, split, out, total):
    members, rows, cols, width = out.shape
    parts = recv.shape[0]
    per = cols // parts * members
    for r in range(rows):
        tokens = recv[:, r * per : (r + 1) * per, :].reshape(parts * per, width)
        out[:, r] = dot(split[...], tokens, TN).astype(BF).reshape(members, cols, width)
    acc = recv[0, base:, :].astype(F32)
    for j in range(1, parts):
        acc = acc + recv[j, base:, :].astype(F32)
    total[...] = acc


def ring(axis, step):
    size = lax.axis_size(axis)
    return [(i, (i + step) % size) for i in range(size)]


def edges(first, last, axis):
    before = lax.ppermute(last, axis, ring(axis, 1))
    after = lax.ppermute(first, axis, ring(axis, -1))
    place, size = lax.axis_index(axis), lax.axis_size(axis)
    zero = jnp.zeros_like(before)
    return jnp.where(place > 0, before, zero), jnp.where(place < size - 1, after, zero)


def local(fields, norm_gain, w_query, w_key, w_value, w_out, mix_kernel, cotangent):
    members, rows, cols, width = fields.shape
    parts = lax.axis_size("mem")
    per = cols // parts
    cells = rows * per
    pad_cells = (rows + 2) * (per + 2)
    params = pltpu.CompilerParams(vmem_limit_bytes=60 * 1024 * 1024)

    with jax.named_scope("halo"):
        before, after = edges(cotangent[:, 0], cotangent[:, rows - 1], "row")

        def column(c):
            parts_c = [before[None, :, c], jnp.swapaxes(cotangent[:, :, c], 0, 1), after[None, :, c]]
            flat = jnp.concatenate(parts_c, axis=0).reshape((rows + 2) * members, width)
            return jnp.pad(flat, ((0, 32 - flat.shape[0]), (0, 0)))

        left, right = edges(column(0), column(cols - 1), "col")

    split = jnp.asarray(split_matrix(parts, members, cols), BF)
    halo = jnp.asarray(halo_matrices(parts, members, rows, cols, 32), BF)
    with jax.named_scope("pack"):
        send = pl.pallas_call(
            pack_kernel,
            out_shape=jax.ShapeDtypeStruct((parts, (cells + pad_cells) * members, width), BF),
            compiler_params=params,
        )(fields, cotangent, before, after, left, right, split, halo)
    with jax.named_scope("to_cells"):
        recv = lax.all_to_all(send, "mem", 0, 0)

    tokens = cells * members * parts
    base = cells * members
    shard = 4 * width // parts
    headsum = np.kron(np.eye(HEADS), np.ones((width // HEADS, width // HEADS)))
    with jax.named_scope("attention"):
        back = pl.pallas_call(
            functools.partial(main_kernel, rows, per),
            out_shape=jax.ShapeDtypeStruct((parts, base + shard + 16, width), BF),
            scratch_shapes=[
                pltpu.VMEM((pad_cells, members * parts, width), F32),
                pltpu.VMEM((tokens, width), F32),
                pltpu.VMEM((tokens, width), F32),
                pltpu.VMEM((cells, width, width), BF),
                pltpu.VMEM((cells, width, width), BF),
            ],
            compiler_params=params,
        )(
            recv,
            norm_gain.reshape(1, width),
            mix_kernel.reshape(9, width),
            w_query,
            w_key,
            w_value,
            w_out,
            jnp.asarray(gather_matrix(parts, 8, members), BF),
            jnp.asarray(gather_matrix(parts, 4, members), BF),
            jnp.asarray(headsum, BF),
        )
    with jax.named_scope("to_members"):
        landed = lax.all_to_all(back, "mem", 0, 0)
    with jax.named_scope("unpack"):
        grad_fields, total = pl.pallas_call(
            functools.partial(unpack_kernel, base, shard),
            out_shape=(
                jax.ShapeDtypeStruct(fields.shape, BF),
                jax.ShapeDtypeStruct((shard + 16, width), F32),
            ),
            compiler_params=params,
        )(landed, split)

    with jax.named_scope("reduce"):
        grid = lax.axis_size("row") * lax.axis_size("col")
        deep = shard // grid
        extras = jnp.pad(total[shard:], ((0, grid - 16), (0, 0))).reshape(grid, 1, width)
        chunk = jnp.concatenate([total[:shard].reshape(grid, deep, width), extras], axis=1)
        chunk = jnp.pad(chunk.astype(BF), ((0, 0), (0, -(deep + 1) % 8), (0, 0)))
        got = lax.all_to_all(chunk, ("row", "col"), 0, 0)
        mine = jnp.sum(got.astype(F32), axis=0, keepdims=True).astype(BF)
        all_got = lax.all_to_all(jnp.broadcast_to(mine, chunk.shape), ("row", "col"), 0, 0)
        piece = all_got[:, :deep].reshape(shard, width)
        extras = all_got[:10, deep].astype(F32)
        pieces = lax.all_gather(piece, "mem", axis=0, tiled=True)

    token_total = parts * members * rows * cols * grid
    scale_all = 1.0 / math.sqrt(token_total)
    grads = pieces.astype(F32) * scale_all
    extras = extras * scale_all
    return (
        grad_fields,
        extras[9],
        grads[:width],
        grads[width : 2 * width],
        grads[2 * width : 3 * width],
        grads[3 * width :],
        extras[:9].reshape(3, 3, width),
    )


def solution(mesh):
    tile = P("mem", "row", "col", None)
    in_specs = (tile, P(), P(), P(), P(), P(), P(), tile)
    out_specs = (tile, P(), P(), P(), P(), P(), P())
    return jax.shard_map(local, mesh=mesh, in_specs=in_specs, out_specs=out_specs, check_vma=False)
```

```python
import functools
import math

import jax
import jax.numpy as jnp
import numpy as np
from jax import lax
from jax.experimental import pallas as pl
from jax.experimental.pallas import tpu as pltpu
from jax.sharding import PartitionSpec as P

HEADS = 8
EPS = 1e-06
BF = jnp.bfloat16
F32 = jnp.float32
NT = (((1,), (1,)), ((), ()))
TN = (((0,), (0,)), ((), ()))


def dot(a, b, dims=None):
    if dims is None:
        return jnp.dot(a, b, preferred_element_type=F32)
    return lax.dot_general(a, b, dims, preferred_element_type=F32)


def split_matrix(parts, members, cols):
    per = cols // parts
    out = np.zeros((parts, per, members, members, cols), np.float32)
    for j in range(parts):
        for c in range(per):
            for m in range(members):
                out[j, c, m, m, j * per + c] = 1
    return out.reshape(parts * per * members, members * cols)


def halo_matrices(parts, members, rows, cols, side):
    per = cols // parts
    mats = []
    for pair in range((rows + 2) // 2):
        out = np.zeros((parts, 2, per + 2, members, 2 * members * cols + 2 * side), np.float32)
        for j in range(parts):
            for q in range(2):
                for c in range(per + 2):
                    for m in range(members):
                        col = j * per + c - 1
                        edge = (2 * pair + q) * members + m
                        if col < 0:
                            src = 2 * members * cols + edge
                        elif col >= cols:
                            src = 2 * members * cols + side + edge
                        else:
                            src = (q * members + m) * cols + col
                        out[j, q, c, m, src] = 1
        mats.append(out.reshape(-1, out.shape[-1]))
    return np.stack(mats)


def gather_matrix(parts, cells, members):
    out = np.zeros((cells, parts, members, parts, cells, members), np.float32)
    for s in range(parts):
        for c in range(cells):
            for m in range(members):
                out[c, s, m, s, c, m] = 1
    return out.reshape(cells * parts * members, -1)


def pack_kernel(fields, cot, before, after, left, right, split, halo, send):
    members, rows, cols, width = fields.shape
    parts = send.shape[0]
    per = cols // parts * members
    for r in range(rows):
        tokens = fields[:, r].reshape(members * cols, width)
        moved = dot(split[...], tokens).astype(BF).reshape(parts, per, width)
        send[:, r * per : (r + 1) * per, :] = moved
    base = rows * per
    lines = [before[...]] + [cot[:, r] for r in range(rows)] + [after[...]]
    lines = [x.reshape(members * cols, width) for x in lines]
    step = 2 * (per + 2 * members)
    for pair in range(halo.shape[0]):
        tokens = jnp.concatenate([lines[2 * pair], lines[2 * pair + 1], left[...], right[...]], axis=0)
        moved = dot(halo[pair], tokens).astype(BF).reshape(parts, step, width)
        send[:, base + pair * step : base + (pair + 1) * step, :] = moved


def main_kernel(
    tile_rows,
    tile_cols,
    recv,
    gain,
    mix,
    wq,
    wk,
    wv,
    wo,
    gather8,
    gather4,
    headsum,
    send,
    padded,
    lhs_a,
    lhs_b,
    mat_k,
    mat_v,
):
    parts, _, width = recv.shape
    head_dim = width // HEADS
    scale = 1.0 / math.sqrt(head_dim)
    cells = tile_rows * tile_cols
    mem_dev = 4
    all_members = parts * mem_dev
    tokens = cells * all_members
    pad_cols = tile_cols + 2
    pad_cells = (tile_rows + 2) * pad_cols
    base = cells * mem_dev

    def regroup(start, count, matrix):
        rows = count * mem_dev
        part = recv[:, start : start + rows, :].reshape(parts * rows, width)
        return dot(matrix[...], part)

    x = jnp.concatenate([regroup(g * 32, 8, gather8) for g in range(cells // 8)], axis=0)
    done = 0
    while done < pad_cells:
        count = 8 if pad_cells - done >= 8 else 4
        block = regroup(base + done * mem_dev, count, gather8 if count == 8 else gather4)
        padded[done : done + count] = block.reshape(count, all_members, width)
        done += count

    def shifted(i, j):
        picked = [
            padded[(r + 2 - i) * pad_cols + 2 - j : (r + 2 - i) * pad_cols + 2 - j + tile_cols]
            for r in range(tile_rows)
        ]
        return jnp.concatenate(picked, axis=0).reshape(tokens, width)

    inv = lax.rsqrt(jnp.mean(x * x, axis=-1, keepdims=True) + EPS)
    normed = x * inv
    inputs = (normed * gain[...]).astype(BF)
    queries = dot(inputs, wq[...]).astype(BF)
    keys = dot(inputs, wk[...]).astype(BF)
    values = dot(inputs, wv[...]).astype(BF)

    conv = jnp.zeros((tokens, width), F32)
    for i in range(3):
        for j in range(3):
            conv = conv + mix[i, j : j + 1, :] * shifted(i, j)
    grad_mixed = conv.astype(BF)
    grad_att = dot(grad_mixed, wo[...], NT).astype(BF)

    row_head = lax.broadcasted_iota(jnp.int32, (width, width), 0) // head_dim
    col_head = lax.broadcasted_iota(jnp.int32, (width, width), 1) // head_dim
    same = row_head == col_head
    lane_head = lax.broadcasted_iota(jnp.int32, (all_members, width), 1) // head_dim

    def expand(block):
        tiled = jnp.concatenate([block] * HEADS, axis=0)
        return jnp.where(same, tiled, jnp.zeros_like(tiled))

    for c in range(cells):
        rows = slice(c * all_members, (c + 1) * all_members)
        mat_k[c] = expand(keys[rows])
        mat_v[c] = expand(values[rows])
    for c in range(cells):
        rows = slice(c * all_members, (c + 1) * all_members)
        lhs_a[rows, :] = dot(queries[rows], mat_k[c], NT)
        lhs_b[rows, :] = dot(grad_att[rows], mat_v[c], NT)

    scores = lhs_a[...] * scale
    lane = lax.broadcasted_iota(jnp.int32, (tokens, 128), 1)
    halves = []
    for h in range(width // 128):
        top = scores[:, h * 128 : (h + 1) * 128]
        step = 1
        while step < all_members:
            up = pltpu.roll(top, step, 1)
            down = pltpu.roll(top, 128 - step, 1)
            top = jnp.maximum(top, jnp.where((lane & step) != 0, up, down))
            step *= 2
        halves.append(top)
    lifted = jnp.exp(scores - jnp.concatenate(halves, axis=1))

    def head_sums(v):
        hi = v.astype(BF)
        lo = (v - hi.astype(F32)).astype(BF)
        return dot(hi, headsum[...]) + dot(lo, headsum[...])

    prob = lifted / head_sums(lifted)
    prob_b = prob.astype(BF)
    grad_prob = lhs_b[...]
    inner = head_sums(prob * grad_prob)
    grad_score = (prob * (grad_prob - inner) * scale).astype(BF)

    att_l, gq_l, gk_l, gv_l = [], [], [], []

    def diagonal(full):
        out = jnp.zeros((all_members, width), F32)
        for h in range(HEADS):
            out = jnp.where(lane_head == h, full[h * all_members : (h + 1) * all_members], out)
        return out

    for c in range(cells):
        rows = slice(c * all_members, (c + 1) * all_members)
        att_l.append(dot(prob_b[rows], mat_v[c]).astype(BF))
        gq_l.append(dot(grad_score[rows], mat_k[c]).astype(BF))
        gk_l.append(diagonal(dot(grad_score[rows], queries[rows], TN)).astype(BF))
        gv_l.append(diagonal(dot(prob_b[rows], grad_att[rows], TN)).astype(BF))
    attended = jnp.concatenate(att_l, axis=0)
    grad_q = jnp.concatenate(gq_l, axis=0)
    grad_k = jnp.concatenate(gk_l, axis=0)
    grad_v = jnp.concatenate(gv_l, axis=0)

    mixed = dot(attended, wo[...]).astype(BF).astype(F32)
    extra = []
    for i in range(3):
        for j in range(3):
            extra.append(jnp.sum(mixed * shifted(i, j), axis=0, keepdims=True))

    grad_in = dot(grad_q, wq[...], NT) + dot(grad_k, wk[...], NT) + dot(grad_v, wv[...], NT)
    extra.append(jnp.sum(grad_in * normed, axis=0, keepdims=True))
    grad_normed = grad_in * gain[...]
    mean = jnp.mean(grad_normed * normed, axis=-1, keepdims=True)
    grad = (shifted(1, 1) + inv * (grad_normed - normed * mean)).astype(BF)
    for g in range(cells // 8):
        back = dot(gather8[...], grad[g * 256 : (g + 1) * 256], TN).astype(BF)
        send[:, g * 32 : (g + 1) * 32, :] = back.reshape(parts, 32, width)

    weights = [
        dot(inputs, grad_q, TN),
        dot(inputs, grad_k, TN),
        dot(inputs, grad_v, TN),
        dot(attended, grad_mixed, TN),
    ]
    shard = 4 * width // parts
    for j in range(parts):
        which, start = divmod(j * shard, width)
        send[j, base : base + shard, :] = weights[which][start : start + shard].astype(BF)
    extras = jnp.concatenate(extra + [jnp.zeros((16 - len(extra), width), F32)], axis=0).astype(BF)
    for j in range(parts):
        send[j, base + shard : base + shard + 16, :] = extras


def unpack_kernel(base, shard, recv, split, out, total):
    members, rows, cols, width = out.shape
    parts = recv.shape[0]
    per = cols // parts * members
    for r in range(rows):
        tokens = recv[:, r * per : (r + 1) * per, :].reshape(parts * per, width)
        out[:, r] = dot(split[...], tokens, TN).astype(BF).reshape(members, cols, width)
    acc = recv[0, base:, :].astype(F32)
    for j in range(1, parts):
        acc = acc + recv[j, base:, :].astype(F32)
    total[...] = acc.astype(BF)


def finish_kernel(scale, place, same_core, other_core, extras, g_q, g_k, g_v, g_o, g_mix, g_gain):
    count, shard, width = same_core.shape
    per = width // shard
    outs = (g_q, g_k, g_v, g_o)
    for p in range(2 * count):
        code = lax.bitwise_xor(place[0], p)
        spot = lax.shift_right_logical(code, 1)
        got = jnp.where(code == 2 * spot, same_core[spot], other_core[spot]).astype(F32)
        outs[p // per][p % per * shard : (p % per + 1) * shard, :] = got * scale
    rest = extras[...].astype(F32) * scale
    for i in range(3):
        g_mix[i] = rest[3 * i : 3 * i + 3]
    g_gain[...] = rest[9:10]


def partner(axis, code):
    return [(i, i ^ code) for i in range(lax.axis_size(axis))]


def meet(values, axis, codes):
    got = [values] + [lax.ppermute(values, axis, partner(axis, k)) for k in codes]
    got = [x.astype(F32) for x in got]
    while len(got) > 1:
        got = [a + b for a, b in zip(got[::2], got[1::2])]
    return lax.optimization_barrier(got[0].astype(BF))


def ring(axis, step):
    size = lax.axis_size(axis)
    return [(i, (i + step) % size) for i in range(size)]


def edges(first, last, axis):
    before = lax.ppermute(last, axis, ring(axis, 1))
    after = lax.ppermute(first, axis, ring(axis, -1))
    place, size = lax.axis_index(axis), lax.axis_size(axis)
    zero = jnp.zeros_like(before)
    return jnp.where(place > 0, before, zero), jnp.where(place < size - 1, after, zero)


def local(fields, norm_gain, w_query, w_key, w_value, w_out, mix_kernel, cotangent):
    members, rows, cols, width = fields.shape
    parts = lax.axis_size("mem")
    per = cols // parts
    cells = rows * per
    pad_cells = (rows + 2) * (per + 2)
    params = pltpu.CompilerParams(vmem_limit_bytes=60 * 1024 * 1024)

    with jax.named_scope("halo"):
        before, after = edges(cotangent[:, 0], cotangent[:, rows - 1], "row")

        def column(c):
            parts_c = [before[None, :, c], jnp.swapaxes(cotangent[:, :, c], 0, 1), after[None, :, c]]
            flat = jnp.concatenate(parts_c, axis=0).reshape((rows + 2) * members, width)
            return jnp.pad(flat, ((0, 32 - flat.shape[0]), (0, 0)))

        left, right = edges(column(0), column(cols - 1), "col")

    split = jnp.asarray(split_matrix(parts, members, cols), BF)
    halo = jnp.asarray(halo_matrices(parts, members, rows, cols, 32), BF)
    with jax.named_scope("pack"):
        send = pl.pallas_call(
            pack_kernel,
            out_shape=jax.ShapeDtypeStruct((parts, (cells + pad_cells) * members, width), BF),
            compiler_params=params,
        )(fields, cotangent, before, after, left, right, split, halo)
    with jax.named_scope("to_cells"):
        recv = lax.all_to_all(send, "mem", 0, 0)

    tokens = cells * members * parts
    base = cells * members
    shard = 4 * width // parts
    headsum = np.kron(np.eye(HEADS), np.ones((width // HEADS, width // HEADS)))
    with jax.named_scope("attention"):
        back = pl.pallas_call(
            functools.partial(main_kernel, rows, per),
            out_shape=jax.ShapeDtypeStruct((parts, base + shard + 16, width), BF),
            scratch_shapes=[
                pltpu.VMEM((pad_cells, members * parts, width), F32),
                pltpu.VMEM((tokens, width), F32),
                pltpu.VMEM((tokens, width), F32),
                pltpu.VMEM((cells, width, width), BF),
                pltpu.VMEM((cells, width, width), BF),
            ],
            compiler_params=params,
        )(
            recv,
            norm_gain.reshape(1, width),
            mix_kernel,
            w_query,
            w_key,
            w_value,
            w_out,
            jnp.asarray(gather_matrix(parts, 8, members), BF),
            jnp.asarray(gather_matrix(parts, 4, members), BF),
            jnp.asarray(headsum, BF),
        )
    with jax.named_scope("to_members"):
        landed = lax.all_to_all(back, "mem", 0, 0)
    with jax.named_scope("unpack"):
        grad_fields, total = pl.pallas_call(
            functools.partial(unpack_kernel, base, shard),
            out_shape=(
                jax.ShapeDtypeStruct(fields.shape, BF),
                jax.ShapeDtypeStruct((shard + 16, width), BF),
            ),
            compiler_params=params,
        )(landed, split)

    with jax.named_scope("reduce"):
        total = meet(total, "row", (1, 2, 3))
        total = meet(total, "col", (2, 4, 6))
        total = meet(total, "col", (1,))
        piece = total[:shard]
        same_core = jnp.stack([piece] + [lax.ppermute(piece, "mem", partner("mem", k)) for k in (2, 4, 6)])
        same_core = lax.optimization_barrier(same_core)
        other_core = lax.ppermute(same_core, "mem", partner("mem", 1))

    grid = lax.axis_size("row") * lax.axis_size("col")
    scale_all = 1.0 / math.sqrt(tokens * grid * parts)
    with jax.named_scope("finish"):
        square = jax.ShapeDtypeStruct((width, width), F32)
        place = lax.axis_index("mem").astype(jnp.int32).reshape(1)
        grads = pl.pallas_call(
            functools.partial(finish_kernel, scale_all),
            in_specs=[pl.BlockSpec(memory_space=pltpu.SMEM)] + [pl.BlockSpec(memory_space=pltpu.VMEM)] * 3,
            out_shape=(square,) * 4 + (jax.ShapeDtypeStruct((3, 3, width), F32), jax.ShapeDtypeStruct((1, width), F32)),
            compiler_params=params,
        )(place, same_core, other_core, total[shard:])
    return (grad_fields, grads[5].reshape(width)) + tuple(grads[:5])


def solution(mesh):
    tile = P("mem", "row", "col", None)
    in_specs = (tile, P(), P(), P(), P(), P(), P(), tile)
    out_specs = (tile, P(), P(), P(), P(), P(), P())
    return jax.shard_map(local, mesh=mesh, in_specs=in_specs, out_specs=out_specs, check_vma=False)
```

```python
import functools
import math

import jax
import jax.numpy as jnp
import numpy as np
from jax import lax
from jax.experimental import pallas as pl
from jax.experimental.pallas import tpu as pltpu
from jax.sharding import PartitionSpec as P

HEADS = 8
EPS = 1e-06
BF = jnp.bfloat16
F32 = jnp.float32
NT = (((1,), (1,)), ((), ()))
TN = (((0,), (0,)), ((), ()))


def dot(a, b, dims=None):
    if dims is None:
        return jnp.dot(a, b, preferred_element_type=F32)
    return lax.dot_general(a, b, dims, preferred_element_type=F32)


def split_matrix(parts, members, cols):
    per = cols // parts
    out = np.zeros((parts, per, members, members, cols), np.float32)
    for j in range(parts):
        for c in range(per):
            for m in range(members):
                out[j, c, m, m, j * per + c] = 1
    return out.reshape(parts * per * members, members * cols)


def halo_matrices(parts, members, rows, cols, side):
    per = cols // parts
    mats = []
    for pair in range((rows + 2) // 2):
        out = np.zeros((parts, 2, per + 2, members, 2 * members * cols + 2 * side), np.float32)
        for j in range(parts):
            for q in range(2):
                for c in range(per + 2):
                    for m in range(members):
                        col = j * per + c - 1
                        edge = (2 * pair + q) * members + m
                        if col < 0:
                            src = 2 * members * cols + edge
                        elif col >= cols:
                            src = 2 * members * cols + side + edge
                        else:
                            src = (q * members + m) * cols + col
                        out[j, q, c, m, src] = 1
        mats.append(out.reshape(-1, out.shape[-1]))
    return np.stack(mats)


def gather_matrix(parts, cells, members):
    out = np.zeros((cells, parts, members, parts, cells, members), np.float32)
    for s in range(parts):
        for c in range(cells):
            for m in range(members):
                out[c, s, m, s, c, m] = 1
    return out.reshape(cells * parts * members, -1)


def pack_fields_kernel(fields, split, send):
    members, rows, cols, width = fields.shape
    parts = send.shape[0]
    per = cols // parts * members
    for r in range(rows):
        tokens = fields[:, r].reshape(members * cols, width)
        moved = dot(split[...], tokens).astype(BF).reshape(parts, per, width)
        send[:, r * per : (r + 1) * per, :] = moved


def pack_cot_kernel(inside, cot, before, after, left, right, halo, send):
    members, rows, cols, width = cot.shape
    parts = send.shape[0]
    per = cols // parts * members
    lines = [before[...]] + [cot[:, r] for r in range(rows)] + [after[...]]
    lines = [x.reshape(members * cols, width) for x in lines]
    sides = [jnp.where(inside[i] > 0, x[...], jnp.zeros_like(x[...])) for i, x in enumerate((left, right))]
    step = 2 * (per + 2 * members)
    for pair in range(halo.shape[0]):
        tokens = jnp.concatenate([lines[2 * pair], lines[2 * pair + 1]] + sides, axis=0)
        moved = dot(halo[pair], tokens).astype(BF).reshape(parts, step, width)
        send[:, pair * step : (pair + 1) * step, :] = moved


def regroup(recv, start, count, members, matrix):
    parts, _, width = recv.shape
    rows = count * members
    return dot(matrix[...], recv[:, start : start + rows, :].reshape(parts * rows, width))


def norm(x):
    inv = lax.rsqrt(jnp.mean(x * x, axis=-1, keepdims=True) + EPS)
    return inv, x * inv


def head_sums(v, headsum):
    hi = v.astype(BF)
    lo = (v - hi.astype(F32)).astype(BF)
    return dot(hi, headsum[...]) + dot(lo, headsum[...])


def expand_all(blocks, mats):
    cells, width, _ = mats.shape
    size = blocks.shape[0] // cells
    head_dim = width // HEADS
    row_head = lax.broadcasted_iota(jnp.int32, (width, width), 0) // head_dim
    col_head = lax.broadcasted_iota(jnp.int32, (width, width), 1) // head_dim
    same = row_head == col_head
    for c in range(cells):
        tiled = jnp.concatenate([blocks[c * size : (c + 1) * size]] * HEADS, axis=0)
        mats[c] = jnp.where(same, tiled, jnp.zeros_like(tiled))


def forward_kernel(
    members,
    recv,
    gain,
    wq,
    wk,
    wv,
    wo,
    gather8,
    headsum,
    x_out,
    q_out,
    k_out,
    v_out,
    prob_out,
    att_out,
    mixed_out,
    sums,
    mat_k,
    mat_v,
):
    parts, _, width = recv.shape
    scale = 1.0 / math.sqrt(width // HEADS)
    all_members = parts * members
    tokens = x_out.shape[0]
    cells = tokens // all_members
    x = jnp.concatenate([regroup(recv, g * 32, 8, members, gather8) for g in range(cells // 8)], axis=0)
    x_out[...] = x.astype(BF)
    _, normed = norm(x)
    inputs = (normed * gain[...]).astype(BF)
    queries = dot(inputs, wq[...]).astype(BF)
    keys = dot(inputs, wk[...]).astype(BF)
    values = dot(inputs, wv[...]).astype(BF)
    q_out[...] = queries
    k_out[...] = keys
    v_out[...] = values
    expand_all(keys, mat_k)
    expand_all(values, mat_v)
    for c in range(cells):
        rows = slice(c * all_members, (c + 1) * all_members)
        sums[rows, :] = dot(queries[rows], mat_k[c], NT)
    scores = sums[...] * scale
    lane = lax.broadcasted_iota(jnp.int32, (tokens, 128), 1)
    halves = []
    for h in range(width // 128):
        top = scores[:, h * 128 : (h + 1) * 128]
        step = 1
        while step < all_members:
            up = pltpu.roll(top, step, 1)
            down = pltpu.roll(top, 128 - step, 1)
            top = jnp.maximum(top, jnp.where((lane & step) != 0, up, down))
            step *= 2
        halves.append(top)
    lifted = jnp.exp(scores - jnp.concatenate(halves, axis=1))
    prob = lifted / head_sums(lifted, headsum)
    prob_out[...] = prob
    prob_b = prob.astype(BF)
    for c in range(cells):
        rows = slice(c * all_members, (c + 1) * all_members)
        att_out[rows, :] = dot(prob_b[rows], mat_v[c]).astype(BF)
    mixed_out[...] = dot(att_out[...], wo[...]).astype(BF)


def backward_kernel(
    tile_rows,
    tile_cols,
    members,
    recv,
    x_in,
    q_in,
    k_in,
    v_in,
    prob_in,
    att_in,
    mixed_in,
    gain,
    mix,
    wq,
    wk,
    wv,
    wo,
    gather8,
    gather4,
    headsum,
    send,
    padded,
    sums,
    mat_k,
    mat_v,
):
    parts, _, width = recv.shape
    head_dim = width // HEADS
    scale = 1.0 / math.sqrt(head_dim)
    cells = tile_rows * tile_cols
    all_members = parts * members
    tokens = cells * all_members
    pad_cols = tile_cols + 2
    pad_cells = (tile_rows + 2) * pad_cols
    done = 0
    while done < pad_cells:
        count = 8 if pad_cells - done >= 8 else 4
        block = regroup(recv, done * members, count, members, gather8 if count == 8 else gather4)
        padded[done : done + count] = block.reshape(count, all_members, width)
        done += count

    def shifted(i, j):
        picked = [
            padded[(r + 2 - i) * pad_cols + 2 - j : (r + 2 - i) * pad_cols + 2 - j + tile_cols]
            for r in range(tile_rows)
        ]
        return jnp.concatenate(picked, axis=0).reshape(tokens, width)

    expand_all(k_in[...], mat_k)
    expand_all(v_in[...], mat_v)
    inv, normed = norm(x_in[...].astype(F32))
    inputs = (normed * gain[...]).astype(BF)
    mixed = mixed_in[...].astype(F32)
    extra = []
    conv = jnp.zeros((tokens, width), F32)
    for i in range(3):
        for j in range(3):
            moved = shifted(i, j)
            conv = conv + mix[i, j : j + 1, :] * moved
            extra.append(jnp.sum(mixed * moved, axis=0, keepdims=True))
    grad_mixed = conv.astype(BF)
    grad_att = dot(grad_mixed, wo[...], NT).astype(BF)
    for c in range(cells):
        rows = slice(c * all_members, (c + 1) * all_members)
        sums[rows, :] = dot(grad_att[rows], mat_v[c], NT)

    prob = prob_in[...]
    prob_b = prob.astype(BF)
    grad_prob = sums[...]
    inner = head_sums(prob * grad_prob, headsum)
    grad_score = (prob * (grad_prob - inner) * scale).astype(BF)
    lane_head = lax.broadcasted_iota(jnp.int32, (all_members, width), 1) // head_dim

    def diagonal(full):
        out = jnp.zeros((all_members, width), F32)
        for h in range(HEADS):
            out = jnp.where(lane_head == h, full[h * all_members : (h + 1) * all_members], out)
        return out

    gq_l, gk_l, gv_l = [], [], []
    for c in range(cells):
        rows = slice(c * all_members, (c + 1) * all_members)
        gq_l.append(dot(grad_score[rows], mat_k[c]).astype(BF))
        gk_l.append(diagonal(dot(grad_score[rows], q_in[rows, :], TN)).astype(BF))
        gv_l.append(diagonal(dot(prob_b[rows], grad_att[rows], TN)).astype(BF))
    grad_q = jnp.concatenate(gq_l, axis=0)
    grad_k = jnp.concatenate(gk_l, axis=0)
    grad_v = jnp.concatenate(gv_l, axis=0)

    grad_in = dot(grad_q, wq[...], NT) + dot(grad_k, wk[...], NT) + dot(grad_v, wv[...], NT)
    extra.append(jnp.sum(grad_in * normed, axis=0, keepdims=True))
    grad_normed = grad_in * gain[...]
    mean = jnp.mean(grad_normed * normed, axis=-1, keepdims=True)
    grad = (shifted(1, 1) + inv * (grad_normed - normed * mean)).astype(BF)
    for g in range(cells // 8):
        back = dot(gather8[...], grad[g * 256 : (g + 1) * 256], TN).astype(BF)
        send[:, g * 32 : (g + 1) * 32, :] = back.reshape(parts, 32, width)

    weights = [
        dot(inputs, grad_q, TN),
        dot(inputs, grad_k, TN),
        dot(inputs, grad_v, TN),
        dot(att_in[...], grad_mixed, TN),
    ]
    base = cells * members
    shard = 4 * width // parts
    for j in range(parts):
        which, start = divmod(j * shard, width)
        send[j, base : base + shard, :] = weights[which][start : start + shard].astype(BF)
    extras = jnp.concatenate(extra + [jnp.zeros((16 - len(extra), width), F32)], axis=0).astype(BF)
    for j in range(parts):
        send[j, base + shard : base + shard + 16, :] = extras


def unpack_kernel(recv, split, out):
    members, rows, cols, width = out.shape
    parts = recv.shape[0]
    per = cols // parts * members
    for r in range(rows):
        tokens = recv[:, r * per : (r + 1) * per, :].reshape(parts * per, width)
        out[:, r] = dot(split[...], tokens, TN).astype(BF).reshape(members, cols, width)


def total_kernel(base, recv, total):
    acc = recv[0, base:, :].astype(F32)
    for j in range(1, recv.shape[0]):
        acc = acc + recv[j, base:, :].astype(F32)
    total[...] = acc.astype(BF)


def finish_kernel(scale, place, same_core, other_core, extras, g_q, g_k, g_v, g_o, g_mix, g_gain):
    count, shard, width = same_core.shape
    per = width // shard
    outs = (g_q, g_k, g_v, g_o)
    for p in range(2 * count):
        code = lax.bitwise_xor(place[0], p)
        spot = lax.shift_right_logical(code, 1)
        got = jnp.where(code == 2 * spot, same_core[spot], other_core[spot]).astype(F32)
        outs[p // per][p % per * shard : (p % per + 1) * shard, :] = got * scale
    rest = extras[...].astype(F32) * scale
    for i in range(3):
        g_mix[i] = rest[3 * i : 3 * i + 3]
    g_gain[...] = rest[9:10]


def partner(axis, code):
    return [(i, i ^ code) for i in range(lax.axis_size(axis))]


def meet(values, axis, codes):
    got = [values] + [lax.ppermute(values, axis, partner(axis, k)) for k in codes]
    got = [x.astype(F32) for x in got]
    while len(got) > 1:
        got = [a + b for a, b in zip(got[::2], got[1::2])]
    return lax.optimization_barrier(got[0].astype(BF))


def ring(axis, step):
    size = lax.axis_size(axis)
    return [(i, (i + step) % size) for i in range(size)]


def local(fields, norm_gain, w_query, w_key, w_value, w_out, mix_kernel, cotangent):
    members, rows, cols, width = fields.shape
    parts = lax.axis_size("mem")
    per = cols // parts
    cells = rows * per
    pad_cells = (rows + 2) * (per + 2)
    tokens = cells * members * parts
    base = cells * members
    shard = 4 * width // parts
    params = pltpu.CompilerParams(vmem_limit_bytes=60 * 1024 * 1024)
    split = jnp.asarray(split_matrix(parts, members, cols), BF)
    halo = jnp.asarray(halo_matrices(parts, members, rows, cols, 32), BF)
    gather8 = jnp.asarray(gather_matrix(parts, 8, members), BF)
    gather4 = jnp.asarray(gather_matrix(parts, 4, members), BF)
    headsum = jnp.asarray(np.kron(np.eye(HEADS), np.ones((width // HEADS, width // HEADS))), BF)
    gain = norm_gain.reshape(1, width)

    with jax.named_scope("halo"):
        row, col = lax.axis_index("row"), lax.axis_index("col")
        before = lax.ppermute(cotangent[:, rows - 1], "row", ring("row", 1))
        after = lax.ppermute(cotangent[:, 0], "row", ring("row", -1))
        zero = jnp.zeros_like(before)
        before = jnp.where(row > 0, before, zero)
        after = jnp.where(row < lax.axis_size("row") - 1, after, zero)

    with jax.named_scope("pack_fields"):
        send_f = pl.pallas_call(
            pack_fields_kernel,
            out_shape=jax.ShapeDtypeStruct((parts, base, width), BF),
            compiler_params=params,
        )(fields, split)
    with jax.named_scope("fields_to_cells"):
        recv_f = lax.all_to_all(send_f, "mem", 0, 0)

    with jax.named_scope("halo_cols"):

        def column(c):
            pieces = [before[None, :, c], jnp.swapaxes(cotangent[:, :, c], 0, 1), after[None, :, c]]
            flat = jnp.concatenate(pieces, axis=0).reshape((rows + 2) * members, width)
            return jnp.pad(flat, ((0, 32 - flat.shape[0]), (0, 0)))

        left = lax.ppermute(column(cols - 1), "col", ring("col", 1))
        right = lax.ppermute(column(0), "col", ring("col", -1))
        inside = jnp.stack([col > 0, col < lax.axis_size("col") - 1]).astype(jnp.int32)

    with jax.named_scope("forward"):
        token = jax.ShapeDtypeStruct((tokens, width), BF)
        token_f = jax.ShapeDtypeStruct((tokens, width), F32)
        mats = [pltpu.VMEM((cells, width, width), BF), pltpu.VMEM((cells, width, width), BF)]
        kept = pl.pallas_call(
            functools.partial(forward_kernel, members),
            out_shape=(token, token, token, token, token_f, token, token),
            scratch_shapes=[pltpu.VMEM((tokens, width), F32)] + mats,
            compiler_params=params,
        )(recv_f, gain, w_query, w_key, w_value, w_out, gather8, headsum)

    with jax.named_scope("pack_cot"):
        smem = pl.BlockSpec(memory_space=pltpu.SMEM)
        vmem = pl.BlockSpec(memory_space=pltpu.VMEM)
        send_c = pl.pallas_call(
            pack_cot_kernel,
            in_specs=[smem] + [vmem] * 6,
            out_shape=jax.ShapeDtypeStruct((parts, pad_cells * members, width), BF),
            compiler_params=params,
        )(inside, cotangent, before, after, left, right, halo)
    with jax.named_scope("cot_to_cells"):
        recv_c = lax.all_to_all(send_c, "mem", 0, 0)

    with jax.named_scope("backward"):
        back = pl.pallas_call(
            functools.partial(backward_kernel, rows, per, members),
            out_shape=jax.ShapeDtypeStruct((parts, base + shard + 16, width), BF),
            scratch_shapes=[
                pltpu.VMEM((pad_cells, members * parts, width), F32),
                pltpu.VMEM((tokens, width), F32),
            ]
            + mats,
            compiler_params=params,
        )(recv_c, *kept, gain, mix_kernel, w_query, w_key, w_value, w_out, gather8, gather4, headsum)
    with jax.named_scope("to_members"):
        landed = lax.all_to_all(back, "mem", 0, 0)
    with jax.named_scope("unpack"):
        total = pl.pallas_call(
            functools.partial(total_kernel, base),
            out_shape=jax.ShapeDtypeStruct((shard + 16, width), BF),
            compiler_params=params,
        )(landed)
        grad_fields = pl.pallas_call(
            unpack_kernel,
            out_shape=jax.ShapeDtypeStruct(fields.shape, BF),
            compiler_params=params,
        )(landed, split)

    with jax.named_scope("reduce"):
        total = meet(total, "row", (1, 2, 3))
        total = meet(total, "col", (2, 4, 6))
        total = meet(total, "col", (1,))
        piece = total[:shard]
        same_core = jnp.stack([piece] + [lax.ppermute(piece, "mem", partner("mem", k)) for k in (2, 4, 6)])
        same_core = lax.optimization_barrier(same_core)
        other_core = lax.ppermute(same_core, "mem", partner("mem", 1))

    grid = lax.axis_size("row") * lax.axis_size("col")
    scale_all = 1.0 / math.sqrt(tokens * grid * parts)
    with jax.named_scope("finish"):
        square = jax.ShapeDtypeStruct((width, width), F32)
        place = lax.axis_index("mem").astype(jnp.int32).reshape(1)
        grads = pl.pallas_call(
            functools.partial(finish_kernel, scale_all),
            in_specs=[pl.BlockSpec(memory_space=pltpu.SMEM)] + [pl.BlockSpec(memory_space=pltpu.VMEM)] * 3,
            out_shape=(square,) * 4 + (jax.ShapeDtypeStruct((3, 3, width), F32), jax.ShapeDtypeStruct((1, width), F32)),
            compiler_params=params,
        )(place, same_core, other_core, total[shard:])
    return (grad_fields, grads[5].reshape(width)) + tuple(grads[:5])


def solution(mesh):
    tile = P("mem", "row", "col", None)
    in_specs = (tile, P(), P(), P(), P(), P(), P(), tile)
    out_specs = (tile, P(), P(), P(), P(), P(), P())
    return jax.shard_map(local, mesh=mesh, in_specs=in_specs, out_specs=out_specs, check_vma=False)
```

```python
import functools
import math

import jax
import jax.numpy as jnp
import numpy as np
from jax import lax
from jax.experimental import pallas as pl
from jax.experimental.pallas import tpu as pltpu
from jax.sharding import PartitionSpec as P

HEADS = 8
EPS = 1e-06
BF = jnp.bfloat16
F32 = jnp.float32
NT = (((1,), (1,)), ((), ()))
TN = (((0,), (0,)), ((), ()))


def dot(a, b, dims=None):
    if dims is None:
        return jnp.dot(a, b, preferred_element_type=F32)
    return lax.dot_general(a, b, dims, preferred_element_type=F32)


def split_matrix(parts, members, cols):
    per = cols // parts
    out = np.zeros((parts, per, members, members, cols), np.float32)
    for j in range(parts):
        for c in range(per):
            for m in range(members):
                out[j, c, m, m, j * per + c] = 1
    return out.reshape(parts * per * members, members * cols)


def halo_matrices(parts, members, rows, cols):
    per = cols // parts
    edge = members * rows
    mats = []
    for pair in range((rows + 2) // 2):
        out = np.zeros((parts, 2, per + 2, members, 2 * members * cols + 6 * edge), np.float32)
        for j in range(parts):
            for q in range(2):
                row = 2 * pair + q - 1
                level = 0 if row < 0 else (2 if row >= rows else 1)
                for c in range(per + 2):
                    for m in range(members):
                        col = j * per + c - 1
                        if 0 <= col < cols:
                            src = (q * members + m) * cols + col
                        else:
                            side = level if col < 0 else 3 + level
                            src = 2 * members * cols + side * edge + m * rows + row % rows
                        out[j, q, c, m, src] = 1
        mats.append(out.reshape(-1, out.shape[-1]))
    return np.stack(mats)


def gather_matrix(parts, cells, members):
    out = np.zeros((cells, parts, members, parts, cells, members), np.float32)
    for s in range(parts):
        for c in range(cells):
            for m in range(members):
                out[c, s, m, s, c, m] = 1
    return out.reshape(cells * parts * members, -1)


def pack_kernel(grid, place, fields, cot, before, after, got, split, halo, send):
    members, rows, cols, width = fields.shape
    parts = send.shape[0]
    per = cols // parts * members
    for r in range(rows):
        tokens = fields[:, r].reshape(members * cols, width)
        moved = dot(split[...], tokens).astype(BF).reshape(parts, per, width)
        send[:, r * per : (r + 1) * per, :] = moved
    base = rows * per

    def masked(inside, x):
        return jnp.where(inside, x, jnp.zeros_like(x))

    row, col = place[0], place[1]
    sides = []
    for dc in (-1, 1):
        for dr in (-1, 0, 1):
            r, c = row + dr, col + dc
            inside = (r >= 0) & (r < grid[0]) & (c >= 0) & (c < grid[1])
            spot = jnp.clip(r, 0, grid[0] - 1) * grid[1] + jnp.clip(c, 0, grid[1] - 1)
            sides.append(masked(inside, got[spot]))
    lines = [masked(row > 0, before[...])] + [cot[:, r] for r in range(rows)]
    lines = [x.reshape(members * cols, width) for x in lines + [masked(row < grid[0] - 1, after[...])]]
    step = 2 * (per + 2 * members)
    for pair in range(halo.shape[0]):
        tokens = jnp.concatenate([lines[2 * pair], lines[2 * pair + 1]] + sides, axis=0)
        moved = dot(halo[pair], tokens).astype(BF).reshape(parts, step, width)
        send[:, base + pair * step : base + (pair + 1) * step, :] = moved


def main_kernel(
    tile_rows,
    tile_cols,
    recv,
    gain,
    mix,
    wq,
    wk,
    wv,
    wo,
    gather8,
    gather4,
    headsum,
    send,
    padded,
    lhs_a,
    lhs_b,
    mat_k,
    mat_v,
):
    parts, _, width = recv.shape
    head_dim = width // HEADS
    scale = 1.0 / math.sqrt(head_dim)
    cells = tile_rows * tile_cols
    mem_dev = 4
    all_members = parts * mem_dev
    tokens = cells * all_members
    pad_cols = tile_cols + 2
    pad_cells = (tile_rows + 2) * pad_cols
    base = cells * mem_dev

    def regroup(start, count, matrix):
        rows = count * mem_dev
        part = recv[:, start : start + rows, :].reshape(parts * rows, width)
        return dot(matrix[...], part)

    x = jnp.concatenate([regroup(g * 32, 8, gather8) for g in range(cells // 8)], axis=0)
    done = 0
    while done < pad_cells:
        count = 8 if pad_cells - done >= 8 else 4
        block = regroup(base + done * mem_dev, count, gather8 if count == 8 else gather4)
        padded[done : done + count] = block.reshape(count, all_members, width)
        done += count

    def shifted(i, j):
        picked = [
            padded[(r + 2 - i) * pad_cols + 2 - j : (r + 2 - i) * pad_cols + 2 - j + tile_cols]
            for r in range(tile_rows)
        ]
        return jnp.concatenate(picked, axis=0).reshape(tokens, width)

    inv = lax.rsqrt(jnp.mean(x * x, axis=-1, keepdims=True) + EPS)
    normed = x * inv
    inputs = (normed * gain[...]).astype(BF)
    queries = dot(inputs, wq[...]).astype(BF)
    keys = dot(inputs, wk[...]).astype(BF)
    values = dot(inputs, wv[...]).astype(BF)

    conv = jnp.zeros((tokens, width), F32)
    for i in range(3):
        for j in range(3):
            conv = conv + mix[i, j : j + 1, :] * shifted(i, j)
    grad_mixed = conv.astype(BF)
    grad_att = dot(grad_mixed, wo[...], NT).astype(BF)

    row_head = lax.broadcasted_iota(jnp.int32, (width, width), 0) // head_dim
    col_head = lax.broadcasted_iota(jnp.int32, (width, width), 1) // head_dim
    same = row_head == col_head
    lane_head = lax.broadcasted_iota(jnp.int32, (all_members, width), 1) // head_dim

    def expand(block):
        tiled = jnp.concatenate([block] * HEADS, axis=0)
        return jnp.where(same, tiled, jnp.zeros_like(tiled))

    for c in range(cells):
        rows = slice(c * all_members, (c + 1) * all_members)
        mat_k[c] = expand(keys[rows])
        mat_v[c] = expand(values[rows])
    for c in range(cells):
        rows = slice(c * all_members, (c + 1) * all_members)
        lhs_a[rows, :] = dot(queries[rows], mat_k[c], NT)
        lhs_b[rows, :] = dot(grad_att[rows], mat_v[c], NT)

    scores = lhs_a[...] * scale
    lane = lax.broadcasted_iota(jnp.int32, (tokens, 128), 1)
    halves = []
    for h in range(width // 128):
        top = scores[:, h * 128 : (h + 1) * 128]
        step = 1
        while step < all_members:
            up = pltpu.roll(top, step, 1)
            down = pltpu.roll(top, 128 - step, 1)
            top = jnp.maximum(top, jnp.where((lane & step) != 0, up, down))
            step *= 2
        halves.append(top)
    lifted = jnp.exp(scores - jnp.concatenate(halves, axis=1))

    def head_sums(v):
        hi = v.astype(BF)
        lo = (v - hi.astype(F32)).astype(BF)
        return dot(hi, headsum[...]) + dot(lo, headsum[...])

    prob = lifted / head_sums(lifted)
    prob_b = prob.astype(BF)
    grad_prob = lhs_b[...]
    inner = head_sums(prob * grad_prob)
    grad_score = (prob * (grad_prob - inner) * scale).astype(BF)

    att_l, gq_l, gk_l, gv_l = [], [], [], []

    def diagonal(full):
        out = jnp.zeros((all_members, width), F32)
        for h in range(HEADS):
            out = jnp.where(lane_head == h, full[h * all_members : (h + 1) * all_members], out)
        return out

    for c in range(cells):
        rows = slice(c * all_members, (c + 1) * all_members)
        att_l.append(dot(prob_b[rows], mat_v[c]).astype(BF))
        gq_l.append(dot(grad_score[rows], mat_k[c]).astype(BF))
        gk_l.append(diagonal(dot(grad_score[rows], queries[rows], TN)).astype(BF))
        gv_l.append(diagonal(dot(prob_b[rows], grad_att[rows], TN)).astype(BF))
    attended = jnp.concatenate(att_l, axis=0)
    grad_q = jnp.concatenate(gq_l, axis=0)
    grad_k = jnp.concatenate(gk_l, axis=0)
    grad_v = jnp.concatenate(gv_l, axis=0)

    mixed = dot(attended, wo[...]).astype(BF).astype(F32)
    extra = []
    for i in range(3):
        for j in range(3):
            extra.append(jnp.sum(mixed * shifted(i, j), axis=0, keepdims=True))

    grad_in = dot(grad_q, wq[...], NT) + dot(grad_k, wk[...], NT) + dot(grad_v, wv[...], NT)
    extra.append(jnp.sum(grad_in * normed, axis=0, keepdims=True))
    grad_normed = grad_in * gain[...]
    mean = jnp.mean(grad_normed * normed, axis=-1, keepdims=True)
    grad = (shifted(1, 1) + inv * (grad_normed - normed * mean)).astype(BF)
    for g in range(cells // 8):
        back = dot(gather8[...], grad[g * 256 : (g + 1) * 256], TN).astype(BF)
        send[:, g * 32 : (g + 1) * 32, :] = back.reshape(parts, 32, width)

    weights = [
        dot(inputs, grad_q, TN),
        dot(inputs, grad_k, TN),
        dot(inputs, grad_v, TN),
        dot(attended, grad_mixed, TN),
    ]
    shard = 4 * width // parts
    for j in range(parts):
        which, start = divmod(j * shard, width)
        send[j, base : base + shard, :] = weights[which][start : start + shard].astype(BF)
    extras = jnp.concatenate(extra + [jnp.zeros((16 - len(extra), width), F32)], axis=0).astype(BF)
    for j in range(parts):
        send[j, base + shard : base + shard + 16, :] = extras


def unpack_kernel(recv, split, out):
    members, rows, cols, width = out.shape
    parts = recv.shape[0]
    per = cols // parts * members
    for r in range(rows):
        tokens = recv[:, r * per : (r + 1) * per, :].reshape(parts * per, width)
        out[:, r] = dot(split[...], tokens, TN).astype(BF).reshape(members, cols, width)


def finish_kernel(scale, place, same_core, other_core, total, g_q, g_k, g_v, g_o, g_mix, g_gain):
    count, shard, width = same_core.shape
    per = width // shard
    outs = (g_q, g_k, g_v, g_o)
    for p in range(2 * count):
        code = lax.bitwise_xor(place[0], p)
        spot = lax.shift_right_logical(code, 1)
        got = jnp.where(code == 2 * spot, same_core[spot], other_core[spot]).astype(F32)
        outs[p // per][p % per * shard : (p % per + 1) * shard, :] = got * scale
    rest = total[shard:, :].astype(F32) * scale
    for i in range(3):
        g_mix[i] = rest[3 * i : 3 * i + 3]
    g_gain[...] = rest[9:10]


def partner(axis, code):
    return [(i, i ^ code) for i in range(lax.axis_size(axis))]


def meet(values, axis, codes):
    got = [values] + [lax.ppermute(values, axis, partner(axis, k)) for k in codes]
    got = [x.astype(F32) for x in got]
    while len(got) > 1:
        got = [a + b for a, b in zip(got[::2], got[1::2])]
    return lax.optimization_barrier(got[0].astype(BF))


def ring(axis, step):
    size = lax.axis_size(axis)
    return [(i, (i + step) % size) for i in range(size)]


def local(fields, norm_gain, w_query, w_key, w_value, w_out, mix_kernel, cotangent):
    members, rows, cols, width = fields.shape
    parts = lax.axis_size("mem")
    per = cols // parts
    cells = rows * per
    pad_cells = (rows + 2) * (per + 2)
    params = pltpu.CompilerParams(vmem_limit_bytes=60 * 1024 * 1024)

    split = jnp.asarray(split_matrix(parts, members, cols), BF)
    halo = jnp.asarray(halo_matrices(parts, members, rows, cols), BF)
    grid = (lax.axis_size("row"), lax.axis_size("col"))
    smem = pl.BlockSpec(memory_space=pltpu.SMEM)
    vmem = pl.BlockSpec(memory_space=pltpu.VMEM)
    with jax.named_scope("halo"):
        row, col = lax.axis_index("row"), lax.axis_index("col")
        place = jnp.stack([row, col]).astype(jnp.int32)
        before = lax.ppermute(cotangent[:, rows - 1], "row", ring("row", 1))
        after = lax.ppermute(cotangent[:, 0], "row", ring("row", -1))
        first = cotangent[:, :, 0].reshape(1, 1, members * rows, width)
        last = cotangent[:, :, cols - 1].reshape(1, 1, members * rows, width)
        to_right = (lax.iota(jnp.int32, grid[1]) == col + 1).reshape(1, grid[1], 1, 1)
        columns = jnp.broadcast_to(jnp.where(to_right, last, first), grid + (members * rows, width))
        columns = columns.reshape(grid[0] * grid[1], members * rows, width)
        got = lax.all_to_all(columns, ("row", "col"), 0, 0)

    with jax.named_scope("pack"):
        send = pl.pallas_call(
            functools.partial(pack_kernel, grid),
            in_specs=[smem] + [vmem] * 7,
            out_shape=jax.ShapeDtypeStruct((parts, (cells + pad_cells) * members, width), BF),
            compiler_params=params,
        )(place, fields, cotangent, before, after, got, split, halo)
    with jax.named_scope("to_cells"):
        recv = lax.all_to_all(send, "mem", 0, 0)

    tokens = cells * members * parts
    base = cells * members
    shard = 4 * width // parts
    headsum = np.kron(np.eye(HEADS), np.ones((width // HEADS, width // HEADS)))
    with jax.named_scope("attention"):
        back = pl.pallas_call(
            functools.partial(main_kernel, rows, per),
            out_shape=jax.ShapeDtypeStruct((parts, base + shard + 16, width), BF),
            scratch_shapes=[
                pltpu.VMEM((pad_cells, members * parts, width), F32),
                pltpu.VMEM((tokens, width), F32),
                pltpu.VMEM((tokens, width), F32),
                pltpu.VMEM((cells, width, width), BF),
                pltpu.VMEM((cells, width, width), BF),
            ],
            compiler_params=params,
        )(
            recv,
            norm_gain.reshape(1, width),
            mix_kernel,
            w_query,
            w_key,
            w_value,
            w_out,
            jnp.asarray(gather_matrix(parts, 8, members), BF),
            jnp.asarray(gather_matrix(parts, 4, members), BF),
            jnp.asarray(headsum, BF),
        )
    with jax.named_scope("to_members"):
        landed = lax.all_to_all(back, "mem", 0, 0)
    with jax.named_scope("unpack"):
        total = jnp.sum(landed[:, base:, :].astype(F32), axis=0)
        total = lax.optimization_barrier(total.astype(BF))
        grad_fields = pl.pallas_call(
            unpack_kernel,
            out_shape=jax.ShapeDtypeStruct(fields.shape, BF),
            compiler_params=params,
        )(landed, split)

    with jax.named_scope("reduce"):
        total = meet(total, "row", (1, 2, 3))
        total = meet(total, "col", (2, 4, 6))
        total = meet(total, "col", (1,))
        piece = total[:shard]
        same_core = jnp.stack([piece] + [lax.ppermute(piece, "mem", partner("mem", k)) for k in (2, 4, 6)])
        same_core = lax.optimization_barrier(same_core)
        other_core = lax.ppermute(same_core, "mem", partner("mem", 1))

    scale_all = 1.0 / math.sqrt(tokens * grid[0] * grid[1] * parts)
    with jax.named_scope("finish"):
        square = jax.ShapeDtypeStruct((width, width), F32)
        own = lax.axis_index("mem").astype(jnp.int32).reshape(1)
        grads = pl.pallas_call(
            functools.partial(finish_kernel, scale_all),
            in_specs=[smem] + [vmem] * 3,
            out_shape=(square,) * 4 + (jax.ShapeDtypeStruct((3, 3, width), F32), jax.ShapeDtypeStruct((1, width), F32)),
            compiler_params=params,
        )(own, same_core, other_core, total)
    return (grad_fields, grads[5].reshape(width)) + tuple(grads[:5])


def solution(mesh):
    tile = P("mem", "row", "col", None)
    in_specs = (tile, P(), P(), P(), P(), P(), P(), tile)
    out_specs = (tile, P(), P(), P(), P(), P(), P())
    return jax.shard_map(local, mesh=mesh, in_specs=in_specs, out_specs=out_specs, check_vma=False)
```

```python
import functools
import math

import jax
import jax.numpy as jnp
import numpy as np
from jax import lax
from jax.experimental import pallas as pl
from jax.experimental.pallas import tpu as pltpu
from jax.sharding import PartitionSpec as P

HEADS = 8
EPS = 1e-06
BF = jnp.bfloat16
F32 = jnp.float32
NT = (((1,), (1,)), ((), ()))
TN = (((0,), (0,)), ((), ()))


def dot(a, b, dims=None):
    if dims is None:
        return jnp.dot(a, b, preferred_element_type=F32)
    return lax.dot_general(a, b, dims, preferred_element_type=F32)


def split_matrix(parts, members, cols):
    per = cols // parts
    out = np.zeros((parts, per, members, members, cols), np.float32)
    for j in range(parts):
        for c in range(per):
            for m in range(members):
                out[j, c, m, m, j * per + c] = 1
    return out.reshape(parts * per * members, members * cols)


def halo_matrices(parts, members, rows, cols):
    per = cols // parts
    edge = members * rows
    mats = []
    for pair in range(rows // 2):
        out = np.zeros((parts, 2, per + 2, members, 2 * members * cols + 2 * edge), np.float32)
        for j in range(parts):
            for q in range(2):
                for c in range(per + 2):
                    for m in range(members):
                        col = j * per + c - 1
                        if 0 <= col < cols:
                            src = (q * members + m) * cols + col
                        else:
                            side = 0 if col < 0 else 1
                            src = 2 * members * cols + side * edge + m * rows + 2 * pair + q
                        out[j, q, c, m, src] = 1
        mats.append(out.reshape(-1, out.shape[-1]))
    return np.stack(mats)


def gather_matrix(parts, cells, members):
    out = np.zeros((cells, parts, members, parts, cells, members), np.float32)
    for s in range(parts):
        for c in range(cells):
            for m in range(members):
                out[c, s, m, s, c, m] = 1
    return out.reshape(cells * parts * members, -1)


def masked(inside, x):
    return jnp.where(inside, x, jnp.zeros_like(x))


def pack_kernel(col_size, place, fields, cot, got, split, halo, send):
    members, rows, cols, width = fields.shape
    parts = send.shape[0]
    per = cols // parts * members
    for r in range(rows):
        tokens = fields[:, r].reshape(members * cols, width)
        moved = dot(split[...], tokens).astype(BF).reshape(parts, per, width)
        send[:, r * per : (r + 1) * per, :] = moved
    base = rows * per
    col = place[1]
    sides = [
        masked(col > 0, got[jnp.maximum(col - 1, 0)]),
        masked(col < col_size - 1, got[jnp.minimum(col + 1, col_size - 1)]),
    ]
    step = 2 * (per + 2 * members)
    for pair in range(rows // 2):
        lines = [cot[:, 2 * pair + q].reshape(members * cols, width) for q in range(2)]
        moved = dot(halo[pair], jnp.concatenate(lines + sides, axis=0)).astype(BF)
        send[:, base + pair * step : base + (pair + 1) * step, :] = moved.reshape(parts, step, width)


def regroup(recv, start, count, members, matrix):
    parts, _, width = recv.shape
    rows = count * members
    return dot(matrix[...], recv[:, start : start + rows, :].reshape(parts * rows, width))


def norm(x):
    inv = lax.rsqrt(jnp.mean(x * x, axis=-1, keepdims=True) + EPS)
    return inv, x * inv


def head_sums(v, headsum):
    hi = v.astype(BF)
    lo = (v - hi.astype(F32)).astype(BF)
    return dot(hi, headsum[...]) + dot(lo, headsum[...])


def expand_all(blocks, mats):
    cells, width, _ = mats.shape
    size = blocks.shape[0] // cells
    head_dim = width // HEADS
    row_head = lax.broadcasted_iota(jnp.int32, (width, width), 0) // head_dim
    col_head = lax.broadcasted_iota(jnp.int32, (width, width), 1) // head_dim
    same = row_head == col_head
    for c in range(cells):
        tiled = jnp.concatenate([blocks[c * size : (c + 1) * size]] * HEADS, axis=0)
        mats[c] = jnp.where(same, tiled, jnp.zeros_like(tiled))


def forward_kernel(
    members,
    recv,
    gain,
    wq,
    wk,
    wv,
    wo,
    gather8,
    headsum,
    x_out,
    q_out,
    k_out,
    v_out,
    prob_out,
    att_out,
    mixed_out,
    sums,
    mat_k,
    mat_v,
):
    parts, _, width = recv.shape
    scale = 1.0 / math.sqrt(width // HEADS)
    all_members = parts * members
    tokens = x_out.shape[0]
    cells = tokens // all_members
    x = jnp.concatenate([regroup(recv, g * 32, 8, members, gather8) for g in range(cells // 8)], axis=0)
    x_out[...] = x.astype(BF)
    _, normed = norm(x)
    inputs = (normed * gain[...]).astype(BF)
    queries = dot(inputs, wq[...]).astype(BF)
    keys = dot(inputs, wk[...]).astype(BF)
    values = dot(inputs, wv[...]).astype(BF)
    q_out[...] = queries
    k_out[...] = keys
    v_out[...] = values
    expand_all(keys, mat_k)
    expand_all(values, mat_v)
    for c in range(cells):
        rows = slice(c * all_members, (c + 1) * all_members)
        sums[rows, :] = dot(queries[rows], mat_k[c], NT)
    scores = sums[...] * scale
    lane = lax.broadcasted_iota(jnp.int32, (tokens, 128), 1)
    halves = []
    for h in range(width // 128):
        top = scores[:, h * 128 : (h + 1) * 128]
        step = 1
        while step < all_members:
            up = pltpu.roll(top, step, 1)
            down = pltpu.roll(top, 128 - step, 1)
            top = jnp.maximum(top, jnp.where((lane & step) != 0, up, down))
            step *= 2
        halves.append(top)
    lifted = jnp.exp(scores - jnp.concatenate(halves, axis=1))
    prob = lifted / head_sums(lifted, headsum)
    prob_out[...] = prob
    prob_b = prob.astype(BF)
    for c in range(cells):
        rows = slice(c * all_members, (c + 1) * all_members)
        att_out[rows, :] = dot(prob_b[rows], mat_v[c]).astype(BF)
    mixed_out[...] = dot(att_out[...], wo[...]).astype(BF)


def backward_kernel(
    tile_rows,
    tile_cols,
    members,
    row_size,
    place,
    recv,
    above,
    below,
    x_in,
    q_in,
    k_in,
    v_in,
    prob_in,
    att_in,
    mixed_in,
    gain,
    mix,
    wq,
    wk,
    wv,
    wo,
    gather8,
    gather6,
    headsum,
    send,
    padded,
    sums,
    mat_k,
    mat_v,
):
    parts, _, width = recv.shape
    head_dim = width // HEADS
    scale = 1.0 / math.sqrt(head_dim)
    cells = tile_rows * tile_cols
    all_members = parts * members
    tokens = cells * all_members
    pad_cols = tile_cols + 2
    pad_cells = (tile_rows + 2) * pad_cols
    base = cells * members
    row = place[0]
    top = dot(gather6[...], masked(row > 0, above[...]))
    padded[:pad_cols] = top.reshape(pad_cols, all_members, width)
    for g in range(tile_rows * pad_cols // 8):
        block = regroup(recv, base + g * 8 * members, 8, members, gather8)
        padded[pad_cols + g * 8 : pad_cols + (g + 1) * 8] = block.reshape(8, all_members, width)
    bottom = dot(gather6[...], masked(row < row_size - 1, below[...]))
    padded[pad_cells - pad_cols :] = bottom.reshape(pad_cols, all_members, width)

    def shifted(i, j):
        picked = [
            padded[(r + 2 - i) * pad_cols + 2 - j : (r + 2 - i) * pad_cols + 2 - j + tile_cols]
            for r in range(tile_rows)
        ]
        return jnp.concatenate(picked, axis=0).reshape(tokens, width)

    expand_all(k_in[...], mat_k)
    expand_all(v_in[...], mat_v)
    inv, normed = norm(x_in[...].astype(F32))
    inputs = (normed * gain[...]).astype(BF)
    mixed = mixed_in[...].astype(F32)
    extra = []
    conv = jnp.zeros((tokens, width), F32)
    for i in range(3):
        for j in range(3):
            moved = shifted(i, j)
            conv = conv + mix[i, j : j + 1, :] * moved
            extra.append(jnp.sum(mixed * moved, axis=0, keepdims=True))
    grad_mixed = conv.astype(BF)
    grad_att = dot(grad_mixed, wo[...], NT).astype(BF)
    for c in range(cells):
        rows = slice(c * all_members, (c + 1) * all_members)
        sums[rows, :] = dot(grad_att[rows], mat_v[c], NT)

    prob = prob_in[...]
    prob_b = prob.astype(BF)
    grad_prob = sums[...]
    inner = head_sums(prob * grad_prob, headsum)
    grad_score = (prob * (grad_prob - inner) * scale).astype(BF)
    lane_head = lax.broadcasted_iota(jnp.int32, (all_members, width), 1) // head_dim

    def diagonal(full):
        out = jnp.zeros((all_members, width), F32)
        for h in range(HEADS):
            out = jnp.where(lane_head == h, full[h * all_members : (h + 1) * all_members], out)
        return out

    gq_l, gk_l, gv_l = [], [], []
    for c in range(cells):
        rows = slice(c * all_members, (c + 1) * all_members)
        gq_l.append(dot(grad_score[rows], mat_k[c]).astype(BF))
        gk_l.append(diagonal(dot(grad_score[rows], q_in[rows, :], TN)).astype(BF))
        gv_l.append(diagonal(dot(prob_b[rows], grad_att[rows], TN)).astype(BF))
    grad_q = jnp.concatenate(gq_l, axis=0)
    grad_k = jnp.concatenate(gk_l, axis=0)
    grad_v = jnp.concatenate(gv_l, axis=0)

    grad_in = dot(grad_q, wq[...], NT) + dot(grad_k, wk[...], NT) + dot(grad_v, wv[...], NT)
    extra.append(jnp.sum(grad_in * normed, axis=0, keepdims=True))
    grad_normed = grad_in * gain[...]
    mean = jnp.mean(grad_normed * normed, axis=-1, keepdims=True)
    grad = (shifted(1, 1) + inv * (grad_normed - normed * mean)).astype(BF)
    for g in range(cells // 8):
        back = dot(gather8[...], grad[g * 256 : (g + 1) * 256], TN).astype(BF)
        send[:, g * 32 : (g + 1) * 32, :] = back.reshape(parts, 32, width)

    weights = [
        dot(inputs, grad_q, TN),
        dot(inputs, grad_k, TN),
        dot(inputs, grad_v, TN),
        dot(att_in[...], grad_mixed, TN),
    ]
    shard = 4 * width // parts
    for j in range(parts):
        which, start = divmod(j * shard, width)
        send[j, base : base + shard, :] = weights[which][start : start + shard].astype(BF)
    extras = jnp.concatenate(extra + [jnp.zeros((16 - len(extra), width), F32)], axis=0).astype(BF)
    for j in range(parts):
        send[j, base + shard : base + shard + 16, :] = extras


def unpack_kernel(recv, split, out):
    members, rows, cols, width = out.shape
    parts = recv.shape[0]
    per = cols // parts * members
    for r in range(rows):
        tokens = recv[:, r * per : (r + 1) * per, :].reshape(parts * per, width)
        out[:, r] = dot(split[...], tokens, TN).astype(BF).reshape(members, cols, width)


def finish_kernel(scale, place, same_core, other_core, total, g_q, g_k, g_v, g_o, g_mix, g_gain):
    count, shard, width = same_core.shape
    per = width // shard
    outs = (g_q, g_k, g_v, g_o)
    for p in range(2 * count):
        code = lax.bitwise_xor(place[0], p)
        spot = lax.shift_right_logical(code, 1)
        got = jnp.where(code == 2 * spot, same_core[spot], other_core[spot]).astype(F32)
        outs[p // per][p % per * shard : (p % per + 1) * shard, :] = got * scale
    rest = total[shard:, :].astype(F32) * scale
    for i in range(3):
        g_mix[i] = rest[3 * i : 3 * i + 3]
    g_gain[...] = rest[9:10]


def partner(axis, code):
    return [(i, i ^ code) for i in range(lax.axis_size(axis))]


def meet(values, axis, codes):
    got = [values] + [lax.ppermute(values, axis, partner(axis, k)) for k in codes]
    got = [x.astype(F32) for x in got]
    while len(got) > 1:
        got = [a + b for a, b in zip(got[::2], got[1::2])]
    return lax.optimization_barrier(got[0].astype(BF))


def ring(axis, step):
    size = lax.axis_size(axis)
    return [(i, (i + step) % size) for i in range(size)]


def local(fields, norm_gain, w_query, w_key, w_value, w_out, mix_kernel, cotangent):
    members, rows, cols, width = fields.shape
    parts = lax.axis_size("mem")
    per = cols // parts
    cells = rows * per
    line = (per + 2) * members
    tokens = cells * members * parts
    base = cells * members
    shard = 4 * width // parts
    grid = (lax.axis_size("row"), lax.axis_size("col"))
    params = pltpu.CompilerParams(vmem_limit_bytes=60 * 1024 * 1024)
    smem = pl.BlockSpec(memory_space=pltpu.SMEM)
    vmem = pl.BlockSpec(memory_space=pltpu.VMEM)
    split = jnp.asarray(split_matrix(parts, members, cols), BF)
    halo = jnp.asarray(halo_matrices(parts, members, rows, cols), BF)
    gather8 = jnp.asarray(gather_matrix(parts, 8, members), BF)
    gather6 = jnp.asarray(gather_matrix(parts, per + 2, members), BF)
    headsum = jnp.asarray(np.kron(np.eye(HEADS), np.ones((width // HEADS, width // HEADS))), BF)
    gain = norm_gain.reshape(1, width)
    row, col = lax.axis_index("row"), lax.axis_index("col")
    place = jnp.stack([row, col]).astype(jnp.int32)

    with jax.named_scope("halo_cols"):
        first = cotangent[:, :, 0].reshape(1, members * rows, width)
        last = cotangent[:, :, cols - 1].reshape(1, members * rows, width)
        to_right = (lax.iota(jnp.int32, grid[1]) == col + 1).reshape(grid[1], 1, 1)
        got = lax.all_to_all(jnp.where(to_right, last, first), "col", 0, 0)
    with jax.named_scope("pack"):
        send = pl.pallas_call(
            functools.partial(pack_kernel, grid[1]),
            in_specs=[smem] + [vmem] * 5,
            out_shape=jax.ShapeDtypeStruct((parts, base + rows * line, width), BF),
            compiler_params=params,
        )(place, fields, cotangent, got, split, halo)
    with jax.named_scope("to_cells"):
        recv = lax.all_to_all(send, "mem", 0, 0)
    with jax.named_scope("halo_rows"):
        top = recv[:, base : base + line].reshape(parts * line, width)
        bottom = recv[:, base + (rows - 1) * line :].reshape(parts * line, width)
        above = lax.ppermute(bottom, "row", ring("row", 1))
        below = lax.ppermute(top, "row", ring("row", -1))

    with jax.named_scope("forward"):
        token = jax.ShapeDtypeStruct((tokens, width), BF)
        token_f = jax.ShapeDtypeStruct((tokens, width), F32)
        mats = [pltpu.VMEM((cells, width, width), BF), pltpu.VMEM((cells, width, width), BF)]
        kept = pl.pallas_call(
            functools.partial(forward_kernel, members),
            out_shape=(token, token, token, token, token_f, token, token),
            scratch_shapes=[pltpu.VMEM((tokens, width), F32)] + mats,
            compiler_params=params,
        )(recv, gain, w_query, w_key, w_value, w_out, gather8, headsum)
    with jax.named_scope("backward"):
        back = pl.pallas_call(
            functools.partial(backward_kernel, rows, per, members, grid[0]),
            in_specs=[smem] + [vmem] * 19,
            out_shape=jax.ShapeDtypeStruct((parts, base + shard + 16, width), BF),
            scratch_shapes=[
                pltpu.VMEM(((rows + 2) * (per + 2), members * parts, width), F32),
                pltpu.VMEM((tokens, width), F32),
            ]
            + mats,
            compiler_params=params,
        )(
            place,
            recv,
            above,
            below,
            *kept,
            gain,
            mix_kernel,
            w_query,
            w_key,
            w_value,
            w_out,
            gather8,
            gather6,
            headsum,
        )
    with jax.named_scope("to_members"):
        landed = lax.all_to_all(back, "mem", 0, 0)
    with jax.named_scope("unpack"):
        total = jnp.sum(landed[:, base:, :].astype(F32), axis=0)
        total = lax.optimization_barrier(total.astype(BF))
        grad_fields = pl.pallas_call(
            unpack_kernel,
            out_shape=jax.ShapeDtypeStruct(fields.shape, BF),
            compiler_params=params,
        )(landed, split)

    with jax.named_scope("reduce"):
        total = meet(total, "row", (1, 2, 3))
        total = meet(total, "col", (2, 4, 6))
        total = meet(total, "col", (1,))
        piece = total[:shard]
        same_core = jnp.stack([piece] + [lax.ppermute(piece, "mem", partner("mem", k)) for k in (2, 4, 6)])
        same_core = lax.optimization_barrier(same_core)
        other_core = lax.ppermute(same_core, "mem", partner("mem", 1))

    scale_all = 1.0 / math.sqrt(tokens * grid[0] * grid[1] * parts)
    with jax.named_scope("finish"):
        square = jax.ShapeDtypeStruct((width, width), F32)
        own = lax.axis_index("mem").astype(jnp.int32).reshape(1)
        grads = pl.pallas_call(
            functools.partial(finish_kernel, scale_all),
            in_specs=[smem] + [vmem] * 3,
            out_shape=(square,) * 4 + (jax.ShapeDtypeStruct((3, 3, width), F32), jax.ShapeDtypeStruct((1, width), F32)),
            compiler_params=params,
        )(own, same_core, other_core, total)
    return (grad_fields, grads[5].reshape(width)) + tuple(grads[:5])


def solution(mesh):
    tile = P("mem", "row", "col", None)
    in_specs = (tile, P(), P(), P(), P(), P(), P(), tile)
    out_specs = (tile, P(), P(), P(), P(), P(), P())
    return jax.shard_map(local, mesh=mesh, in_specs=in_specs, out_specs=out_specs, check_vma=False)
```

```python
import functools
import math

import jax
import jax.numpy as jnp
import numpy as np
from jax import lax
from jax.experimental import pallas as pl
from jax.experimental.pallas import tpu as pltpu
from jax.sharding import PartitionSpec as P

HEADS = 8
EPS = 1e-06
BF = jnp.bfloat16
F32 = jnp.float32
NT = (((1,), (1,)), ((), ()))
TN = (((0,), (0,)), ((), ()))


def dot(a, b, dims=None):
    if dims is None:
        return jnp.dot(a, b, preferred_element_type=F32)
    return lax.dot_general(a, b, dims, preferred_element_type=F32)


def split_matrix(parts, members, cols):
    per = cols // parts
    out = np.zeros((parts, per, members, members, cols), np.float32)
    for j in range(parts):
        for c in range(per):
            for m in range(members):
                out[j, c, m, m, j * per + c] = 1
    return out.reshape(parts * per * members, members * cols)


def halo_matrices(parts, members, rows, cols):
    per = cols // parts
    edge = members * rows
    mats = []
    for pair in range((rows + 2) // 2):
        out = np.zeros((parts, 2, per + 2, members, 2 * members * cols + 6 * edge), np.float32)
        for j in range(parts):
            for q in range(2):
                row = 2 * pair + q - 1
                level = 0 if row < 0 else (2 if row >= rows else 1)
                for c in range(per + 2):
                    for m in range(members):
                        col = j * per + c - 1
                        if 0 <= col < cols:
                            src = (q * members + m) * cols + col
                        else:
                            side = level if col < 0 else 3 + level
                            src = 2 * members * cols + side * edge + m * rows + row % rows
                        out[j, q, c, m, src] = 1
        mats.append(out.reshape(-1, out.shape[-1]))
    return np.stack(mats)


def gather_matrix(parts, cells, members):
    out = np.zeros((cells, parts, members, parts, cells, members), np.float32)
    for s in range(parts):
        for c in range(cells):
            for m in range(members):
                out[c, s, m, s, c, m] = 1
    return out.reshape(cells * parts * members, -1)


def pack_kernel(grid, place, fields, cot, before, after, got, split, halo, send):
    members, rows, cols, width = fields.shape
    parts = send.shape[0]
    per = cols // parts * members
    for r in range(rows):
        tokens = fields[:, r].reshape(members * cols, width)
        moved = dot(split[...], tokens).astype(BF).reshape(parts, per, width)
        send[:, r * per : (r + 1) * per, :] = moved
    base = rows * per

    def masked(inside, x):
        return jnp.where(inside, x, jnp.zeros_like(x))

    row, col = place[0], place[1]
    sides = []
    for dc in (-1, 1):
        for dr in (-1, 0, 1):
            r, c = row + dr, col + dc
            inside = (r >= 0) & (r < grid[0]) & (c >= 0) & (c < grid[1])
            spot = jnp.clip(r, 0, grid[0] - 1) * grid[1] + jnp.clip(c, 0, grid[1] - 1)
            sides.append(masked(inside, got[spot]))
    lines = [masked(row > 0, before[...])] + [cot[:, r] for r in range(rows)]
    lines = [x.reshape(members * cols, width) for x in lines + [masked(row < grid[0] - 1, after[...])]]
    step = 2 * (per + 2 * members)
    for pair in range(halo.shape[0]):
        tokens = jnp.concatenate([lines[2 * pair], lines[2 * pair + 1]] + sides, axis=0)
        moved = dot(halo[pair], tokens).astype(BF).reshape(parts, step, width)
        send[:, base + pair * step : base + (pair + 1) * step, :] = moved


def main_kernel(
    tile_rows,
    tile_cols,
    recv,
    gain,
    mix,
    wq,
    wk,
    wv,
    wo,
    gather8,
    gather4,
    headsum,
    send,
    padded,
    lhs_a,
    lhs_b,
    mat_k,
    mat_v,
):
    parts, _, width = recv.shape
    head_dim = width // HEADS
    scale = 1.0 / math.sqrt(head_dim)
    cells = tile_rows * tile_cols
    mem_dev = 4
    all_members = parts * mem_dev
    tokens = cells * all_members
    pad_cols = tile_cols + 2
    pad_cells = (tile_rows + 2) * pad_cols
    base = cells * mem_dev

    def regroup(start, count, matrix):
        rows = count * mem_dev
        part = recv[:, start : start + rows, :].reshape(parts * rows, width)
        return dot(matrix[...], part)

    x = jnp.concatenate([regroup(g * 32, 8, gather8) for g in range(cells // 8)], axis=0)
    done = 0
    while done < pad_cells:
        count = 8 if pad_cells - done >= 8 else 4
        block = regroup(base + done * mem_dev, count, gather8 if count == 8 else gather4)
        padded[done : done + count] = block.reshape(count, all_members, width)
        done += count

    def shifted(i, j):
        picked = [
            padded[(r + 2 - i) * pad_cols + 2 - j : (r + 2 - i) * pad_cols + 2 - j + tile_cols]
            for r in range(tile_rows)
        ]
        return jnp.concatenate(picked, axis=0).reshape(tokens, width)

    inv = lax.rsqrt(jnp.mean(x * x, axis=-1, keepdims=True) + EPS)
    normed = x * inv
    inputs = (normed * gain[...]).astype(BF)
    queries = dot(inputs, wq[...]).astype(BF)
    keys = dot(inputs, wk[...]).astype(BF)
    values = dot(inputs, wv[...]).astype(BF)

    conv = jnp.zeros((tokens, width), F32)
    for i in range(3):
        for j in range(3):
            conv = conv + mix[i, j : j + 1, :] * shifted(i, j)
    grad_mixed = conv.astype(BF)
    grad_att = dot(grad_mixed, wo[...], NT).astype(BF)

    row_head = lax.broadcasted_iota(jnp.int32, (width, width), 0) // head_dim
    col_head = lax.broadcasted_iota(jnp.int32, (width, width), 1) // head_dim
    same = row_head == col_head
    lane_head = lax.broadcasted_iota(jnp.int32, (all_members, width), 1) // head_dim

    def expand(block):
        tiled = jnp.concatenate([block] * HEADS, axis=0)
        return jnp.where(same, tiled, jnp.zeros_like(tiled))

    for c in range(cells):
        rows = slice(c * all_members, (c + 1) * all_members)
        mat_k[c] = expand(keys[rows])
        mat_v[c] = expand(values[rows])
    for c in range(cells):
        rows = slice(c * all_members, (c + 1) * all_members)
        lhs_a[rows, :] = dot(queries[rows], mat_k[c], NT)
        lhs_b[rows, :] = dot(grad_att[rows], mat_v[c], NT)

    scores = lhs_a[...] * scale
    lane = lax.broadcasted_iota(jnp.int32, (tokens, 128), 1)
    halves = []
    for h in range(width // 128):
        top = scores[:, h * 128 : (h + 1) * 128]
        step = 1
        while step < all_members:
            up = pltpu.roll(top, step, 1)
            down = pltpu.roll(top, 128 - step, 1)
            top = jnp.maximum(top, jnp.where((lane & step) != 0, up, down))
            step *= 2
        halves.append(top)
    lifted = jnp.exp(scores - jnp.concatenate(halves, axis=1))

    def head_sums(v):
        hi = v.astype(BF)
        lo = (v - hi.astype(F32)).astype(BF)
        return dot(hi, headsum[...]) + dot(lo, headsum[...])

    prob = lifted / head_sums(lifted)
    prob_b = prob.astype(BF)
    grad_prob = lhs_b[...]
    inner = head_sums(prob * grad_prob)
    grad_score = (prob * (grad_prob - inner) * scale).astype(BF)

    att_l, gq_l, gk_l, gv_l = [], [], [], []

    def diagonal(full):
        out = jnp.zeros((all_members, width), F32)
        for h in range(HEADS):
            out = jnp.where(lane_head == h, full[h * all_members : (h + 1) * all_members], out)
        return out

    for c in range(cells):
        rows = slice(c * all_members, (c + 1) * all_members)
        att_l.append(dot(prob_b[rows], mat_v[c]).astype(BF))
        gq_l.append(dot(grad_score[rows], mat_k[c]).astype(BF))
        gk_l.append(diagonal(dot(grad_score[rows], queries[rows], TN)).astype(BF))
        gv_l.append(diagonal(dot(prob_b[rows], grad_att[rows], TN)).astype(BF))
    attended = jnp.concatenate(att_l, axis=0)
    grad_q = jnp.concatenate(gq_l, axis=0)
    grad_k = jnp.concatenate(gk_l, axis=0)
    grad_v = jnp.concatenate(gv_l, axis=0)

    mixed = dot(attended, wo[...]).astype(BF).astype(F32)
    extra = []
    for i in range(3):
        for j in range(3):
            extra.append(jnp.sum(mixed * shifted(i, j), axis=0, keepdims=True))

    grad_in = dot(grad_q, wq[...], NT) + dot(grad_k, wk[...], NT) + dot(grad_v, wv[...], NT)
    extra.append(jnp.sum(grad_in * normed, axis=0, keepdims=True))
    grad_normed = grad_in * gain[...]
    mean = jnp.mean(grad_normed * normed, axis=-1, keepdims=True)
    grad = (shifted(1, 1) + inv * (grad_normed - normed * mean)).astype(BF)
    for g in range(cells // 8):
        back = dot(gather8[...], grad[g * 256 : (g + 1) * 256], TN).astype(BF)
        send[:, g * 32 : (g + 1) * 32, :] = back.reshape(parts, 32, width)

    weights = [
        dot(inputs, grad_q, TN),
        dot(inputs, grad_k, TN),
        dot(inputs, grad_v, TN),
        dot(attended, grad_mixed, TN),
    ]
    shard = 4 * width // parts
    for j in range(parts):
        which, start = divmod(j * shard, width)
        send[j, base : base + shard, :] = weights[which][start : start + shard].astype(BF)
    extras = jnp.concatenate(extra + [jnp.zeros((16 - len(extra), width), F32)], axis=0).astype(BF)
    for j in range(parts):
        send[j, base + shard : base + shard + 16, :] = extras


def unpack_kernel(recv, split, out):
    members, rows, cols, width = out.shape
    parts = recv.shape[0]
    per = cols // parts * members
    for r in range(rows):
        tokens = recv[:, r * per : (r + 1) * per, :].reshape(parts * per, width)
        out[:, r] = dot(split[...], tokens, TN).astype(BF).reshape(members, cols, width)


def finish_kernel(scale, place, same_core, other_core, total, g_q, g_k, g_v, g_o, g_mix, g_gain):
    count, shard, width = same_core.shape
    per = width // shard
    outs = (g_q, g_k, g_v, g_o)
    for p in range(2 * count):
        code = lax.bitwise_xor(place[0], p)
        spot = lax.shift_right_logical(code, 1)
        got = jnp.where(code == 2 * spot, same_core[spot], other_core[spot]).astype(F32)
        outs[p // per][p % per * shard : (p % per + 1) * shard, :] = got * scale
    rest = total[shard:, :].astype(F32) * scale
    for i in range(3):
        g_mix[i] = rest[3 * i : 3 * i + 3]
    g_gain[...] = rest[9:10]


def partner(axis, code):
    return [(i, i ^ code) for i in range(lax.axis_size(axis))]


def meet(values, axis, codes):
    got = [values] + [lax.ppermute(values, axis, partner(axis, k)) for k in codes]
    got = [x.astype(F32) for x in got]
    while len(got) > 1:
        got = [a + b for a, b in zip(got[::2], got[1::2])]
    return lax.optimization_barrier(got[0].astype(BF))


def near(x):
    return pltpu.with_memory_space_constraint(x, pltpu.VMEM)


def ring(axis, step):
    size = lax.axis_size(axis)
    return [(i, (i + step) % size) for i in range(size)]


def local(fields, norm_gain, w_query, w_key, w_value, w_out, mix_kernel, cotangent):
    members, rows, cols, width = fields.shape
    parts = lax.axis_size("mem")
    per = cols // parts
    cells = rows * per
    pad_cells = (rows + 2) * (per + 2)
    params = pltpu.CompilerParams(vmem_limit_bytes=40 * 1024 * 1024)

    split = jnp.asarray(split_matrix(parts, members, cols), BF)
    halo = jnp.asarray(halo_matrices(parts, members, rows, cols), BF)
    grid = (lax.axis_size("row"), lax.axis_size("col"))
    smem = pl.BlockSpec(memory_space=pltpu.SMEM)
    vmem = pl.BlockSpec(memory_space=pltpu.VMEM)
    with jax.named_scope("halo"):
        row, col = lax.axis_index("row"), lax.axis_index("col")
        place = jnp.stack([row, col]).astype(jnp.int32)
        before = lax.ppermute(cotangent[:, rows - 1], "row", ring("row", 1))
        after = lax.ppermute(cotangent[:, 0], "row", ring("row", -1))
        first = cotangent[:, :, 0].reshape(1, 1, members * rows, width)
        last = cotangent[:, :, cols - 1].reshape(1, 1, members * rows, width)
        to_right = (lax.iota(jnp.int32, grid[1]) == col + 1).reshape(1, grid[1], 1, 1)
        columns = jnp.broadcast_to(jnp.where(to_right, last, first), grid + (members * rows, width))
        columns = columns.reshape(grid[0] * grid[1], members * rows, width)
        got = lax.all_to_all(columns, ("row", "col"), 0, 0)

    with jax.named_scope("pack"):
        send = pl.pallas_call(
            functools.partial(pack_kernel, grid),
            in_specs=[smem] + [vmem] * 7,
            out_shape=pltpu.VMEM((parts, (cells + pad_cells) * members, width), BF),
            compiler_params=params,
        )(place, fields, cotangent, near(before), near(after), near(got), split, halo)
    with jax.named_scope("to_cells"):
        recv = lax.all_to_all(send, "mem", 0, 0)

    tokens = cells * members * parts
    base = cells * members
    shard = 4 * width // parts
    headsum = np.kron(np.eye(HEADS), np.ones((width // HEADS, width // HEADS)))
    with jax.named_scope("attention"):
        back = pl.pallas_call(
            functools.partial(main_kernel, rows, per),
            out_shape=pltpu.VMEM((parts, base + shard + 16, width), BF),
            scratch_shapes=[
                pltpu.VMEM((pad_cells, members * parts, width), F32),
                pltpu.VMEM((tokens, width), F32),
                pltpu.VMEM((tokens, width), F32),
                pltpu.VMEM((cells, width, width), BF),
                pltpu.VMEM((cells, width, width), BF),
            ],
            compiler_params=params,
        )(
            near(recv),
            norm_gain.reshape(1, width),
            mix_kernel,
            w_query,
            w_key,
            w_value,
            w_out,
            jnp.asarray(gather_matrix(parts, 8, members), BF),
            jnp.asarray(gather_matrix(parts, 4, members), BF),
            jnp.asarray(headsum, BF),
        )
    with jax.named_scope("to_members"):
        landed = lax.all_to_all(back, "mem", 0, 0)
    with jax.named_scope("unpack"):
        total = jnp.sum(landed[:, base:, :].astype(F32), axis=0)
        total = lax.optimization_barrier(total.astype(BF))
        grad_fields = pl.pallas_call(
            unpack_kernel,
            out_shape=jax.ShapeDtypeStruct(fields.shape, BF),
            compiler_params=params,
        )(near(landed), split)

    with jax.named_scope("reduce"):
        total = meet(total, "row", (1, 2, 3))
        total = meet(total, "col", (2, 4, 6))
        total = meet(total, "col", (1,))
        total, grad_fields = lax.optimization_barrier((total, grad_fields))
        piece = total[:shard]
        same_core = jnp.stack([piece] + [lax.ppermute(piece, "mem", partner("mem", k)) for k in (2, 4, 6)])
        same_core = lax.optimization_barrier(same_core)
        other_core = lax.ppermute(same_core, "mem", partner("mem", 1))

    scale_all = 1.0 / math.sqrt(tokens * grid[0] * grid[1] * parts)
    with jax.named_scope("finish"):
        square = jax.ShapeDtypeStruct((width, width), F32)
        own = lax.axis_index("mem").astype(jnp.int32).reshape(1)
        grads = pl.pallas_call(
            functools.partial(finish_kernel, scale_all),
            in_specs=[smem] + [vmem] * 3,
            out_shape=(square,) * 4 + (jax.ShapeDtypeStruct((3, 3, width), F32), jax.ShapeDtypeStruct((1, width), F32)),
            compiler_params=params,
        )(own, near(same_core), near(other_core), near(total))
    return (grad_fields, grads[5].reshape(width)) + tuple(grads[:5])


def solution(mesh):
    tile = P("mem", "row", "col", None)
    in_specs = (tile, P(), P(), P(), P(), P(), P(), tile)
    out_specs = (tile, P(), P(), P(), P(), P(), P())
    return jax.shard_map(local, mesh=mesh, in_specs=in_specs, out_specs=out_specs, check_vma=False)
```

```python
import functools
import math

import jax
import jax.numpy as jnp
import numpy as np
from jax import lax
from jax.experimental import pallas as pl
from jax.experimental.pallas import tpu as pltpu
from jax.sharding import PartitionSpec as P

HEADS = 8
EPS = 1e-06
BF = jnp.bfloat16
F32 = jnp.float32
NT = (((1,), (1,)), ((), ()))
TN = (((0,), (0,)), ((), ()))


def dot(a, b, dims=None):
    if dims is None:
        return jnp.dot(a, b, preferred_element_type=F32)
    return lax.dot_general(a, b, dims, preferred_element_type=F32)


def split_matrix(parts, members, cols):
    per = cols // parts
    out = np.zeros((parts, per, members, members, cols), np.float32)
    for j in range(parts):
        for c in range(per):
            for m in range(members):
                out[j, c, m, m, j * per + c] = 1
    return out.reshape(parts * per * members, members * cols)


def halo_matrices(parts, members, rows, cols):
    per = cols // parts
    edge = members * rows
    mats = []
    for pair in range(rows // 2):
        out = np.zeros((parts, 2, per + 2, members, 2 * members * cols + 2 * edge), np.float32)
        for j in range(parts):
            for q in range(2):
                for c in range(per + 2):
                    for m in range(members):
                        col = j * per + c - 1
                        if 0 <= col < cols:
                            src = (q * members + m) * cols + col
                        else:
                            side = 0 if col < 0 else 1
                            src = 2 * members * cols + side * edge + m * rows + 2 * pair + q
                        out[j, q, c, m, src] = 1
        mats.append(out.reshape(-1, out.shape[-1]))
    return np.stack(mats)


def gather_matrix(parts, cells, members):
    out = np.zeros((cells, parts, members, parts, cells, members), np.float32)
    for s in range(parts):
        for c in range(cells):
            for m in range(members):
                out[c, s, m, s, c, m] = 1
    return out.reshape(cells * parts * members, -1)


def masked(inside, x):
    return jnp.where(inside, x, jnp.zeros_like(x))


def pack_kernel(col_size, place, fields, cot, got, split, halo, send):
    members, rows, cols, width = fields.shape
    parts = send.shape[0]
    per = cols // parts * members
    for r in range(rows):
        tokens = fields[:, r].reshape(members * cols, width)
        moved = dot(split[...], tokens).astype(BF).reshape(parts, per, width)
        send[:, r * per : (r + 1) * per, :] = moved
    base = rows * per
    col = place[1]
    sides = [
        masked(col > 0, got[jnp.maximum(col - 1, 0)]),
        masked(col < col_size - 1, got[jnp.minimum(col + 1, col_size - 1)]),
    ]
    step = 2 * (per + 2 * members)
    for pair in range(rows // 2):
        lines = [cot[:, 2 * pair + q].reshape(members * cols, width) for q in range(2)]
        moved = dot(halo[pair], jnp.concatenate(lines + sides, axis=0)).astype(BF)
        send[:, base + pair * step : base + (pair + 1) * step, :] = moved.reshape(parts, step, width)


def regroup(recv, start, count, members, matrix):
    parts, _, width = recv.shape
    rows = count * members
    return dot(matrix[...], recv[:, start : start + rows, :].reshape(parts * rows, width))


def norm(x):
    inv = lax.rsqrt(jnp.mean(x * x, axis=-1, keepdims=True) + EPS)
    return inv, x * inv


def head_sums(v, headsum):
    hi = v.astype(BF)
    lo = (v - hi.astype(F32)).astype(BF)
    return dot(hi, headsum[...]) + dot(lo, headsum[...])


def expand_all(blocks, mats):
    cells, width, _ = mats.shape
    size = blocks.shape[0] // cells
    head_dim = width // HEADS
    row_head = lax.broadcasted_iota(jnp.int32, (width, width), 0) // head_dim
    col_head = lax.broadcasted_iota(jnp.int32, (width, width), 1) // head_dim
    same = row_head == col_head
    for c in range(cells):
        tiled = jnp.concatenate([blocks[c * size : (c + 1) * size]] * HEADS, axis=0)
        mats[c] = jnp.where(same, tiled, jnp.zeros_like(tiled))


def forward_kernel(
    members,
    recv,
    gain,
    wq,
    wk,
    wv,
    wo,
    gather8,
    headsum,
    x_out,
    q_out,
    k_out,
    v_out,
    prob_out,
    att_out,
    mixed_out,
    sums,
    mat_k,
    mat_v,
):
    parts, _, width = recv.shape
    scale = 1.0 / math.sqrt(width // HEADS)
    all_members = parts * members
    tokens = x_out.shape[0]
    cells = tokens // all_members
    x = jnp.concatenate([regroup(recv, g * 32, 8, members, gather8) for g in range(cells // 8)], axis=0)
    x_out[...] = x.astype(BF)
    _, normed = norm(x)
    inputs = (normed * gain[...]).astype(BF)
    queries = dot(inputs, wq[...]).astype(BF)
    keys = dot(inputs, wk[...]).astype(BF)
    values = dot(inputs, wv[...]).astype(BF)
    q_out[...] = queries
    k_out[...] = keys
    v_out[...] = values
    expand_all(keys, mat_k)
    expand_all(values, mat_v)
    for c in range(cells):
        rows = slice(c * all_members, (c + 1) * all_members)
        sums[rows, :] = dot(queries[rows], mat_k[c], NT)
    scores = sums[...] * scale
    lane = lax.broadcasted_iota(jnp.int32, (tokens, 128), 1)
    halves = []
    for h in range(width // 128):
        top = scores[:, h * 128 : (h + 1) * 128]
        step = 1
        while step < all_members:
            up = pltpu.roll(top, step, 1)
            down = pltpu.roll(top, 128 - step, 1)
            top = jnp.maximum(top, jnp.where((lane & step) != 0, up, down))
            step *= 2
        halves.append(top)
    lifted = jnp.exp(scores - jnp.concatenate(halves, axis=1))
    prob = lifted / head_sums(lifted, headsum)
    prob_out[...] = prob
    prob_b = prob.astype(BF)
    for c in range(cells):
        rows = slice(c * all_members, (c + 1) * all_members)
        att_out[rows, :] = dot(prob_b[rows], mat_v[c]).astype(BF)
    mixed_out[...] = dot(att_out[...], wo[...]).astype(BF)


def backward_kernel(
    tile_rows,
    tile_cols,
    members,
    row_size,
    place,
    recv,
    above,
    below,
    x_in,
    q_in,
    k_in,
    v_in,
    prob_in,
    att_in,
    mixed_in,
    gain,
    mix,
    wq,
    wk,
    wv,
    wo,
    gather8,
    gather6,
    headsum,
    send,
    padded,
    sums,
    mat_k,
    mat_v,
):
    parts, _, width = recv.shape
    head_dim = width // HEADS
    scale = 1.0 / math.sqrt(head_dim)
    cells = tile_rows * tile_cols
    all_members = parts * members
    tokens = cells * all_members
    pad_cols = tile_cols + 2
    pad_cells = (tile_rows + 2) * pad_cols
    base = cells * members
    row = place[0]
    top = dot(gather6[...], masked(row > 0, above[...]))
    padded[:pad_cols] = top.reshape(pad_cols, all_members, width)
    for g in range(tile_rows * pad_cols // 8):
        block = regroup(recv, base + g * 8 * members, 8, members, gather8)
        padded[pad_cols + g * 8 : pad_cols + (g + 1) * 8] = block.reshape(8, all_members, width)
    bottom = dot(gather6[...], masked(row < row_size - 1, below[...]))
    padded[pad_cells - pad_cols :] = bottom.reshape(pad_cols, all_members, width)

    def shifted(i, j):
        picked = [
            padded[(r + 2 - i) * pad_cols + 2 - j : (r + 2 - i) * pad_cols + 2 - j + tile_cols]
            for r in range(tile_rows)
        ]
        return jnp.concatenate(picked, axis=0).reshape(tokens, width)

    expand_all(k_in[...], mat_k)
    expand_all(v_in[...], mat_v)
    inv, normed = norm(x_in[...].astype(F32))
    inputs = (normed * gain[...]).astype(BF)
    mixed = mixed_in[...].astype(F32)
    extra = []
    conv = jnp.zeros((tokens, width), F32)
    for i in range(3):
        for j in range(3):
            moved = shifted(i, j)
            conv = conv + mix[i, j : j + 1, :] * moved
            extra.append(jnp.sum(mixed * moved, axis=0, keepdims=True))
    grad_mixed = conv.astype(BF)
    grad_att = dot(grad_mixed, wo[...], NT).astype(BF)
    for c in range(cells):
        rows = slice(c * all_members, (c + 1) * all_members)
        sums[rows, :] = dot(grad_att[rows], mat_v[c], NT)

    prob = prob_in[...]
    prob_b = prob.astype(BF)
    grad_prob = sums[...]
    inner = head_sums(prob * grad_prob, headsum)
    grad_score = (prob * (grad_prob - inner) * scale).astype(BF)
    lane_head = lax.broadcasted_iota(jnp.int32, (all_members, width), 1) // head_dim

    def diagonal(full):
        out = jnp.zeros((all_members, width), F32)
        for h in range(HEADS):
            out = jnp.where(lane_head == h, full[h * all_members : (h + 1) * all_members], out)
        return out

    gq_l, gk_l, gv_l = [], [], []
    for c in range(cells):
        rows = slice(c * all_members, (c + 1) * all_members)
        gq_l.append(dot(grad_score[rows], mat_k[c]).astype(BF))
        gk_l.append(diagonal(dot(grad_score[rows], q_in[rows, :], TN)).astype(BF))
        gv_l.append(diagonal(dot(prob_b[rows], grad_att[rows], TN)).astype(BF))
    grad_q = jnp.concatenate(gq_l, axis=0)
    grad_k = jnp.concatenate(gk_l, axis=0)
    grad_v = jnp.concatenate(gv_l, axis=0)

    grad_in = dot(grad_q, wq[...], NT) + dot(grad_k, wk[...], NT) + dot(grad_v, wv[...], NT)
    extra.append(jnp.sum(grad_in * normed, axis=0, keepdims=True))
    grad_normed = grad_in * gain[...]
    mean = jnp.mean(grad_normed * normed, axis=-1, keepdims=True)
    grad = (shifted(1, 1) + inv * (grad_normed - normed * mean)).astype(BF)
    for g in range(cells // 8):
        back = dot(gather8[...], grad[g * 256 : (g + 1) * 256], TN).astype(BF)
        send[:, g * 32 : (g + 1) * 32, :] = back.reshape(parts, 32, width)

    weights = [
        dot(inputs, grad_q, TN),
        dot(inputs, grad_k, TN),
        dot(inputs, grad_v, TN),
        dot(att_in[...], grad_mixed, TN),
    ]
    shard = 4 * width // parts
    for j in range(parts):
        which, start = divmod(j * shard, width)
        send[j, base : base + shard, :] = weights[which][start : start + shard].astype(BF)
    extras = jnp.concatenate(extra + [jnp.zeros((16 - len(extra), width), F32)], axis=0).astype(BF)
    for j in range(parts):
        send[j, base + shard : base + shard + 16, :] = extras


def unpack_kernel(recv, split, out):
    members, rows, cols, width = out.shape
    parts = recv.shape[0]
    per = cols // parts * members
    for r in range(rows):
        tokens = recv[:, r * per : (r + 1) * per, :].reshape(parts * per, width)
        out[:, r] = dot(split[...], tokens, TN).astype(BF).reshape(members, cols, width)


def finish_kernel(scale, place, same_core, other_core, total, g_q, g_k, g_v, g_o, g_mix, g_gain):
    count, shard, width = same_core.shape
    per = width // shard
    outs = (g_q, g_k, g_v, g_o)
    for p in range(2 * count):
        code = lax.bitwise_xor(place[0], p)
        spot = lax.shift_right_logical(code, 1)
        got = jnp.where(code == 2 * spot, same_core[spot], other_core[spot]).astype(F32)
        outs[p // per][p % per * shard : (p % per + 1) * shard, :] = got * scale
    rest = total[shard:, :].astype(F32) * scale
    for i in range(3):
        g_mix[i] = rest[3 * i : 3 * i + 3]
    g_gain[...] = rest[9:10]


def partner(axis, code):
    return [(i, i ^ code) for i in range(lax.axis_size(axis))]


def meet(values, axis, codes):
    got = [values] + [lax.ppermute(values, axis, partner(axis, k)) for k in codes]
    got = [x.astype(F32) for x in got]
    while len(got) > 1:
        got = [a + b for a, b in zip(got[::2], got[1::2])]
    return lax.optimization_barrier(got[0].astype(BF))


def near(x):
    return pltpu.with_memory_space_constraint(x, pltpu.VMEM)


def ring(axis, step):
    size = lax.axis_size(axis)
    return [(i, (i + step) % size) for i in range(size)]


def local(fields, norm_gain, w_query, w_key, w_value, w_out, mix_kernel, cotangent):
    members, rows, cols, width = fields.shape
    parts = lax.axis_size("mem")
    per = cols // parts
    cells = rows * per
    line = (per + 2) * members
    tokens = cells * members * parts
    base = cells * members
    shard = 4 * width // parts
    grid = (lax.axis_size("row"), lax.axis_size("col"))
    params = pltpu.CompilerParams(vmem_limit_bytes=40 * 1024 * 1024)
    smem = pl.BlockSpec(memory_space=pltpu.SMEM)
    vmem = pl.BlockSpec(memory_space=pltpu.VMEM)
    split = jnp.asarray(split_matrix(parts, members, cols), BF)
    halo = jnp.asarray(halo_matrices(parts, members, rows, cols), BF)
    gather8 = jnp.asarray(gather_matrix(parts, 8, members), BF)
    gather6 = jnp.asarray(gather_matrix(parts, per + 2, members), BF)
    headsum = jnp.asarray(np.kron(np.eye(HEADS), np.ones((width // HEADS, width // HEADS))), BF)
    gain = norm_gain.reshape(1, width)
    row, col = lax.axis_index("row"), lax.axis_index("col")
    place = jnp.stack([row, col]).astype(jnp.int32)

    with jax.named_scope("halo_cols"):
        first = cotangent[:, :, 0].reshape(1, members * rows, width)
        last = cotangent[:, :, cols - 1].reshape(1, members * rows, width)
        to_right = (lax.iota(jnp.int32, grid[1]) == col + 1).reshape(grid[1], 1, 1)
        got = lax.all_to_all(jnp.where(to_right, last, first), "col", 0, 0)
    with jax.named_scope("pack"):
        send = pl.pallas_call(
            functools.partial(pack_kernel, grid[1]),
            in_specs=[smem] + [vmem] * 5,
            out_shape=pltpu.VMEM((parts, base + rows * line, width), BF),
            compiler_params=params,
        )(place, fields, cotangent, near(got), split, halo)
    with jax.named_scope("to_cells"):
        recv = lax.all_to_all(send, "mem", 0, 0)
    with jax.named_scope("halo_rows"):
        top = recv[:, base : base + line].reshape(parts * line, width)
        bottom = recv[:, base + (rows - 1) * line :].reshape(parts * line, width)
        above = lax.ppermute(bottom, "row", ring("row", 1))
        below = lax.ppermute(top, "row", ring("row", -1))

    with jax.named_scope("forward"):
        token = pltpu.VMEM((tokens, width), BF)
        token_f = pltpu.VMEM((tokens, width), F32)
        mats = [pltpu.VMEM((cells, width, width), BF), pltpu.VMEM((cells, width, width), BF)]
        kept = pl.pallas_call(
            functools.partial(forward_kernel, members),
            out_shape=(token, token, token, token, token_f, token, token),
            scratch_shapes=[pltpu.VMEM((tokens, width), F32)] + mats,
            compiler_params=params,
        )(near(recv), gain, w_query, w_key, w_value, w_out, gather8, headsum)
    with jax.named_scope("backward"):
        back = pl.pallas_call(
            functools.partial(backward_kernel, rows, per, members, grid[0]),
            in_specs=[smem] + [vmem] * 19,
            out_shape=pltpu.VMEM((parts, base + shard + 16, width), BF),
            scratch_shapes=[
                pltpu.VMEM(((rows + 2) * (per + 2), members * parts, width), F32),
                pltpu.VMEM((tokens, width), F32),
            ]
            + mats,
            compiler_params=params,
        )(
            place,
            near(recv),
            near(above),
            near(below),
            *[near(x) for x in kept],
            gain,
            mix_kernel,
            w_query,
            w_key,
            w_value,
            w_out,
            gather8,
            gather6,
            headsum,
        )
    with jax.named_scope("to_members"):
        landed = lax.all_to_all(back, "mem", 0, 0)
    with jax.named_scope("unpack"):
        total = jnp.sum(landed[:, base:, :].astype(F32), axis=0)
        total = lax.optimization_barrier(total.astype(BF))
        grad_fields = pl.pallas_call(
            unpack_kernel,
            out_shape=jax.ShapeDtypeStruct(fields.shape, BF),
            compiler_params=params,
        )(near(landed), split)

    with jax.named_scope("reduce"):
        total = meet(total, "row", (1, 2, 3))
        total = meet(total, "col", (2, 4, 6))
        total = meet(total, "col", (1,))
        total, grad_fields = lax.optimization_barrier((total, grad_fields))
        piece = total[:shard]
        same_core = jnp.stack([piece] + [lax.ppermute(piece, "mem", partner("mem", k)) for k in (2, 4, 6)])
        same_core = lax.optimization_barrier(same_core)
        other_core = lax.ppermute(same_core, "mem", partner("mem", 1))

    scale_all = 1.0 / math.sqrt(tokens * grid[0] * grid[1] * parts)
    with jax.named_scope("finish"):
        square = jax.ShapeDtypeStruct((width, width), F32)
        own = lax.axis_index("mem").astype(jnp.int32).reshape(1)
        grads = pl.pallas_call(
            functools.partial(finish_kernel, scale_all),
            in_specs=[smem] + [vmem] * 3,
            out_shape=(square,) * 4 + (jax.ShapeDtypeStruct((3, 3, width), F32), jax.ShapeDtypeStruct((1, width), F32)),
            compiler_params=params,
        )(own, near(same_core), near(other_core), near(total))
    return (grad_fields, grads[5].reshape(width)) + tuple(grads[:5])


def solution(mesh):
    tile = P("mem", "row", "col", None)
    in_specs = (tile, P(), P(), P(), P(), P(), P(), tile)
    out_specs = (tile, P(), P(), P(), P(), P(), P())
    return jax.shard_map(local, mesh=mesh, in_specs=in_specs, out_specs=out_specs, check_vma=False)
```

```python
import functools
import math

import jax
import jax.numpy as jnp
import numpy as np
from jax import lax
from jax.experimental import pallas as pl
from jax.experimental.pallas import tpu as pltpu
from jax.sharding import PartitionSpec as P

HEADS = 8
EPS = 1e-06
BF = jnp.bfloat16
F32 = jnp.float32
NT = (((1,), (1,)), ((), ()))
TN = (((0,), (0,)), ((), ()))


def dot(a, b, dims=None):
    if dims is None:
        return jnp.dot(a, b, preferred_element_type=F32)
    return lax.dot_general(a, b, dims, preferred_element_type=F32)


def split_matrix(parts, members, cols):
    per = cols // parts
    out = np.zeros((parts, per, members, members, cols), np.float32)
    for j in range(parts):
        for c in range(per):
            for m in range(members):
                out[j, c, m, m, j * per + c] = 1
    return out.reshape(parts * per * members, members * cols)


def gather_matrix(parts, cells, members):
    out = np.zeros((cells, parts, members, parts, cells, members), np.float32)
    for s in range(parts):
        for c in range(cells):
            for m in range(members):
                out[c, s, m, s, c, m] = 1
    return out.reshape(cells * parts * members, -1)


def pack_kernel(fields, cot, split, send):
    members, rows, cols, width = fields.shape
    parts = send.shape[0]
    per = cols // parts * members
    for k, source in enumerate((fields, cot)):
        for r in range(rows):
            tokens = source[:, r].reshape(members * cols, width)
            moved = dot(split[...], tokens).astype(BF).reshape(parts, per, width)
            start = (k * rows + r) * per
            send[:, start : start + per, :] = moved


def order_kernel(members, recv, gather8, x_out, cot_out):
    rows, per, all_members, width = cot_out.shape
    cells = rows * per
    for g in range(cells // 8):
        x_out[g * 8 * all_members : (g + 1) * 8 * all_members, :] = regroup(recv, g * 8 * members, 8, members, gather8).astype(BF)
        block = regroup(recv, (cells + g * 8) * members, 8, members, gather8).astype(BF)
        cot_out[g * 8 // per : (g + 1) * 8 // per] = block.reshape(8 // per, per, all_members, width)


def regroup(recv, start, count, members, matrix):
    parts, _, width = recv.shape
    rows = count * members
    return dot(matrix[...], recv[:, start : start + rows, :].reshape(parts * rows, width))


def norm(x):
    inv = lax.rsqrt(jnp.mean(x * x, axis=-1, keepdims=True) + EPS)
    return inv, x * inv


def head_sums(v, headsum):
    hi = v.astype(BF)
    lo = (v - hi.astype(F32)).astype(BF)
    return dot(hi, headsum[...]) + dot(lo, headsum[...])


def expand_all(blocks, mats):
    cells, width, _ = mats.shape
    size = blocks.shape[0] // cells
    head_dim = width // HEADS
    row_head = lax.broadcasted_iota(jnp.int32, (width, width), 0) // head_dim
    col_head = lax.broadcasted_iota(jnp.int32, (width, width), 1) // head_dim
    same = row_head == col_head
    for c in range(cells):
        tiled = jnp.concatenate([blocks[c * size : (c + 1) * size]] * HEADS, axis=0)
        mats[c] = jnp.where(same, tiled, jnp.zeros_like(tiled))


def forward_kernel(
    cells,
    x_in,
    gain,
    wq,
    wk,
    wv,
    wo,
    headsum,
    q_out,
    prob_out,
    att_out,
    mixed_out,
    mat_k,
    mat_v,
    sums,
):
    tokens, width = x_in.shape
    scale = 1.0 / math.sqrt(width // HEADS)
    all_members = tokens // cells
    x = x_in[...].astype(F32)
    _, normed = norm(x)
    inputs = (normed * gain[...]).astype(BF)
    queries = dot(inputs, wq[...]).astype(BF)
    keys = dot(inputs, wk[...]).astype(BF)
    values = dot(inputs, wv[...]).astype(BF)
    q_out[...] = queries
    expand_all(keys, mat_k)
    expand_all(values, mat_v)
    for c in range(cells):
        rows = slice(c * all_members, (c + 1) * all_members)
        sums[rows, :] = dot(queries[rows], mat_k[c], NT)
    scores = sums[...] * scale
    lane = lax.broadcasted_iota(jnp.int32, (tokens, 128), 1)
    halves = []
    for h in range(width // 128):
        top = scores[:, h * 128 : (h + 1) * 128]
        step = 1
        while step < all_members:
            up = pltpu.roll(top, step, 1)
            down = pltpu.roll(top, 128 - step, 1)
            top = jnp.maximum(top, jnp.where((lane & step) != 0, up, down))
            step *= 2
        halves.append(top)
    lifted = jnp.exp(scores - jnp.concatenate(halves, axis=1))
    prob = lifted / head_sums(lifted, headsum)
    prob_out[...] = prob
    prob_b = prob.astype(BF)
    for c in range(cells):
        rows = slice(c * all_members, (c + 1) * all_members)
        att_out[rows, :] = dot(prob_b[rows], mat_v[c]).astype(BF)
    mixed_out[...] = dot(att_out[...], wo[...]).astype(BF)


def backward_kernel(
    sizes,
    place,
    cot,
    left,
    right,
    above,
    below,
    x_in,
    q_in,
    prob_in,
    att_in,
    mixed_in,
    mat_k,
    mat_v,
    gain,
    mix,
    wq,
    wk,
    wv,
    wo,
    gather8,
    headsum,
    send,
    padded,
    sums,
):
    parts = send.shape[0]
    tile_rows, tile_cols, all_members, width = cot.shape
    members = all_members // parts
    head_dim = width // HEADS
    scale = 1.0 / math.sqrt(head_dim)
    cells = tile_rows * tile_cols
    tokens = cells * all_members
    pad_cols = tile_cols + 2
    base = cells * members
    row, block = place[0], place[1]

    def side(inside, x):
        x = x.astype(F32)
        return jnp.where(inside, x, jnp.zeros_like(x))

    in_left, in_right = block > 0, block < sizes[1] - 1
    edges = {0: (above, row > 0), tile_rows + 1: (below, row < sizes[0] - 1)}
    for r in range(tile_rows + 2):
        start = r * pad_cols
        if r in edges:
            source, inside = edges[r]
            padded[start] = side(inside & in_left, source[0])
            padded[start + 1 : start + 1 + tile_cols] = side(inside, source[1 : 1 + tile_cols])
            padded[start + 1 + tile_cols] = side(inside & in_right, source[1 + tile_cols])
        else:
            padded[start] = side(in_left, left[r - 1])
            padded[start + 1 : start + 1 + tile_cols] = cot[r - 1].astype(F32)
            padded[start + 1 + tile_cols] = side(in_right, right[r - 1])

    def shifted(i, j):
        picked = [
            padded[(r + 2 - i) * pad_cols + 2 - j : (r + 2 - i) * pad_cols + 2 - j + tile_cols]
            for r in range(tile_rows)
        ]
        return jnp.concatenate(picked, axis=0).reshape(tokens, width)

    inv, normed = norm(x_in[...].astype(F32))
    inputs = (normed * gain[...]).astype(BF)
    mixed = mixed_in[...].astype(F32)
    extra = []
    conv = jnp.zeros((tokens, width), F32)
    for i in range(3):
        for j in range(3):
            moved = shifted(i, j)
            conv = conv + mix[i, j : j + 1, :] * moved
            extra.append(jnp.sum(mixed * moved, axis=0, keepdims=True))
    grad_mixed = conv.astype(BF)
    grad_att = dot(grad_mixed, wo[...], NT).astype(BF)
    for c in range(cells):
        rows = slice(c * all_members, (c + 1) * all_members)
        sums[rows, :] = dot(grad_att[rows], mat_v[c], NT)

    prob = prob_in[...]
    prob_b = prob.astype(BF)
    grad_prob = sums[...]
    inner = head_sums(prob * grad_prob, headsum)
    grad_score = (prob * (grad_prob - inner) * scale).astype(BF)
    lane_head = lax.broadcasted_iota(jnp.int32, (all_members, width), 1) // head_dim

    def diagonal(full):
        out = jnp.zeros((all_members, width), F32)
        for h in range(HEADS):
            out = jnp.where(lane_head == h, full[h * all_members : (h + 1) * all_members], out)
        return out

    gq_l, gk_l, gv_l = [], [], []
    for c in range(cells):
        rows = slice(c * all_members, (c + 1) * all_members)
        gq_l.append(dot(grad_score[rows], mat_k[c]).astype(BF))
        gk_l.append(diagonal(dot(grad_score[rows], q_in[rows, :], TN)).astype(BF))
        gv_l.append(diagonal(dot(prob_b[rows], grad_att[rows], TN)).astype(BF))
    grad_q = jnp.concatenate(gq_l, axis=0)
    grad_k = jnp.concatenate(gk_l, axis=0)
    grad_v = jnp.concatenate(gv_l, axis=0)

    grad_in = dot(grad_q, wq[...], NT) + dot(grad_k, wk[...], NT) + dot(grad_v, wv[...], NT)
    extra.append(jnp.sum(grad_in * normed, axis=0, keepdims=True))
    grad_normed = grad_in * gain[...]
    mean = jnp.mean(grad_normed * normed, axis=-1, keepdims=True)
    grad = (shifted(1, 1) + inv * (grad_normed - normed * mean)).astype(BF)
    for g in range(cells // 8):
        back = dot(gather8[...], grad[g * 256 : (g + 1) * 256], TN).astype(BF)
        send[:, g * 32 : (g + 1) * 32, :] = back.reshape(parts, 32, width)

    weights = [
        dot(inputs, grad_q, TN),
        dot(inputs, grad_k, TN),
        dot(inputs, grad_v, TN),
        dot(att_in[...], grad_mixed, TN),
    ]
    shard = 4 * width // parts
    for j in range(parts):
        which, start = divmod(j * shard, width)
        send[j, base : base + shard, :] = weights[which][start : start + shard].astype(BF)
    extras = jnp.concatenate(extra + [jnp.zeros((16 - len(extra), width), F32)], axis=0).astype(BF)
    for j in range(parts):
        send[j, base + shard : base + shard + 16, :] = extras


def unpack_kernel(recv, split, out):
    members, rows, cols, width = out.shape
    parts = recv.shape[0]
    per = cols // parts * members
    for r in range(rows):
        tokens = recv[:, r * per : (r + 1) * per, :].reshape(parts * per, width)
        out[:, r] = dot(split[...], tokens, TN).astype(BF).reshape(members, cols, width)


def finish_kernel(scale, place, same_core, other_core, total, g_q, g_k, g_v, g_o, g_mix, g_gain):
    count, shard, width = same_core.shape
    per = width // shard
    outs = (g_q, g_k, g_v, g_o)
    for p in range(2 * count):
        code = lax.bitwise_xor(place[0], p)
        spot = lax.shift_right_logical(code, 1)
        got = jnp.where(code == 2 * spot, same_core[spot], other_core[spot]).astype(F32)
        outs[p // per][p % per * shard : (p % per + 1) * shard, :] = got * scale
    rest = total[shard:, :].astype(F32) * scale
    for i in range(3):
        g_mix[i] = rest[3 * i : 3 * i + 3]
    g_gain[...] = rest[9:10]


def partner(axis, code):
    return [(i, i ^ code) for i in range(lax.axis_size(axis))]


def meet(values, axis, codes):
    got = [values] + [lax.ppermute(values, axis, partner(axis, k)) for k in codes]
    got = [x.astype(F32) for x in got]
    while len(got) > 1:
        got = [a + b for a, b in zip(got[::2], got[1::2])]
    return lax.optimization_barrier(got[0].astype(BF))


def near(x):
    return pltpu.with_memory_space_constraint(x, pltpu.VMEM)


def ring(axis, step):
    size = lax.axis_size(axis)
    return [(i, (i + step) % size) for i in range(size)]


def local(fields, norm_gain, w_query, w_key, w_value, w_out, mix_kernel, cotangent):
    members, rows, cols, width = fields.shape
    parts = lax.axis_size("mem")
    per = cols // parts
    cells = rows * per
    tokens = cells * members * parts
    base = cells * members
    shard = 4 * width // parts
    grid = (lax.axis_size("row"), lax.axis_size("col"))
    params = pltpu.CompilerParams(vmem_limit_bytes=40 * 1024 * 1024)
    smem = pl.BlockSpec(memory_space=pltpu.SMEM)
    vmem = pl.BlockSpec(memory_space=pltpu.VMEM)
    split = jnp.asarray(split_matrix(parts, members, cols), BF)
    gather8 = jnp.asarray(gather_matrix(parts, 8, members), BF)
    headsum = jnp.asarray(np.kron(np.eye(HEADS), np.ones((width // HEADS, width // HEADS))), BF)
    gain = norm_gain.reshape(1, width)
    blocks = parts * grid[1]
    place = jnp.stack([lax.axis_index("row"), lax.axis_index("col") * parts + lax.axis_index("mem")]).astype(jnp.int32)

    with jax.named_scope("pack"):
        send = pl.pallas_call(
            pack_kernel,
            out_shape=pltpu.VMEM((parts, 2 * base, width), BF),
            compiler_params=params,
        )(fields, cotangent, split)
    with jax.named_scope("to_cells"):
        recv = lax.all_to_all(send, "mem", 0, 0)
    with jax.named_scope("order"):
        x, cot = pl.pallas_call(
            functools.partial(order_kernel, members),
            out_shape=(pltpu.VMEM((tokens, width), BF), pltpu.VMEM((rows, per, parts * members, width), BF)),
            compiler_params=params,
        )(near(recv), gather8)
    with jax.named_scope("halo_cols"):
        flat = [b % parts * grid[1] + b // parts for b in range(blocks)]
        up = list(zip(flat, flat[1:] + flat[:1]))
        down = [(j, i) for i, j in up]
        left = lax.ppermute(cot[:, per - 1], ("mem", "col"), up)
        right = lax.ppermute(cot[:, 0], ("mem", "col"), down)
    with jax.named_scope("forward"):
        token = pltpu.VMEM((tokens, width), BF)
        token_f = pltpu.VMEM((tokens, width), F32)
        mat = pltpu.VMEM((cells, width, width), BF)
        kept = pl.pallas_call(
            functools.partial(forward_kernel, cells),
            out_shape=(token, token_f, token, token, mat, mat),
            scratch_shapes=[pltpu.VMEM((tokens, width), F32)],
            compiler_params=params,
        )(near(x), gain, w_query, w_key, w_value, w_out, headsum)
    with jax.named_scope("halo_rows"):
        top, bottom = [jnp.concatenate([left[r : r + 1], cot[r], right[r : r + 1]], axis=0) for r in (0, rows - 1)]
        above = lax.ppermute(bottom, "row", ring("row", 1))
        below = lax.ppermute(top, "row", ring("row", -1))
    with jax.named_scope("backward"):
        back = pl.pallas_call(
            functools.partial(backward_kernel, (grid[0], blocks)),
            in_specs=[smem] + [vmem] * 20,
            out_shape=pltpu.VMEM((parts, base + shard + 16, width), BF),
            scratch_shapes=[
                pltpu.VMEM(((rows + 2) * (per + 2), members * parts, width), F32),
                pltpu.VMEM((tokens, width), F32),
            ],
            compiler_params=params,
        )(
            place,
            *[near(a) for a in (cot, left, right, above, below, x, *kept)],
            gain,
            mix_kernel,
            w_query,
            w_key,
            w_value,
            w_out,
            gather8,
            headsum,
        )
    with jax.named_scope("to_members"):
        landed = lax.all_to_all(back, "mem", 0, 0)
    with jax.named_scope("unpack"):
        total = jnp.sum(landed[:, base:, :].astype(F32), axis=0)
        total = lax.optimization_barrier(total.astype(BF))
        grad_fields = pl.pallas_call(
            unpack_kernel,
            out_shape=jax.ShapeDtypeStruct(fields.shape, BF),
            compiler_params=params,
        )(near(landed), split)

    with jax.named_scope("reduce"):
        total = meet(total, "row", (1, 2, 3))
        total = meet(total, "col", (2, 4, 6))
        total = meet(total, "col", (1,))
        total, grad_fields = lax.optimization_barrier((total, grad_fields))
        piece = total[:shard]
        same_core = jnp.stack([piece] + [lax.ppermute(piece, "mem", partner("mem", k)) for k in (2, 4, 6)])
        same_core = lax.optimization_barrier(same_core)
        other_core = lax.ppermute(same_core, "mem", partner("mem", 1))

    scale_all = 1.0 / math.sqrt(tokens * grid[0] * grid[1] * parts)
    with jax.named_scope("finish"):
        square = jax.ShapeDtypeStruct((width, width), F32)
        own = lax.axis_index("mem").astype(jnp.int32).reshape(1)
        grads = pl.pallas_call(
            functools.partial(finish_kernel, scale_all),
            in_specs=[smem] + [vmem] * 3,
            out_shape=(square,) * 4 + (jax.ShapeDtypeStruct((3, 3, width), F32), jax.ShapeDtypeStruct((1, width), F32)),
            compiler_params=params,
        )(own, near(same_core), near(other_core), near(total))
    return (grad_fields, grads[5].reshape(width)) + tuple(grads[:5])


def solution(mesh):
    tile = P("mem", "row", "col", None)
    in_specs = (tile, P(), P(), P(), P(), P(), P(), tile)
    out_specs = (tile, P(), P(), P(), P(), P(), P())
    return jax.shard_map(local, mesh=mesh, in_specs=in_specs, out_specs=out_specs, check_vma=False)
```

```python
import functools
import math

import jax
import jax.numpy as jnp
import numpy as np
from jax import lax
from jax.experimental import pallas as pl
from jax.experimental.pallas import tpu as pltpu
from jax.sharding import PartitionSpec as P

HEADS = 8
EPS = 1e-06
BF = jnp.bfloat16
F32 = jnp.float32
NT = (((1,), (1,)), ((), ()))
TN = (((0,), (0,)), ((), ()))


def dot(a, b, dims=None):
    if dims is None:
        return jnp.dot(a, b, preferred_element_type=F32)
    return lax.dot_general(a, b, dims, preferred_element_type=F32)


def snake(place, parts):
    return jnp.where(place % 2 == 0, place // 2, parts - 1 - place // 2)


def split_matrix(parts, members, cols):
    size = members * cols
    per = cols // parts
    out = lax.broadcasted_iota(jnp.int32, (size, size), 0)
    src = lax.broadcasted_iota(jnp.int32, (size, size), 1)
    part, col, member = out // (per * members), out // members % per, out % members
    hit = (src // cols == member) & (src % cols == snake(part, parts) * per + col)
    return jnp.where(hit, 1.0, 0.0).astype(BF)


def gather_matrix(parts, cells, members):
    out = np.zeros((cells, parts, members, parts, cells, members), np.float32)
    for s in range(parts):
        for c in range(cells):
            for m in range(members):
                out[c, s, m, s, c, m] = 1
    return out.reshape(cells * parts * members, -1)


def pack_kernel(fields, cot, send):
    members, rows, cols, width = fields.shape
    parts = send.shape[0]
    per = cols // parts * members
    split = split_matrix(parts, members, cols)
    for k, source in enumerate((fields, cot)):
        for r in range(rows):
            tokens = source[:, r].reshape(members * cols, width)
            moved = dot(split, tokens).astype(BF).reshape(parts, per, width)
            start = (k * rows + r) * per
            send[:, start : start + per, :] = moved


def order_kernel(members, recv, gather8, x_out, cot_out):
    rows, per, all_members, width = cot_out.shape
    cells = rows * per
    for g in range(cells // 8):
        x_out[g * 8 * all_members : (g + 1) * 8 * all_members, :] = regroup(recv, g * 8 * members, 8, members, gather8).astype(BF)
        block = regroup(recv, (cells + g * 8) * members, 8, members, gather8).astype(BF)
        cot_out[g * 8 // per : (g + 1) * 8 // per] = block.reshape(8 // per, per, all_members, width)


def regroup(recv, start, count, members, matrix):
    parts, _, width = recv.shape
    rows = count * members
    return dot(matrix[...], recv[:, start : start + rows, :].reshape(parts * rows, width))


def norm(x):
    inv = lax.rsqrt(jnp.mean(x * x, axis=-1, keepdims=True) + EPS)
    return inv, x * inv


def head_sums(v, headsum):
    hi = v.astype(BF)
    lo = (v - hi.astype(F32)).astype(BF)
    return dot(hi, headsum[...]) + dot(lo, headsum[...])


def expand_all(blocks, mats):
    cells, width, _ = mats.shape
    size = blocks.shape[0] // cells
    head_dim = width // HEADS
    row_head = lax.broadcasted_iota(jnp.int32, (width, width), 0) // head_dim
    col_head = lax.broadcasted_iota(jnp.int32, (width, width), 1) // head_dim
    same = row_head == col_head
    for c in range(cells):
        tiled = jnp.concatenate([blocks[c * size : (c + 1) * size]] * HEADS, axis=0)
        mats[c] = jnp.where(same, tiled, jnp.zeros_like(tiled))


def forward_kernel(
    cells,
    x_in,
    gain,
    wq,
    wk,
    wv,
    wo,
    headsum,
    q_out,
    prob_out,
    att_out,
    mixed_out,
    mat_k,
    mat_v,
    sums,
):
    tokens, width = x_in.shape
    scale = 1.0 / math.sqrt(width // HEADS)
    all_members = tokens // cells
    x = x_in[...].astype(F32)
    _, normed = norm(x)
    inputs = (normed * gain[...]).astype(BF)
    queries = dot(inputs, wq[...]).astype(BF)
    keys = dot(inputs, wk[...]).astype(BF)
    values = dot(inputs, wv[...]).astype(BF)
    q_out[...] = queries
    expand_all(keys, mat_k)
    expand_all(values, mat_v)
    for c in range(cells):
        rows = slice(c * all_members, (c + 1) * all_members)
        sums[rows, :] = dot(queries[rows], mat_k[c], NT)
    scores = sums[...] * scale
    lane = lax.broadcasted_iota(jnp.int32, (tokens, 128), 1)
    halves = []
    for h in range(width // 128):
        top = scores[:, h * 128 : (h + 1) * 128]
        step = 1
        while step < all_members:
            up = pltpu.roll(top, step, 1)
            down = pltpu.roll(top, 128 - step, 1)
            top = jnp.maximum(top, jnp.where((lane & step) != 0, up, down))
            step *= 2
        halves.append(top)
    lifted = jnp.exp(scores - jnp.concatenate(halves, axis=1))
    prob = lifted / head_sums(lifted, headsum)
    prob_out[...] = prob
    prob_b = prob.astype(BF)
    for c in range(cells):
        rows = slice(c * all_members, (c + 1) * all_members)
        att_out[rows, :] = dot(prob_b[rows], mat_v[c]).astype(BF)
    mixed_out[...] = dot(att_out[...], wo[...]).astype(BF)


def backward_kernel(
    sizes,
    place,
    cot,
    left,
    right,
    above,
    below,
    x_in,
    q_in,
    prob_in,
    att_in,
    mixed_in,
    mat_k,
    mat_v,
    gain,
    mix,
    wq,
    wk,
    wv,
    wo,
    gather8,
    headsum,
    send,
    padded,
    sums,
):
    parts = send.shape[0]
    tile_rows, tile_cols, all_members, width = cot.shape
    members = all_members // parts
    head_dim = width // HEADS
    scale = 1.0 / math.sqrt(head_dim)
    cells = tile_rows * tile_cols
    tokens = cells * all_members
    pad_cols = tile_cols + 2
    base = cells * members
    row, block = place[0], place[1]

    def side(inside, x):
        x = x.astype(F32)
        return jnp.where(inside, x, jnp.zeros_like(x))

    in_left, in_right = block > 0, block < sizes[1] - 1
    edges = {0: (above, row > 0), tile_rows + 1: (below, row < sizes[0] - 1)}
    for r in range(tile_rows + 2):
        start = r * pad_cols
        if r in edges:
            source, inside = edges[r]
            padded[start] = side(inside & in_left, source[0])
            padded[start + 1 : start + 1 + tile_cols] = side(inside, source[1 : 1 + tile_cols])
            padded[start + 1 + tile_cols] = side(inside & in_right, source[1 + tile_cols])
        else:
            padded[start] = side(in_left, left[r - 1])
            padded[start + 1 : start + 1 + tile_cols] = cot[r - 1].astype(F32)
            padded[start + 1 + tile_cols] = side(in_right, right[r - 1])

    def shifted(i, j):
        picked = [
            padded[(r + 2 - i) * pad_cols + 2 - j : (r + 2 - i) * pad_cols + 2 - j + tile_cols]
            for r in range(tile_rows)
        ]
        return jnp.concatenate(picked, axis=0).reshape(tokens, width)

    inv, normed = norm(x_in[...].astype(F32))
    inputs = (normed * gain[...]).astype(BF)
    mixed = mixed_in[...].astype(F32)
    extra = []
    conv = jnp.zeros((tokens, width), F32)
    for i in range(3):
        for j in range(3):
            moved = shifted(i, j)
            conv = conv + mix[i, j : j + 1, :] * moved
            extra.append(jnp.sum(mixed * moved, axis=0, keepdims=True))
    grad_mixed = conv.astype(BF)
    grad_att = dot(grad_mixed, wo[...], NT).astype(BF)
    for c in range(cells):
        rows = slice(c * all_members, (c + 1) * all_members)
        sums[rows, :] = dot(grad_att[rows], mat_v[c], NT)

    prob = prob_in[...]
    prob_b = prob.astype(BF)
    grad_prob = sums[...]
    inner = head_sums(prob * grad_prob, headsum)
    grad_score = (prob * (grad_prob - inner) * scale).astype(BF)
    lane_head = lax.broadcasted_iota(jnp.int32, (all_members, width), 1) // head_dim

    def diagonal(full):
        out = jnp.zeros((all_members, width), F32)
        for h in range(HEADS):
            out = jnp.where(lane_head == h, full[h * all_members : (h + 1) * all_members], out)
        return out

    gq_l, gk_l, gv_l = [], [], []
    for c in range(cells):
        rows = slice(c * all_members, (c + 1) * all_members)
        gq_l.append(dot(grad_score[rows], mat_k[c]).astype(BF))
        gk_l.append(diagonal(dot(grad_score[rows], q_in[rows, :], TN)).astype(BF))
        gv_l.append(diagonal(dot(prob_b[rows], grad_att[rows], TN)).astype(BF))
    grad_q = jnp.concatenate(gq_l, axis=0)
    grad_k = jnp.concatenate(gk_l, axis=0)
    grad_v = jnp.concatenate(gv_l, axis=0)

    grad_in = dot(grad_q, wq[...], NT) + dot(grad_k, wk[...], NT) + dot(grad_v, wv[...], NT)
    extra.append(jnp.sum(grad_in * normed, axis=0, keepdims=True))
    grad_normed = grad_in * gain[...]
    mean = jnp.mean(grad_normed * normed, axis=-1, keepdims=True)
    grad = (shifted(1, 1) + inv * (grad_normed - normed * mean)).astype(BF)
    for g in range(cells // 8):
        back = dot(gather8[...], grad[g * 256 : (g + 1) * 256], TN).astype(BF)
        send[:, g * 32 : (g + 1) * 32, :] = back.reshape(parts, 32, width)

    weights = [
        dot(inputs, grad_q, TN),
        dot(inputs, grad_k, TN),
        dot(inputs, grad_v, TN),
        dot(att_in[...], grad_mixed, TN),
    ]
    shard = 4 * width // parts
    for j in range(parts):
        which, start = divmod(j * shard, width)
        send[j, base : base + shard, :] = weights[which][start : start + shard].astype(BF)
    extras = jnp.concatenate(extra + [jnp.zeros((16 - len(extra), width), F32)], axis=0).astype(BF)
    for j in range(parts):
        send[j, base + shard : base + shard + 16, :] = extras


def unpack_kernel(recv, out):
    members, rows, cols, width = out.shape
    parts = recv.shape[0]
    per = cols // parts * members
    split = split_matrix(parts, members, cols)
    for r in range(rows):
        tokens = recv[:, r * per : (r + 1) * per, :].reshape(parts * per, width)
        out[:, r] = dot(split, tokens, TN).astype(BF).reshape(members, cols, width)


def finish_kernel(scale, place, same_core, other_core, total, g_q, g_k, g_v, g_o, g_mix, g_gain):
    count, shard, width = same_core.shape
    per = width // shard
    outs = (g_q, g_k, g_v, g_o)
    for p in range(2 * count):
        code = lax.bitwise_xor(place[0], p)
        spot = lax.shift_right_logical(code, 1)
        got = jnp.where(code == 2 * spot, same_core[spot], other_core[spot]).astype(F32)
        outs[p // per][p % per * shard : (p % per + 1) * shard, :] = got * scale
    rest = total[shard:, :].astype(F32) * scale
    for i in range(3):
        g_mix[i] = rest[3 * i : 3 * i + 3]
    g_gain[...] = rest[9:10]


def partner(axis, code):
    return [(i, i ^ code) for i in range(lax.axis_size(axis))]


def meet(values, axis, codes):
    got = [values] + [lax.ppermute(values, axis, partner(axis, k)) for k in codes]
    got = [x.astype(F32) for x in got]
    while len(got) > 1:
        got = [a + b for a, b in zip(got[::2], got[1::2])]
    return lax.optimization_barrier(got[0].astype(BF))


def near(x):
    return pltpu.with_memory_space_constraint(x, pltpu.VMEM)


def swap(last, first, spot, axis, where, wrap):
    size = len(where)
    got = []
    for odd in (0, 1):
        pairs = []
        for a in range(odd, size if wrap else size - 1, 2):
            b = (a + 1) % size
            pairs += [(where[a], where[b]), (where[b], where[a])]
        got.append(lax.ppermute(jnp.where(spot % 2 == odd, last, first), axis, pairs))
    even = spot % 2 == 0
    return jnp.where(even, got[0], got[1]), jnp.where(even, got[1], got[0])


def local(fields, norm_gain, w_query, w_key, w_value, w_out, mix_kernel, cotangent):
    members, rows, cols, width = fields.shape
    parts = lax.axis_size("mem")
    per = cols // parts
    cells = rows * per
    tokens = cells * members * parts
    base = cells * members
    shard = 4 * width // parts
    grid = (lax.axis_size("row"), lax.axis_size("col"))
    params = pltpu.CompilerParams(vmem_limit_bytes=40 * 1024 * 1024)
    smem = pl.BlockSpec(memory_space=pltpu.SMEM)
    vmem = pl.BlockSpec(memory_space=pltpu.VMEM)
    gather8 = jnp.asarray(gather_matrix(parts, 8, members), BF)
    headsum = jnp.asarray(np.kron(np.eye(HEADS), np.ones((width // HEADS, width // HEADS))), BF)
    gain = norm_gain.reshape(1, width)
    blocks = parts * grid[1]
    block = lax.axis_index("col") * parts + snake(lax.axis_index("mem"), parts)
    place = jnp.stack([lax.axis_index("row"), block]).astype(jnp.int32)

    with jax.named_scope("pack"):
        send = pl.pallas_call(
            pack_kernel,
            out_shape=pltpu.VMEM((parts, 2 * base, width), BF),
            compiler_params=params,
        )(fields, cotangent)
    with jax.named_scope("to_cells"):
        recv = lax.all_to_all(send, "mem", 0, 0)
    with jax.named_scope("order"):
        x, cot = pl.pallas_call(
            functools.partial(order_kernel, members),
            out_shape=(pltpu.VMEM((tokens, width), BF), pltpu.VMEM((rows, per, parts * members, width), BF)),
            compiler_params=params,
        )(near(recv), gather8)
        x, w_query, w_key, w_value, w_out = lax.optimization_barrier((x, w_query, w_key, w_value, w_out))
    with jax.named_scope("halo_cols"):
        where = {}
        for mem in range(parts):
            inner = mem // 2 if mem % 2 == 0 else parts - 1 - mem // 2
            for c in range(grid[1]):
                where[c * parts + inner] = mem * grid[1] + c
        right, left = swap(cot[:, per - 1], cot[:, 0], block, ("mem", "col"), where, True)
    with jax.named_scope("forward"):
        token = pltpu.VMEM((tokens, width), BF)
        token_f = pltpu.VMEM((tokens, width), F32)
        mat = pltpu.VMEM((cells, width, width), BF)
        kept = pl.pallas_call(
            functools.partial(forward_kernel, cells),
            out_shape=(token, token_f, token, token, mat, mat),
            scratch_shapes=[pltpu.VMEM((tokens, width), F32)],
            compiler_params=params,
        )(near(x), gain, w_query, w_key, w_value, w_out, headsum)
    with jax.named_scope("halo_rows"):
        top, bottom = [jnp.concatenate([left[r : r + 1], cot[r], right[r : r + 1]], axis=0) for r in (0, rows - 1)]
        rows_at = {r: r for r in range(grid[0])}
        below, above = swap(bottom, top, lax.axis_index("row"), "row", rows_at, False)
    with jax.named_scope("backward"):
        back = pl.pallas_call(
            functools.partial(backward_kernel, (grid[0], blocks)),
            in_specs=[smem] + [vmem] * 20,
            out_shape=pltpu.VMEM((parts, base + shard + 16, width), BF),
            scratch_shapes=[
                pltpu.VMEM(((rows + 2) * (per + 2), members * parts, width), F32),
                pltpu.VMEM((tokens, width), F32),
            ],
            compiler_params=params,
        )(
            place,
            *[near(a) for a in (cot, left, right, above, below, x, *kept)],
            gain,
            mix_kernel,
            w_query,
            w_key,
            w_value,
            w_out,
            gather8,
            headsum,
        )
    with jax.named_scope("to_members"):
        landed = lax.all_to_all(back, "mem", 0, 0)
    with jax.named_scope("unpack"):
        total = jnp.sum(landed[:, base:, :].astype(F32), axis=0)
        total = lax.optimization_barrier(total.astype(BF))
        grad_fields = pl.pallas_call(
            unpack_kernel,
            out_shape=jax.ShapeDtypeStruct(fields.shape, BF),
            compiler_params=params,
        )(near(landed))

    with jax.named_scope("reduce"):
        total = meet(total, "row", (1, 2, 3))
        total = meet(total, "col", (2, 4, 6))
        total = meet(total, "col", (1,))
        total, grad_fields = lax.optimization_barrier((total, grad_fields))
        piece = total[:shard]
        same_core = jnp.stack([piece] + [lax.ppermute(piece, "mem", partner("mem", k)) for k in (2, 4, 6)])
        same_core = lax.optimization_barrier(same_core)
        other_core = lax.ppermute(same_core, "mem", partner("mem", 1))

    scale_all = 1.0 / math.sqrt(tokens * grid[0] * grid[1] * parts)
    with jax.named_scope("finish"):
        square = jax.ShapeDtypeStruct((width, width), F32)
        own = lax.axis_index("mem").astype(jnp.int32).reshape(1)
        grads = pl.pallas_call(
            functools.partial(finish_kernel, scale_all),
            in_specs=[smem] + [vmem] * 3,
            out_shape=(square,) * 4 + (jax.ShapeDtypeStruct((3, 3, width), F32), jax.ShapeDtypeStruct((1, width), F32)),
            compiler_params=params,
        )(own, near(same_core), near(other_core), near(total))
    return (grad_fields, grads[5].reshape(width)) + tuple(grads[:5])


def solution(mesh):
    tile = P("mem", "row", "col", None)
    in_specs = (tile, P(), P(), P(), P(), P(), P(), tile)
    out_specs = (tile, P(), P(), P(), P(), P(), P())
    return jax.shard_map(local, mesh=mesh, in_specs=in_specs, out_specs=out_specs, check_vma=False)
```

```python
import functools
import math

import jax
import jax.numpy as jnp
import numpy as np
from jax import lax
from jax.experimental import pallas as pl
from jax.experimental.pallas import tpu as pltpu
from jax.sharding import PartitionSpec as P

HEADS = 8
EPS = 1e-06
BF = jnp.bfloat16
F32 = jnp.float32
NT = (((1,), (1,)), ((), ()))
TN = (((0,), (0,)), ((), ()))


def dot(a, b, dims=None):
    if dims is None:
        return jnp.dot(a, b, preferred_element_type=F32)
    return lax.dot_general(a, b, dims, preferred_element_type=F32)


def snake(place, parts):
    return jnp.where(place % 2 == 0, place // 2, parts - 1 - place // 2)


def split_matrix(parts, members, cols):
    size = members * cols
    per = cols // parts
    out = lax.broadcasted_iota(jnp.int32, (size, size), 0)
    src = lax.broadcasted_iota(jnp.int32, (size, size), 1)
    part, col, member = out // (per * members), out // members % per, out % members
    hit = (src // cols == member) & (src % cols == snake(part, parts) * per + col)
    return jnp.where(hit, 1.0, 0.0).astype(BF)


def gather_matrix(parts, cells, members):
    out = np.zeros((cells, parts, members, parts, cells, members), np.float32)
    for s in range(parts):
        for c in range(cells):
            for m in range(members):
                out[c, s, m, s, c, m] = 1
    return out.reshape(cells * parts * members, -1)


def pack_kernel(fields, cot, send):
    members, rows, cols, width = fields.shape
    parts = send.shape[0]
    per = cols // parts * members
    split = split_matrix(parts, members, cols)
    for k, source in enumerate((fields, cot)):
        for r in range(rows):
            tokens = source[:, r].reshape(members * cols, width)
            moved = dot(split, tokens).astype(BF).reshape(parts, per, width)
            start = (k * rows + r) * per
            send[:, start : start + per, :] = moved


def order_kernel(members, recv, gather8, x_out, cot_out):
    rows, per, all_members, width = cot_out.shape
    cells = rows * per
    for g in range(cells // 8):
        x_out[g * 8 * all_members : (g + 1) * 8 * all_members, :] = regroup(recv, g * 8 * members, 8, members, gather8).astype(BF)
        block = regroup(recv, (cells + g * 8) * members, 8, members, gather8).astype(BF)
        cot_out[g * 8 // per : (g + 1) * 8 // per] = block.reshape(8 // per, per, all_members, width)


def regroup(recv, start, count, members, matrix):
    parts, _, width = recv.shape
    rows = count * members
    return dot(matrix[...], recv[:, start : start + rows, :].reshape(parts * rows, width))


def norm(x):
    inv = lax.rsqrt(jnp.mean(x * x, axis=-1, keepdims=True) + EPS)
    return inv, x * inv


def head_sums(v, headsum):
    hi = v.astype(BF)
    lo = (v - hi.astype(F32)).astype(BF)
    return dot(hi, headsum[...]) + dot(lo, headsum[...])


def expand_all(blocks, mats):
    cells, width, _ = mats.shape
    size = blocks.shape[0] // cells
    head_dim = width // HEADS
    row_head = lax.broadcasted_iota(jnp.int32, (width, width), 0) // head_dim
    col_head = lax.broadcasted_iota(jnp.int32, (width, width), 1) // head_dim
    same = row_head == col_head
    for c in range(cells):
        tiled = jnp.concatenate([blocks[c * size : (c + 1) * size]] * HEADS, axis=0)
        mats[c] = jnp.where(same, tiled, jnp.zeros_like(tiled))


def forward_kernel(
    cells,
    x_in,
    gain,
    wq,
    wk,
    wv,
    wo,
    headsum,
    q_out,
    prob_out,
    att_out,
    mixed_out,
    mat_k,
    mat_v,
    sums,
):
    tokens, width = x_in.shape
    scale = 1.0 / math.sqrt(width // HEADS)
    all_members = tokens // cells
    x = x_in[...].astype(F32)
    _, normed = norm(x)
    inputs = (normed * gain[...]).astype(BF)
    queries = dot(inputs, wq[...]).astype(BF)
    keys = dot(inputs, wk[...]).astype(BF)
    values = dot(inputs, wv[...]).astype(BF)
    q_out[...] = queries
    expand_all(keys, mat_k)
    expand_all(values, mat_v)
    for c in range(cells):
        rows = slice(c * all_members, (c + 1) * all_members)
        sums[rows, :] = dot(queries[rows], mat_k[c], NT)
    scores = sums[...] * scale
    lane = lax.broadcasted_iota(jnp.int32, (tokens, 128), 1)
    halves = []
    for h in range(width // 128):
        top = scores[:, h * 128 : (h + 1) * 128]
        step = 1
        while step < all_members:
            up = pltpu.roll(top, step, 1)
            down = pltpu.roll(top, 128 - step, 1)
            top = jnp.maximum(top, jnp.where((lane & step) != 0, up, down))
            step *= 2
        halves.append(top)
    lifted = jnp.exp(scores - jnp.concatenate(halves, axis=1))
    prob = lifted / head_sums(lifted, headsum)
    prob_out[...] = prob
    prob_b = prob.astype(BF)
    for c in range(cells):
        rows = slice(c * all_members, (c + 1) * all_members)
        att_out[rows, :] = dot(prob_b[rows], mat_v[c]).astype(BF)
    mixed_out[...] = dot(att_out[...], wo[...]).astype(BF)


def backward_kernel(picked, sizes, ends, place, cot, left, right, *refs):
    if ends:
        above, below, part_in, grads_in, extra_in = refs[:5]
        refs = refs[5:]
    x_in, q_in, prob_in, att_in, mixed_in, mat_k, mat_v, gain, mix, wq, wk, wv, wo, gather8, headsum = refs[:15]
    outs, (padded, sums) = refs[15:-2], refs[-2:]
    tile_rows, tile_cols, all_members, width = cot.shape
    head_dim = width // HEADS
    scale = 1.0 / math.sqrt(head_dim)
    pad_cols = tile_cols + 2
    line = tile_cols * all_members
    cells = [r * tile_cols + c for r in picked for c in range(tile_cols)]
    tokens = len(cells) * all_members
    row, block = place[0], place[1]

    def pick(ref):
        return jnp.concatenate([ref[r * line : (r + 1) * line, :] for r in picked], axis=0)

    def side(inside, x):
        x = x.astype(F32)
        return jnp.where(inside, x, jnp.zeros_like(x))

    in_left, in_right = block > 0, block < sizes[1] - 1
    for r in range(tile_rows + 2):
        start = r * pad_cols
        if 0 < r <= tile_rows:
            padded[start] = side(in_left, left[r - 1])
            padded[start + 1 : start + 1 + tile_cols] = cot[r - 1].astype(F32)
            padded[start + 1 + tile_cols] = side(in_right, right[r - 1])
        elif ends:
            source, inside = (above, row > 0) if r == 0 else (below, row < sizes[0] - 1)
            padded[start] = side(inside & in_left, source[0])
            padded[start + 1 : start + 1 + tile_cols] = side(inside, source[1 : 1 + tile_cols])
            padded[start + 1 + tile_cols] = side(inside & in_right, source[1 + tile_cols])

    def shifted(i, j):
        moved = [
            padded[(r + 2 - i) * pad_cols + 2 - j : (r + 2 - i) * pad_cols + 2 - j + tile_cols] for r in picked
        ]
        return jnp.concatenate(moved, axis=0).reshape(tokens, width)

    inv, normed = norm(pick(x_in).astype(F32))
    inputs = (normed * gain[...]).astype(BF)
    queries = pick(q_in)
    attended = pick(att_in)
    mixed = pick(mixed_in).astype(F32)
    extra = []
    conv = jnp.zeros((tokens, width), F32)
    for i in range(3):
        for j in range(3):
            moved = shifted(i, j)
            conv = conv + mix[i, j : j + 1, :] * moved
            extra.append(jnp.sum(mixed * moved, axis=0, keepdims=True))
    grad_mixed = conv.astype(BF)
    grad_att = dot(grad_mixed, wo[...], NT).astype(BF)
    for k, c in enumerate(cells):
        rows = slice(k * all_members, (k + 1) * all_members)
        sums[rows, :] = dot(grad_att[rows], mat_v[c], NT)

    prob = pick(prob_in)
    prob_b = prob.astype(BF)
    grad_prob = sums[...]
    inner = head_sums(prob * grad_prob, headsum)
    grad_score = (prob * (grad_prob - inner) * scale).astype(BF)
    lane_head = lax.broadcasted_iota(jnp.int32, (all_members, width), 1) // head_dim

    def diagonal(full):
        out = jnp.zeros((all_members, width), F32)
        for h in range(HEADS):
            out = jnp.where(lane_head == h, full[h * all_members : (h + 1) * all_members], out)
        return out

    gq_l, gk_l, gv_l = [], [], []
    for k, c in enumerate(cells):
        rows = slice(k * all_members, (k + 1) * all_members)
        gq_l.append(dot(grad_score[rows], mat_k[c]).astype(BF))
        gk_l.append(diagonal(dot(grad_score[rows], queries[rows], TN)).astype(BF))
        gv_l.append(diagonal(dot(prob_b[rows], grad_att[rows], TN)).astype(BF))
    grad_q = jnp.concatenate(gq_l, axis=0)
    grad_k = jnp.concatenate(gk_l, axis=0)
    grad_v = jnp.concatenate(gv_l, axis=0)

    grad_in = dot(grad_q, wq[...], NT) + dot(grad_k, wk[...], NT) + dot(grad_v, wv[...], NT)
    extra.append(jnp.sum(grad_in * normed, axis=0, keepdims=True))
    grad_normed = grad_in * gain[...]
    mean = jnp.mean(grad_normed * normed, axis=-1, keepdims=True)
    grad = (shifted(1, 1) + inv * (grad_normed - normed * mean)).astype(BF)
    back = dot(gather8[...], grad, TN).astype(BF)
    weights = [
        dot(inputs, grad_q, TN),
        dot(inputs, grad_k, TN),
        dot(inputs, grad_v, TN),
        dot(attended, grad_mixed, TN),
    ]
    extras = jnp.concatenate(extra + [jnp.zeros((16 - len(extra), width), F32)], axis=0)
    if not ends:
        part_out, grads_out, extra_out = outs
        part_out[...] = back.reshape(part_out.shape)
        for k in range(4):
            grads_out[k] = weights[k]
        extra_out[...] = extras
        return
    (send,) = outs
    parts = send.shape[0]
    members = all_members // parts
    base = tile_rows * tile_cols * members
    shard = 4 * width // parts
    step = tile_cols * members
    back = back.reshape(parts, len(picked) * step, width)
    for k, r in enumerate(picked):
        send[:, r * step : (r + 1) * step, :] = back[:, k * step : (k + 1) * step]
    send[:, step : base - step, :] = part_in[...]
    for j in range(parts):
        which, start = divmod(j * shard, width)
        total = weights[which][start : start + shard] + grads_in[which, start : start + shard, :]
        send[j, base : base + shard, :] = total.astype(BF)
        send[j, base + shard : base + shard + 16, :] = (extras + extra_in[...]).astype(BF)


def unpack_kernel(recv, out):
    members, rows, cols, width = out.shape
    parts = recv.shape[0]
    per = cols // parts * members
    split = split_matrix(parts, members, cols)
    for r in range(rows):
        tokens = recv[:, r * per : (r + 1) * per, :].reshape(parts * per, width)
        out[:, r] = dot(split, tokens, TN).astype(BF).reshape(members, cols, width)


def finish_kernel(scale, place, same_core, other_core, total, g_q, g_k, g_v, g_o, g_mix, g_gain):
    count, shard, width = same_core.shape
    per = width // shard
    outs = (g_q, g_k, g_v, g_o)
    for p in range(2 * count):
        code = lax.bitwise_xor(place[0], p)
        spot = lax.shift_right_logical(code, 1)
        got = jnp.where(code == 2 * spot, same_core[spot], other_core[spot]).astype(F32)
        outs[p // per][p % per * shard : (p % per + 1) * shard, :] = got * scale
    rest = total[shard:, :].astype(F32) * scale
    for i in range(3):
        g_mix[i] = rest[3 * i : 3 * i + 3]
    g_gain[...] = rest[9:10]


def partner(axis, code):
    return [(i, i ^ code) for i in range(lax.axis_size(axis))]


def meet(values, axis, codes):
    got = [values] + [lax.ppermute(values, axis, partner(axis, k)) for k in codes]
    got = [x.astype(F32) for x in got]
    while len(got) > 1:
        got = [a + b for a, b in zip(got[::2], got[1::2])]
    return lax.optimization_barrier(got[0].astype(BF))


def near(x):
    return pltpu.with_memory_space_constraint(x, pltpu.VMEM)


def swap(last, first, spot, axis, where, wrap):
    size = len(where)
    got = []
    for odd in (0, 1):
        pairs = []
        for a in range(odd, size if wrap else size - 1, 2):
            b = (a + 1) % size
            pairs += [(where[a], where[b]), (where[b], where[a])]
        got.append(lax.ppermute(jnp.where(spot % 2 == odd, last, first), axis, pairs))
    even = spot % 2 == 0
    return jnp.where(even, got[0], got[1]), jnp.where(even, got[1], got[0])


def local(fields, norm_gain, w_query, w_key, w_value, w_out, mix_kernel, cotangent):
    members, rows, cols, width = fields.shape
    parts = lax.axis_size("mem")
    per = cols // parts
    cells = rows * per
    tokens = cells * members * parts
    base = cells * members
    shard = 4 * width // parts
    grid = (lax.axis_size("row"), lax.axis_size("col"))
    params = pltpu.CompilerParams(vmem_limit_bytes=40 * 1024 * 1024)
    smem = pl.BlockSpec(memory_space=pltpu.SMEM)
    vmem = pl.BlockSpec(memory_space=pltpu.VMEM)
    gather8 = jnp.asarray(gather_matrix(parts, 8, members), BF)
    headsum = jnp.asarray(np.kron(np.eye(HEADS), np.ones((width // HEADS, width // HEADS))), BF)
    gain = norm_gain.reshape(1, width)
    blocks = parts * grid[1]
    block = lax.axis_index("col") * parts + snake(lax.axis_index("mem"), parts)
    place = jnp.stack([lax.axis_index("row"), block]).astype(jnp.int32)

    with jax.named_scope("pack"):
        send = pl.pallas_call(
            pack_kernel,
            out_shape=pltpu.VMEM((parts, 2 * base, width), BF),
            compiler_params=params,
        )(fields, cotangent)
    with jax.named_scope("to_cells"):
        recv = lax.all_to_all(send, "mem", 0, 0)
    with jax.named_scope("order"):
        x, cot = pl.pallas_call(
            functools.partial(order_kernel, members),
            out_shape=(pltpu.VMEM((tokens, width), BF), pltpu.VMEM((rows, per, parts * members, width), BF)),
            compiler_params=params,
        )(near(recv), gather8)
        x, w_query, w_key, w_value, w_out = lax.optimization_barrier((x, w_query, w_key, w_value, w_out))
    with jax.named_scope("halo_cols"):
        where = {}
        for mem in range(parts):
            inner = mem // 2 if mem % 2 == 0 else parts - 1 - mem // 2
            for c in range(grid[1]):
                where[c * parts + inner] = mem * grid[1] + c
        right, left = swap(cot[:, per - 1], cot[:, 0], block, ("mem", "col"), where, True)
    with jax.named_scope("forward"):
        token = pltpu.VMEM((tokens, width), BF)
        token_f = pltpu.VMEM((tokens, width), F32)
        mat = pltpu.VMEM((cells, width, width), BF)
        kept = pl.pallas_call(
            functools.partial(forward_kernel, cells),
            out_shape=(token, token_f, token, token, mat, mat),
            scratch_shapes=[pltpu.VMEM((tokens, width), F32)],
            compiler_params=params,
        )(near(x), gain, w_query, w_key, w_value, w_out, headsum)
    left, right, *kept = lax.optimization_barrier((left, right, *kept))
    with jax.named_scope("halo_rows"):
        top, bottom = [jnp.concatenate([left[r : r + 1], cot[r], right[r : r + 1]], axis=0) for r in (0, rows - 1)]
        rows_at = {r: r for r in range(grid[0])}
        below, above = swap(bottom, top, lax.axis_index("row"), "row", rows_at, False)

    half = tokens // 2
    scratch = [
        pltpu.VMEM(((rows + 2) * (per + 2), members * parts, width), F32),
        pltpu.VMEM((half, width), F32),
    ]
    halo = [near(a) for a in (cot, left, right)]
    rest = [near(a) for a in (x, *kept)] + [gain, mix_kernel, w_query, w_key, w_value, w_out, gather8, headsum]
    with jax.named_scope("backward_inner"):
        inner = pl.pallas_call(
            functools.partial(backward_kernel, tuple(range(1, rows - 1)), (grid[0], blocks), False),
            in_specs=[smem] + [vmem] * 18,
            out_shape=(
                pltpu.VMEM((parts, base // 2, width), BF),
                pltpu.VMEM((4, width, width), F32),
                pltpu.VMEM((16, width), F32),
            ),
            scratch_shapes=scratch,
            compiler_params=params,
        )(place, *halo, *rest)
    with jax.named_scope("backward_ends"):
        back = pl.pallas_call(
            functools.partial(backward_kernel, (0, rows - 1), (grid[0], blocks), True),
            in_specs=[smem] + [vmem] * 23,
            out_shape=pltpu.VMEM((parts, base + shard + 16, width), BF),
            scratch_shapes=scratch,
            compiler_params=params,
        )(place, *halo, *[near(a) for a in (above, below, *inner)], *rest)
    with jax.named_scope("to_members"):
        landed = lax.all_to_all(back, "mem", 0, 0)
    with jax.named_scope("unpack"):
        total = jnp.sum(landed[:, base:, :].astype(F32), axis=0)
        total = lax.optimization_barrier(total.astype(BF))
        grad_fields = pl.pallas_call(
            unpack_kernel,
            out_shape=jax.ShapeDtypeStruct(fields.shape, BF),
            compiler_params=params,
        )(near(landed))

    with jax.named_scope("reduce"):
        total = meet(total, "row", (1, 2, 3))
        total = meet(total, "col", (2, 4, 6))
        total = meet(total, "col", (1,))
        total, grad_fields = lax.optimization_barrier((total, grad_fields))
        piece = total[:shard]
        same_core = jnp.stack([piece] + [lax.ppermute(piece, "mem", partner("mem", k)) for k in (2, 4, 6)])
        same_core = lax.optimization_barrier(same_core)
        other_core = lax.ppermute(same_core, "mem", partner("mem", 1))

    scale_all = 1.0 / math.sqrt(tokens * grid[0] * grid[1] * parts)
    with jax.named_scope("finish"):
        square = jax.ShapeDtypeStruct((width, width), F32)
        own = lax.axis_index("mem").astype(jnp.int32).reshape(1)
        grads = pl.pallas_call(
            functools.partial(finish_kernel, scale_all),
            in_specs=[smem] + [vmem] * 3,
            out_shape=(square,) * 4 + (jax.ShapeDtypeStruct((3, 3, width), F32), jax.ShapeDtypeStruct((1, width), F32)),
            compiler_params=params,
        )(own, near(same_core), near(other_core), near(total))
    return (grad_fields, grads[5].reshape(width)) + tuple(grads[:5])


def solution(mesh):
    tile = P("mem", "row", "col", None)
    in_specs = (tile, P(), P(), P(), P(), P(), P(), tile)
    out_specs = (tile, P(), P(), P(), P(), P(), P())
    return jax.shard_map(local, mesh=mesh, in_specs=in_specs, out_specs=out_specs, check_vma=False)
```

```python
import functools
import math

import jax
import jax.numpy as jnp
import numpy as np
from jax import lax
from jax.experimental import pallas as pl
from jax.experimental.pallas import tpu as pltpu
from jax.sharding import PartitionSpec as P

HEADS = 8
EPS = 1e-06
BF = jnp.bfloat16
F32 = jnp.float32
NT = (((1,), (1,)), ((), ()))
TN = (((0,), (0,)), ((), ()))


def dot(a, b, dims=None):
    if dims is None:
        return jnp.dot(a, b, preferred_element_type=F32)
    return lax.dot_general(a, b, dims, preferred_element_type=F32)


def snake(place, parts):
    return jnp.where(place % 2 == 0, place // 2, parts - 1 - place // 2)


def split_matrix(parts, members, cols):
    size = members * cols
    per = cols // parts
    out = lax.broadcasted_iota(jnp.int32, (size, size), 0)
    src = lax.broadcasted_iota(jnp.int32, (size, size), 1)
    part, col, member = out // (per * members), out // members % per, out % members
    hit = (src // cols == member) & (src % cols == snake(part, parts) * per + col)
    return jnp.where(hit, 1.0, 0.0).astype(BF)


def gather_matrix(parts, cells, members):
    out = np.zeros((cells, parts, members, parts, cells, members), np.float32)
    for s in range(parts):
        for c in range(cells):
            for m in range(members):
                out[c, s, m, s, c, m] = 1
    return out.reshape(cells * parts * members, -1)


def pack_kernel(fields, cot, send, held, sems):
    members, rows, cols, width = fields.shape
    parts = send.shape[0]
    per = cols // parts * members
    copies = []
    for k, source in enumerate((fields, cot)):
        for r in range(rows):
            copies.append(pltpu.make_async_copy(source.at[:, r], held.at[k, r], sems.at[k, r]))
    for copy in copies:
        copy.start()
    split = split_matrix(parts, members, cols)
    for k in range(2):
        for r in range(rows):
            copies[k * rows + r].wait()
            tokens = held[k, r].reshape(members * cols, width)
            moved = dot(split, tokens).astype(BF).reshape(parts, per, width)
            start = (k * rows + r) * per
            send[:, start : start + per, :] = moved


def order_kernel(members, recv, gather8, x_out, cot_out):
    rows, per, all_members, width = cot_out.shape
    cells = rows * per
    for g in range(cells // 8):
        x_out[g * 8 * all_members : (g + 1) * 8 * all_members, :] = regroup(recv, g * 8 * members, 8, members, gather8).astype(BF)
        block = regroup(recv, (cells + g * 8) * members, 8, members, gather8).astype(BF)
        cot_out[g * 8 // per : (g + 1) * 8 // per] = block.reshape(8 // per, per, all_members, width)


def regroup(recv, start, count, members, matrix):
    parts, _, width = recv.shape
    rows = count * members
    return dot(matrix[...], recv[:, start : start + rows, :].reshape(parts * rows, width))


def norm(x):
    inv = lax.rsqrt(jnp.mean(x * x, axis=-1, keepdims=True) + EPS)
    return inv, x * inv


def head_sums(v, headsum):
    hi = v.astype(BF)
    lo = (v - hi.astype(F32)).astype(BF)
    return dot(hi, headsum[...]) + dot(lo, headsum[...])


def expand_all(blocks, mats):
    cells, width, _ = mats.shape
    size = blocks.shape[0] // cells
    head_dim = width // HEADS
    row_head = lax.broadcasted_iota(jnp.int32, (width, width), 0) // head_dim
    col_head = lax.broadcasted_iota(jnp.int32, (width, width), 1) // head_dim
    same = row_head == col_head
    for c in range(cells):
        tiled = jnp.concatenate([blocks[c * size : (c + 1) * size]] * HEADS, axis=0)
        mats[c] = jnp.where(same, tiled, jnp.zeros_like(tiled))


def forward_kernel(
    cells,
    x_in,
    gain,
    wq,
    wk,
    wv,
    wo,
    headsum,
    q_out,
    prob_out,
    att_out,
    mixed_out,
    mat_k,
    mat_v,
    sums,
):
    tokens, width = x_in.shape
    scale = 1.0 / math.sqrt(width // HEADS)
    all_members = tokens // cells
    x = x_in[...].astype(F32)
    _, normed = norm(x)
    inputs = (normed * gain[...]).astype(BF)
    queries = dot(inputs, wq[...]).astype(BF)
    keys = dot(inputs, wk[...]).astype(BF)
    values = dot(inputs, wv[...]).astype(BF)
    q_out[...] = queries
    expand_all(keys, mat_k)
    expand_all(values, mat_v)
    for c in range(cells):
        rows = slice(c * all_members, (c + 1) * all_members)
        sums[rows, :] = dot(queries[rows], mat_k[c], NT)
    scores = sums[...] * scale
    lane = lax.broadcasted_iota(jnp.int32, (tokens, 128), 1)
    halves = []
    for h in range(width // 128):
        top = scores[:, h * 128 : (h + 1) * 128]
        step = 1
        while step < all_members:
            up = pltpu.roll(top, step, 1)
            down = pltpu.roll(top, 128 - step, 1)
            top = jnp.maximum(top, jnp.where((lane & step) != 0, up, down))
            step *= 2
        halves.append(top)
    lifted = jnp.exp(scores - jnp.concatenate(halves, axis=1))
    prob = lifted / head_sums(lifted, headsum)
    prob_out[...] = prob
    prob_b = prob.astype(BF)
    for c in range(cells):
        rows = slice(c * all_members, (c + 1) * all_members)
        att_out[rows, :] = dot(prob_b[rows], mat_v[c]).astype(BF)
    mixed_out[...] = dot(att_out[...], wo[...]).astype(BF)


def backward_kernel(picked, sizes, outer, place, cot, above, below, *refs):
    if outer:
        left, right, part_in, grads_in, extra_in = refs[:5]
        refs = refs[5:]
    x_in, q_in, prob_in, att_in, mixed_in, mat_k, mat_v, gain, mix, wq, wk, wv, wo, gather8, headsum = refs[:15]
    outs, (padded, sums) = refs[15:-2], refs[-2:]
    tile_rows, tile_cols, all_members, width = cot.shape
    head_dim = width // HEADS
    scale = 1.0 / math.sqrt(head_dim)
    pad_cols = tile_cols + 2
    spots = [(r, c) for r in range(tile_rows) for c in picked]
    cells = [r * tile_cols + c for r, c in spots]
    tokens = len(cells) * all_members
    row, block = place[0], place[1]

    def pick(ref):
        return jnp.concatenate([ref[c * all_members : (c + 1) * all_members, :] for c in cells], axis=0)

    def side(inside, x):
        x = x.astype(F32)
        return jnp.where(inside, x, jnp.zeros_like(x))

    in_left, in_right = block > 0, block < sizes[1] - 1
    in_above, in_below = row > 0, row < sizes[0] - 1
    padded[1 : 1 + tile_cols] = side(in_above, above[...])
    padded[(tile_rows + 1) * pad_cols + 1 : (tile_rows + 1) * pad_cols + 1 + tile_cols] = side(in_below, below[...])
    for r in range(tile_rows):
        padded[(r + 1) * pad_cols + 1 : (r + 1) * pad_cols + 1 + tile_cols] = cot[r].astype(F32)
    if outer:
        for r in range(tile_rows + 2):
            near_l, near_r = in_left, in_right
            if r == 0:
                near_l, near_r = in_left & in_above, in_right & in_above
            elif r == tile_rows + 1:
                near_l, near_r = in_left & in_below, in_right & in_below
            padded[r * pad_cols] = side(near_l, left[r])
            padded[r * pad_cols + 1 + tile_cols] = side(near_r, right[r])

    def shifted(i, j):
        moved = [padded[(r + 2 - i) * pad_cols + c + 2 - j] for r, c in spots]
        return jnp.concatenate(moved, axis=0)

    inv, normed = norm(pick(x_in).astype(F32))
    inputs = (normed * gain[...]).astype(BF)
    queries = pick(q_in)
    attended = pick(att_in)
    mixed = pick(mixed_in).astype(F32)
    extra = []
    conv = jnp.zeros((tokens, width), F32)
    for i in range(3):
        for j in range(3):
            moved = shifted(i, j)
            conv = conv + mix[i, j : j + 1, :] * moved
            extra.append(jnp.sum(mixed * moved, axis=0, keepdims=True))
    grad_mixed = conv.astype(BF)
    grad_att = dot(grad_mixed, wo[...], NT).astype(BF)
    for k, c in enumerate(cells):
        rows = slice(k * all_members, (k + 1) * all_members)
        sums[rows, :] = dot(grad_att[rows], mat_v[c], NT)

    prob = pick(prob_in)
    prob_b = prob.astype(BF)
    grad_prob = sums[...]
    inner = head_sums(prob * grad_prob, headsum)
    grad_score = (prob * (grad_prob - inner) * scale).astype(BF)
    lane_head = lax.broadcasted_iota(jnp.int32, (all_members, width), 1) // head_dim

    def diagonal(full):
        out = jnp.zeros((all_members, width), F32)
        for h in range(HEADS):
            out = jnp.where(lane_head == h, full[h * all_members : (h + 1) * all_members], out)
        return out

    gq_l, gk_l, gv_l = [], [], []
    for k, c in enumerate(cells):
        rows = slice(k * all_members, (k + 1) * all_members)
        gq_l.append(dot(grad_score[rows], mat_k[c]).astype(BF))
        gk_l.append(diagonal(dot(grad_score[rows], queries[rows], TN)).astype(BF))
        gv_l.append(diagonal(dot(prob_b[rows], grad_att[rows], TN)).astype(BF))
    grad_q = jnp.concatenate(gq_l, axis=0)
    grad_k = jnp.concatenate(gk_l, axis=0)
    grad_v = jnp.concatenate(gv_l, axis=0)

    grad_in = dot(grad_q, wq[...], NT) + dot(grad_k, wk[...], NT) + dot(grad_v, wv[...], NT)
    extra.append(jnp.sum(grad_in * normed, axis=0, keepdims=True))
    grad_normed = grad_in * gain[...]
    mean = jnp.mean(grad_normed * normed, axis=-1, keepdims=True)
    grad = (shifted(1, 1) + inv * (grad_normed - normed * mean)).astype(BF)
    weights = [
        dot(inputs, grad_q, TN),
        dot(inputs, grad_k, TN),
        dot(inputs, grad_v, TN),
        dot(attended, grad_mixed, TN),
    ]
    extras = jnp.concatenate(extra + [jnp.zeros((16 - len(extra), width), F32)], axis=0)
    if not outer:
        part_out, grads_out, extra_out = outs
        part_out[...] = grad
        for k in range(4):
            grads_out[k] = weights[k]
        extra_out[...] = extras
        return
    (send,) = outs
    parts = send.shape[0]
    members = all_members // parts
    base = tile_rows * tile_cols * members
    shard = 4 * width // parts
    done = {c: grad[k * all_members : (k + 1) * all_members] for k, c in enumerate(cells)}
    others = [c for c in range(tile_rows * tile_cols) if c not in done]
    for k, c in enumerate(others):
        done[c] = part_in[k * all_members : (k + 1) * all_members, :]
    for g in range(len(done) // 8):
        group = jnp.concatenate([done[c] for c in range(g * 8, (g + 1) * 8)], axis=0)
        back = dot(gather8[...], group, TN).astype(BF)
        send[:, g * 8 * members : (g + 1) * 8 * members, :] = back.reshape(parts, 8 * members, width)
    for j in range(parts):
        which, start = divmod(j * shard, width)
        total = weights[which][start : start + shard] + grads_in[which, start : start + shard, :]
        send[j, base : base + shard, :] = total.astype(BF)
        send[j, base + shard : base + shard + 16, :] = (extras + extra_in[...]).astype(BF)


def unpack_kernel(recv, out):
    members, rows, cols, width = out.shape
    parts = recv.shape[0]
    per = cols // parts * members
    split = split_matrix(parts, members, cols)
    for r in range(rows):
        tokens = recv[:, r * per : (r + 1) * per, :].reshape(parts * per, width)
        out[:, r] = dot(split, tokens, TN).astype(BF).reshape(members, cols, width)


def finish_kernel(scale, place, same_core, other_core, total, g_q, g_k, g_v, g_o, g_mix, g_gain):
    count, shard, width = same_core.shape
    per = width // shard
    outs = (g_q, g_k, g_v, g_o)
    for p in range(2 * count):
        code = lax.bitwise_xor(place[0], p)
        spot = lax.shift_right_logical(code, 1)
        got = jnp.where(code == 2 * spot, same_core[spot], other_core[spot]).astype(F32)
        outs[p // per][p % per * shard : (p % per + 1) * shard, :] = got * scale
    rest = total[shard:, :].astype(F32) * scale
    for i in range(3):
        g_mix[i] = rest[3 * i : 3 * i + 3]
    g_gain[...] = rest[9:10]


def partner(axis, code):
    return [(i, i ^ code) for i in range(lax.axis_size(axis))]


def meet(values, axis, codes):
    got = [values] + [lax.ppermute(values, axis, partner(axis, k)) for k in codes]
    got = [x.astype(F32) for x in got]
    while len(got) > 1:
        got = [a + b for a, b in zip(got[::2], got[1::2])]
    return lax.optimization_barrier(got[0].astype(BF))


def near(x):
    return pltpu.with_memory_space_constraint(x, pltpu.VMEM)


def swap(last, first, spot, axis, where, wrap):
    size = len(where)
    got = []
    for odd in (0, 1):
        pairs = []
        for a in range(odd, size if wrap else size - 1, 2):
            b = (a + 1) % size
            pairs += [(where[a], where[b]), (where[b], where[a])]
        got.append(lax.ppermute(jnp.where(spot % 2 == odd, last, first), axis, pairs))
    even = spot % 2 == 0
    return jnp.where(even, got[0], got[1]), jnp.where(even, got[1], got[0])


def local(fields, norm_gain, w_query, w_key, w_value, w_out, mix_kernel, cotangent):
    members, rows, cols, width = fields.shape
    parts = lax.axis_size("mem")
    per = cols // parts
    cells = rows * per
    tokens = cells * members * parts
    base = cells * members
    shard = 4 * width // parts
    grid = (lax.axis_size("row"), lax.axis_size("col"))
    params = pltpu.CompilerParams(vmem_limit_bytes=40 * 1024 * 1024)
    smem = pl.BlockSpec(memory_space=pltpu.SMEM)
    vmem = pl.BlockSpec(memory_space=pltpu.VMEM)
    gather8 = jnp.asarray(gather_matrix(parts, 8, members), BF)
    headsum = jnp.asarray(np.kron(np.eye(HEADS), np.ones((width // HEADS, width // HEADS))), BF)
    gain = norm_gain.reshape(1, width)
    blocks = parts * grid[1]
    block = lax.axis_index("col") * parts + snake(lax.axis_index("mem"), parts)
    place = jnp.stack([lax.axis_index("row"), block]).astype(jnp.int32)

    with jax.named_scope("pack"):
        send = pl.pallas_call(
            pack_kernel,
            in_specs=[pl.BlockSpec(memory_space=pltpu.MemorySpace.HBM)] * 2,
            scratch_shapes=[pltpu.VMEM((2, rows, members, cols, width), BF), pltpu.SemaphoreType.DMA((2, rows))],
            out_shape=pltpu.VMEM((parts, 2 * base, width), BF),
            compiler_params=params,
        )(*[pltpu.with_memory_space_constraint(a, pltpu.MemorySpace.HBM) for a in (fields, cotangent)])
    with jax.named_scope("to_cells"):
        recv = lax.all_to_all(send, "mem", 0, 0)
    with jax.named_scope("order"):
        x, cot = pl.pallas_call(
            functools.partial(order_kernel, members),
            out_shape=(pltpu.VMEM((tokens, width), BF), pltpu.VMEM((rows, per, parts * members, width), BF)),
            compiler_params=params,
        )(near(recv), gather8)
        x, w_query, w_key, w_value, w_out = lax.optimization_barrier((x, w_query, w_key, w_value, w_out))
    with jax.named_scope("halo_rows"):
        rows_at = {r: r for r in range(grid[0])}
        below, above = swap(cot[rows - 1], cot[0], lax.axis_index("row"), "row", rows_at, False)
    with jax.named_scope("forward"):
        token = pltpu.VMEM((tokens, width), BF)
        token_f = pltpu.VMEM((tokens, width), F32)
        mat = pltpu.VMEM((cells, width, width), BF)
        kept = pl.pallas_call(
            functools.partial(forward_kernel, cells),
            out_shape=(token, token_f, token, token, mat, mat),
            scratch_shapes=[pltpu.VMEM((tokens, width), F32)],
            compiler_params=params,
        )(near(x), gain, w_query, w_key, w_value, w_out, headsum)
    above, below, *kept = lax.optimization_barrier((above, below, *kept))
    with jax.named_scope("halo_cols"):
        where = {}
        for mem in range(parts):
            inner = mem // 2 if mem % 2 == 0 else parts - 1 - mem // 2
            for c in range(grid[1]):
                where[c * parts + inner] = mem * grid[1] + c
        last, first = [
            jnp.concatenate([above[c : c + 1], cot[:, c], below[c : c + 1]], axis=0) for c in (per - 1, 0)
        ]
        right, left = swap(last, first, block, ("mem", "col"), where, True)

    half = tokens // 2
    scratch = [
        pltpu.VMEM(((rows + 2) * (per + 2), members * parts, width), F32),
        pltpu.VMEM((half, width), F32),
    ]
    halo = [near(a) for a in (cot, above, below)]
    rest = [near(a) for a in (x, *kept)] + [gain, mix_kernel, w_query, w_key, w_value, w_out, gather8, headsum]
    with jax.named_scope("backward_inner"):
        inner = pl.pallas_call(
            functools.partial(backward_kernel, tuple(range(1, per - 1)), (grid[0], blocks), False),
            in_specs=[smem] + [vmem] * 18,
            out_shape=(
                pltpu.VMEM((half, width), BF),
                pltpu.VMEM((4, width, width), F32),
                pltpu.VMEM((16, width), F32),
            ),
            scratch_shapes=scratch,
            compiler_params=params,
        )(place, *halo, *rest)
    with jax.named_scope("backward_outer"):
        back = pl.pallas_call(
            functools.partial(backward_kernel, (0, per - 1), (grid[0], blocks), True),
            in_specs=[smem] + [vmem] * 23,
            out_shape=pltpu.VMEM((parts, base + shard + 16, width), BF),
            scratch_shapes=scratch,
            compiler_params=params,
        )(place, *halo, *[near(a) for a in (left, right, *inner)], *rest)
    with jax.named_scope("to_members"):
        landed = lax.all_to_all(back, "mem", 0, 0)
    with jax.named_scope("unpack"):
        total = jnp.sum(landed[:, base:, :].astype(F32), axis=0)
        total = lax.optimization_barrier(total.astype(BF))
        grad_fields = pl.pallas_call(
            unpack_kernel,
            out_shape=jax.ShapeDtypeStruct(fields.shape, BF),
            compiler_params=params,
        )(near(landed))

    with jax.named_scope("reduce"):
        total = meet(total, "row", (1, 2, 3))
        total = meet(total, "col", (2, 4, 6))
        total = meet(total, "col", (1,))
        total, grad_fields = lax.optimization_barrier((total, grad_fields))
        piece = total[:shard]
        same_core = jnp.stack([piece] + [lax.ppermute(piece, "mem", partner("mem", k)) for k in (2, 4, 6)])
        same_core = lax.optimization_barrier(same_core)
        other_core = lax.ppermute(same_core, "mem", partner("mem", 1))

    scale_all = 1.0 / math.sqrt(tokens * grid[0] * grid[1] * parts)
    with jax.named_scope("finish"):
        square = jax.ShapeDtypeStruct((width, width), F32)
        own = lax.axis_index("mem").astype(jnp.int32).reshape(1)
        grads = pl.pallas_call(
            functools.partial(finish_kernel, scale_all),
            in_specs=[smem] + [vmem] * 3,
            out_shape=(square,) * 4 + (jax.ShapeDtypeStruct((3, 3, width), F32), jax.ShapeDtypeStruct((1, width), F32)),
            compiler_params=params,
        )(own, near(same_core), near(other_core), near(total))
    return (grad_fields, grads[5].reshape(width)) + tuple(grads[:5])


def solution(mesh):
    tile = P("mem", "row", "col", None)
    in_specs = (tile, P(), P(), P(), P(), P(), P(), tile)
    out_specs = (tile, P(), P(), P(), P(), P(), P())
    return jax.shard_map(local, mesh=mesh, in_specs=in_specs, out_specs=out_specs, check_vma=False)
```

```python
import functools
import math

import jax
import jax.numpy as jnp
import numpy as np
from jax import lax
from jax.experimental import pallas as pl
from jax.experimental.pallas import tpu as pltpu
from jax.sharding import PartitionSpec as P

HEADS = 8
EPS = 1e-06
BF = jnp.bfloat16
F32 = jnp.float32
NT = (((1,), (1,)), ((), ()))
TN = (((0,), (0,)), ((), ()))


def dot(a, b, dims=None):
    if dims is None:
        return jnp.dot(a, b, preferred_element_type=F32)
    return lax.dot_general(a, b, dims, preferred_element_type=F32)


def snake(place, parts):
    return jnp.where(place % 2 == 0, place // 2, parts - 1 - place // 2)


def split_matrix(parts, members, cols):
    size = members * cols
    per = cols // parts
    out = lax.broadcasted_iota(jnp.int32, (size, size), 0)
    src = lax.broadcasted_iota(jnp.int32, (size, size), 1)
    part, col, member = out // (per * members), out // members % per, out % members
    hit = (src // cols == member) & (src % cols == snake(part, parts) * per + col)
    return jnp.where(hit, 1.0, 0.0).astype(BF)


def gather_matrix(parts, cells, members):
    out = np.zeros((cells, parts, members, parts, cells, members), np.float32)
    for s in range(parts):
        for c in range(cells):
            for m in range(members):
                out[c, s, m, s, c, m] = 1
    return out.reshape(cells * parts * members, -1)


def pack_kernel(fields, cot, send, held, sems):
    members, rows, cols, width = fields.shape
    parts = send.shape[0]
    per = cols // parts * members
    copies = []
    for k, source in enumerate((fields, cot)):
        for r in range(rows):
            copies.append(pltpu.make_async_copy(source.at[:, r], held.at[k, r], sems.at[k, r]))
    for copy in copies:
        copy.start()
    split = split_matrix(parts, members, cols)
    for k in range(2):
        for r in range(rows):
            copies[k * rows + r].wait()
            tokens = held[k, r].reshape(members * cols, width)
            moved = dot(split, tokens).astype(BF).reshape(parts, per, width)
            start = (k * rows + r) * per
            send[:, start : start + per, :] = moved


def hold_kernel(after, *refs):
    count = len(refs) // 2
    for source, held in zip(refs[:count], refs[count:]):
        held[...] = source[...]


def order_kernel(members, recv, gather8, x_out, cot_out):
    rows, per, all_members, width = cot_out.shape
    cells = rows * per
    for g in range(cells // 8):
        x_out[g * 8 * all_members : (g + 1) * 8 * all_members, :] = regroup(recv, g * 8 * members, 8, members, gather8).astype(BF)
        block = regroup(recv, (cells + g * 8) * members, 8, members, gather8).astype(BF)
        cot_out[g * 8 // per : (g + 1) * 8 // per] = block.reshape(8 // per, per, all_members, width)


def regroup(recv, start, count, members, matrix):
    parts, _, width = recv.shape
    rows = count * members
    return dot(matrix[...], recv[:, start : start + rows, :].reshape(parts * rows, width))


def norm(x):
    inv = lax.rsqrt(jnp.mean(x * x, axis=-1, keepdims=True) + EPS)
    return inv, x * inv


def head_sums(v, headsum):
    hi = v.astype(BF)
    lo = (v - hi.astype(F32)).astype(BF)
    return dot(hi, headsum[...]) + dot(lo, headsum[...])


def expand_all(blocks, mats):
    cells, width, _ = mats.shape
    size = blocks.shape[0] // cells
    head_dim = width // HEADS
    row_head = lax.broadcasted_iota(jnp.int32, (width, width), 0) // head_dim
    col_head = lax.broadcasted_iota(jnp.int32, (width, width), 1) // head_dim
    same = row_head == col_head
    for c in range(cells):
        tiled = jnp.concatenate([blocks[c * size : (c + 1) * size]] * HEADS, axis=0)
        mats[c] = jnp.where(same, tiled, jnp.zeros_like(tiled))


def forward_kernel(
    cells,
    x_in,
    gain,
    wq,
    wk,
    wv,
    wo,
    headsum,
    q_out,
    prob_out,
    att_out,
    mixed_out,
    mat_k,
    mat_v,
    sums,
):
    tokens, width = x_in.shape
    scale = 1.0 / math.sqrt(width // HEADS)
    all_members = tokens // cells
    x = x_in[...].astype(F32)
    _, normed = norm(x)
    inputs = (normed * gain[...]).astype(BF)
    queries = dot(inputs, wq[...]).astype(BF)
    keys = dot(inputs, wk[...]).astype(BF)
    values = dot(inputs, wv[...]).astype(BF)
    q_out[...] = queries
    expand_all(keys, mat_k)
    expand_all(values, mat_v)
    for c in range(cells):
        rows = slice(c * all_members, (c + 1) * all_members)
        sums[rows, :] = dot(queries[rows], mat_k[c], NT)
    scores = sums[...] * scale
    lane = lax.broadcasted_iota(jnp.int32, (tokens, 128), 1)
    halves = []
    for h in range(width // 128):
        top = scores[:, h * 128 : (h + 1) * 128]
        step = 1
        while step < all_members:
            up = pltpu.roll(top, step, 1)
            down = pltpu.roll(top, 128 - step, 1)
            top = jnp.maximum(top, jnp.where((lane & step) != 0, up, down))
            step *= 2
        halves.append(top)
    lifted = jnp.exp(scores - jnp.concatenate(halves, axis=1))
    prob = lifted / head_sums(lifted, headsum)
    prob_out[...] = prob
    prob_b = prob.astype(BF)
    for c in range(cells):
        rows = slice(c * all_members, (c + 1) * all_members)
        att_out[rows, :] = dot(prob_b[rows], mat_v[c]).astype(BF)
    mixed_out[...] = dot(att_out[...], wo[...]).astype(BF)


def backward_kernel(picked, sizes, outer, place, cot, above, below, *refs):
    if outer:
        left, right, part_in, grads_in, extra_in = refs[:5]
        refs = refs[5:]
    x_in, q_in, prob_in, att_in, mixed_in, mat_k, mat_v, gain, mix, wq, wk, wv, wo, gather8, headsum = refs[:15]
    outs, (padded, sums) = refs[15:-2], refs[-2:]
    tile_rows, tile_cols, all_members, width = cot.shape
    head_dim = width // HEADS
    scale = 1.0 / math.sqrt(head_dim)
    pad_cols = tile_cols + 2
    spots = [(r, c) for r in range(tile_rows) for c in picked]
    cells = [r * tile_cols + c for r, c in spots]
    tokens = len(cells) * all_members
    row, block = place[0], place[1]

    def pick(ref):
        return jnp.concatenate([ref[c * all_members : (c + 1) * all_members, :] for c in cells], axis=0)

    def side(inside, x):
        x = x.astype(F32)
        return jnp.where(inside, x, jnp.zeros_like(x))

    in_left, in_right = block > 0, block < sizes[1] - 1
    in_above, in_below = row > 0, row < sizes[0] - 1
    padded[1 : 1 + tile_cols] = side(in_above, above[...])
    padded[(tile_rows + 1) * pad_cols + 1 : (tile_rows + 1) * pad_cols + 1 + tile_cols] = side(in_below, below[...])
    for r in range(tile_rows):
        padded[(r + 1) * pad_cols + 1 : (r + 1) * pad_cols + 1 + tile_cols] = cot[r].astype(F32)
    if outer:
        for r in range(tile_rows + 2):
            near_l, near_r = in_left, in_right
            if r == 0:
                near_l, near_r = in_left & in_above, in_right & in_above
            elif r == tile_rows + 1:
                near_l, near_r = in_left & in_below, in_right & in_below
            padded[r * pad_cols] = side(near_l, left[r])
            padded[r * pad_cols + 1 + tile_cols] = side(near_r, right[r])

    def shifted(i, j):
        moved = [padded[(r + 2 - i) * pad_cols + c + 2 - j] for r, c in spots]
        return jnp.concatenate(moved, axis=0)

    inv, normed = norm(pick(x_in).astype(F32))
    inputs = (normed * gain[...]).astype(BF)
    queries = pick(q_in)
    attended = pick(att_in)
    mixed = pick(mixed_in).astype(F32)
    extra = []
    conv = jnp.zeros((tokens, width), F32)
    for i in range(3):
        for j in range(3):
            moved = shifted(i, j)
            conv = conv + mix[i, j : j + 1, :] * moved
            extra.append(jnp.sum(mixed * moved, axis=0, keepdims=True))
    grad_mixed = conv.astype(BF)
    grad_att = dot(grad_mixed, wo[...], NT).astype(BF)
    for k, c in enumerate(cells):
        rows = slice(k * all_members, (k + 1) * all_members)
        sums[rows, :] = dot(grad_att[rows], mat_v[c], NT)

    prob = pick(prob_in)
    prob_b = prob.astype(BF)
    grad_prob = sums[...]
    inner = head_sums(prob * grad_prob, headsum)
    grad_score = (prob * (grad_prob - inner) * scale).astype(BF)
    lane_head = lax.broadcasted_iota(jnp.int32, (all_members, width), 1) // head_dim

    def diagonal(full):
        out = jnp.zeros((all_members, width), F32)
        for h in range(HEADS):
            out = jnp.where(lane_head == h, full[h * all_members : (h + 1) * all_members], out)
        return out

    gq_l, gk_l, gv_l = [], [], []
    for k, c in enumerate(cells):
        rows = slice(k * all_members, (k + 1) * all_members)
        gq_l.append(dot(grad_score[rows], mat_k[c]).astype(BF))
        gk_l.append(diagonal(dot(grad_score[rows], queries[rows], TN)).astype(BF))
        gv_l.append(diagonal(dot(prob_b[rows], grad_att[rows], TN)).astype(BF))
    grad_q = jnp.concatenate(gq_l, axis=0)
    grad_k = jnp.concatenate(gk_l, axis=0)
    grad_v = jnp.concatenate(gv_l, axis=0)

    grad_in = dot(grad_q, wq[...], NT) + dot(grad_k, wk[...], NT) + dot(grad_v, wv[...], NT)
    extra.append(jnp.sum(grad_in * normed, axis=0, keepdims=True))
    grad_normed = grad_in * gain[...]
    mean = jnp.mean(grad_normed * normed, axis=-1, keepdims=True)
    grad = (shifted(1, 1) + inv * (grad_normed - normed * mean)).astype(BF)
    weights = [
        dot(inputs, grad_q, TN),
        dot(inputs, grad_k, TN),
        dot(inputs, grad_v, TN),
        dot(attended, grad_mixed, TN),
    ]
    extras = jnp.concatenate(extra + [jnp.zeros((16 - len(extra), width), F32)], axis=0)
    if not outer:
        part_out, grads_out, extra_out = outs
        part_out[...] = grad
        for k in range(4):
            grads_out[k] = weights[k]
        extra_out[...] = extras
        return
    (send,) = outs
    parts = send.shape[0]
    members = all_members // parts
    base = tile_rows * tile_cols * members
    shard = 4 * width // parts
    done = {c: grad[k * all_members : (k + 1) * all_members] for k, c in enumerate(cells)}
    others = [c for c in range(tile_rows * tile_cols) if c not in done]
    for k, c in enumerate(others):
        done[c] = part_in[k * all_members : (k + 1) * all_members, :]
    for g in range(len(done) // 8):
        group = jnp.concatenate([done[c] for c in range(g * 8, (g + 1) * 8)], axis=0)
        back = dot(gather8[...], group, TN).astype(BF)
        send[:, g * 8 * members : (g + 1) * 8 * members, :] = back.reshape(parts, 8 * members, width)
    for j in range(parts):
        which, start = divmod(j * shard, width)
        total = weights[which][start : start + shard] + grads_in[which, start : start + shard, :]
        send[j, base : base + shard, :] = total.astype(BF)
        send[j, base + shard : base + shard + 16, :] = (extras + extra_in[...]).astype(BF)


def unpack_kernel(recv, out):
    members, rows, cols, width = out.shape
    parts = recv.shape[0]
    per = cols // parts * members
    split = split_matrix(parts, members, cols)
    for r in range(rows):
        tokens = recv[:, r * per : (r + 1) * per, :].reshape(parts * per, width)
        out[:, r] = dot(split, tokens, TN).astype(BF).reshape(members, cols, width)


def finish_kernel(scale, place, pair, pair_far, other, other_far, total, g_q, g_k, g_v, g_o, g_mix, g_gain):
    _, shard, width = pair.shape
    per = width // shard
    outs = (g_q, g_k, g_v, g_o)
    for p in range(8):
        code = lax.bitwise_xor(place[0], p)
        step = lax.shift_right_logical(code, 1)
        distant = step >= 2
        spot = jnp.where(distant, 3 - step, step)
        same = jnp.where(distant, pair_far[spot], pair[spot])
        cross = jnp.where(distant, other_far[spot], other[spot])
        got = jnp.where(code == 2 * step, same, cross).astype(F32)
        outs[p // per][p % per * shard : (p % per + 1) * shard, :] = got * scale
    rest = total[shard:, :].astype(F32) * scale
    for i in range(3):
        g_mix[i] = rest[3 * i : 3 * i + 3]
    g_gain[...] = rest[9:10]


def partner(axis, code):
    return [(i, i ^ code) for i in range(lax.axis_size(axis))]


def meet(values, axis, codes):
    got = [values] + [lax.ppermute(values, axis, partner(axis, k)) for k in codes]
    got = [x.astype(F32) for x in got]
    while len(got) > 1:
        got = [a + b for a, b in zip(got[::2], got[1::2])]
    return lax.optimization_barrier(got[0].astype(BF))


def far(x):
    return pltpu.with_memory_space_constraint(x, pltpu.MemorySpace.HBM)


def near(x):
    return pltpu.with_memory_space_constraint(x, pltpu.VMEM)


def swap(last, first, spot, axis, where, wrap):
    size = len(where)
    got = []
    for odd in (0, 1):
        pairs = []
        for a in range(odd, size if wrap else size - 1, 2):
            b = (a + 1) % size
            pairs += [(where[a], where[b]), (where[b], where[a])]
        got.append(lax.ppermute(jnp.where(spot % 2 == odd, last, first), axis, pairs))
    even = spot % 2 == 0
    return jnp.where(even, got[0], got[1]), jnp.where(even, got[1], got[0])


def local(fields, norm_gain, w_query, w_key, w_value, w_out, mix_kernel, cotangent):
    members, rows, cols, width = fields.shape
    parts = lax.axis_size("mem")
    per = cols // parts
    cells = rows * per
    tokens = cells * members * parts
    base = cells * members
    shard = 4 * width // parts
    grid = (lax.axis_size("row"), lax.axis_size("col"))
    params = pltpu.CompilerParams(vmem_limit_bytes=40 * 1024 * 1024)
    smem = pl.BlockSpec(memory_space=pltpu.SMEM)
    vmem = pl.BlockSpec(memory_space=pltpu.VMEM)
    gather8 = jnp.asarray(gather_matrix(parts, 8, members), BF)
    headsum = jnp.asarray(np.kron(np.eye(HEADS), np.ones((width // HEADS, width // HEADS))), BF)
    gain = norm_gain.reshape(1, width)
    blocks = parts * grid[1]
    block = lax.axis_index("col") * parts + snake(lax.axis_index("mem"), parts)
    place = jnp.stack([lax.axis_index("row"), block]).astype(jnp.int32)

    with jax.named_scope("pack"):
        send = pl.pallas_call(
            pack_kernel,
            in_specs=[pl.BlockSpec(memory_space=pltpu.MemorySpace.HBM)] * 2,
            scratch_shapes=[pltpu.VMEM((2, rows, members, cols, width), BF), pltpu.SemaphoreType.DMA((2, rows))],
            out_shape=pltpu.VMEM((parts, 2 * base, width), BF),
            compiler_params=params,
        )(far(fields), far(cotangent))
    with jax.named_scope("hold"):
        kinds = (w_query, w_key, w_value, w_out, gather8, headsum)
        held = pl.pallas_call(
            hold_kernel,
            in_specs=[pl.BlockSpec(memory_space=pl.ANY)] + [vmem] * len(kinds),
            out_shape=tuple(pltpu.VMEM(a.shape, a.dtype) for a in kinds),
            compiler_params=params,
        )(near(send), *[far(a) for a in kinds])
        w_query, w_key, w_value, w_out, gather8, headsum = [near(a) for a in held]
    with jax.named_scope("to_cells"):
        recv = lax.all_to_all(send, "mem", 0, 0)
    with jax.named_scope("order"):
        x, cot = pl.pallas_call(
            functools.partial(order_kernel, members),
            out_shape=(pltpu.VMEM((tokens, width), BF), pltpu.VMEM((rows, per, parts * members, width), BF)),
            compiler_params=params,
        )(near(recv), gather8)
    with jax.named_scope("halo_rows"):
        rows_at = {r: r for r in range(grid[0])}
        below, above = swap(cot[rows - 1], cot[0], lax.axis_index("row"), "row", rows_at, False)
    with jax.named_scope("forward"):
        token = pltpu.VMEM((tokens, width), BF)
        token_f = pltpu.VMEM((tokens, width), F32)
        mat = pltpu.VMEM((cells, width, width), BF)
        kept = pl.pallas_call(
            functools.partial(forward_kernel, cells),
            out_shape=(token, token_f, token, token, mat, mat),
            scratch_shapes=[pltpu.VMEM((tokens, width), F32)],
            compiler_params=params,
        )(near(x), gain, w_query, w_key, w_value, w_out, headsum)
    above, below, *kept = lax.optimization_barrier((above, below, *kept))
    with jax.named_scope("halo_cols"):
        where = {}
        for mem in range(parts):
            inner = mem // 2 if mem % 2 == 0 else parts - 1 - mem // 2
            for c in range(grid[1]):
                where[c * parts + inner] = mem * grid[1] + c
        last, first = [
            jnp.concatenate([above[c : c + 1], cot[:, c], below[c : c + 1]], axis=0) for c in (per - 1, 0)
        ]
        right, left = swap(last, first, block, ("mem", "col"), where, True)

    half = tokens // 2
    scratch = [
        pltpu.VMEM(((rows + 2) * (per + 2), members * parts, width), F32),
        pltpu.VMEM((half, width), F32),
    ]
    halo = [near(a) for a in (cot, above, below)]
    rest = [near(a) for a in (x, *kept)] + [gain, mix_kernel, w_query, w_key, w_value, w_out, gather8, headsum]
    with jax.named_scope("backward_inner"):
        inner = pl.pallas_call(
            functools.partial(backward_kernel, tuple(range(1, per - 1)), (grid[0], blocks), False),
            in_specs=[smem] + [vmem] * 18,
            out_shape=(
                pltpu.VMEM((half, width), BF),
                pltpu.VMEM((4, width, width), F32),
                pltpu.VMEM((16, width), F32),
            ),
            scratch_shapes=scratch,
            compiler_params=params,
        )(place, *halo, *rest)
    with jax.named_scope("backward_outer"):
        back = pl.pallas_call(
            functools.partial(backward_kernel, (0, per - 1), (grid[0], blocks), True),
            in_specs=[smem] + [vmem] * 23,
            out_shape=pltpu.VMEM((parts, base + shard + 16, width), BF),
            scratch_shapes=scratch,
            compiler_params=params,
        )(place, *halo, *[near(a) for a in (left, right, *inner)], *rest)
    with jax.named_scope("to_members"):
        landed = lax.all_to_all(back, "mem", 0, 0)
    with jax.named_scope("unpack"):
        total = jnp.sum(landed[:, base:, :].astype(F32), axis=0)
        total = lax.optimization_barrier(total.astype(BF))
        grad_fields = pl.pallas_call(
            unpack_kernel,
            out_shape=jax.ShapeDtypeStruct(fields.shape, BF),
            compiler_params=params,
        )(near(landed))

    with jax.named_scope("reduce"):
        total = meet(total, "row", (1, 2, 3))
        total = meet(total, "col", (2, 4, 6))
        total = meet(total, "col", (1,))
        total, grad_fields = lax.optimization_barrier((total, grad_fields))
        piece = total[:shard]
        next_x = lax.ppermute(piece, "mem", partner("mem", 2))
        pair = lax.optimization_barrier(jnp.stack([piece, next_x]))
        pair_far = lax.ppermute(pair, "mem", partner("mem", 6))
        other = lax.ppermute(pair, "mem", partner("mem", 1))
        other_far = lax.ppermute(pair_far, "mem", partner("mem", 1))

    scale_all = 1.0 / math.sqrt(tokens * grid[0] * grid[1] * parts)
    with jax.named_scope("finish"):
        square = jax.ShapeDtypeStruct((width, width), F32)
        own = lax.axis_index("mem").astype(jnp.int32).reshape(1)
        grads = pl.pallas_call(
            functools.partial(finish_kernel, scale_all),
            in_specs=[smem] + [vmem] * 5,
            out_shape=(square,) * 4 + (jax.ShapeDtypeStruct((3, 3, width), F32), jax.ShapeDtypeStruct((1, width), F32)),
            compiler_params=params,
        )(own, *[near(a) for a in (pair, pair_far, other, other_far, total)])
    return (grad_fields, grads[5].reshape(width)) + tuple(grads[:5])


def solution(mesh):
    tile = P("mem", "row", "col", None)
    in_specs = (tile, P(), P(), P(), P(), P(), P(), tile)
    out_specs = (tile, P(), P(), P(), P(), P(), P())
    return jax.shard_map(local, mesh=mesh, in_specs=in_specs, out_specs=out_specs, check_vma=False)
```

```python
import functools
import math

import jax
import jax.numpy as jnp
import numpy as np
from jax import lax
from jax.experimental import pallas as pl
from jax.experimental.pallas import tpu as pltpu
from jax.sharding import PartitionSpec as P

HEADS = 8
EPS = 1e-06
BF = jnp.bfloat16
F32 = jnp.float32
NT = (((1,), (1,)), ((), ()))
TN = (((0,), (0,)), ((), ()))


def dot(a, b, dims=None):
    if dims is None:
        return jnp.dot(a, b, preferred_element_type=F32)
    return lax.dot_general(a, b, dims, preferred_element_type=F32)


def snake(place, parts):
    return jnp.where(place % 2 == 0, place // 2, parts - 1 - place // 2)


def split_matrix(parts, members, cols):
    size = members * cols
    per = cols // parts
    out = lax.broadcasted_iota(jnp.int32, (size, size), 0)
    src = lax.broadcasted_iota(jnp.int32, (size, size), 1)
    part, col, member = out // (per * members), out // members % per, out % members
    hit = (src // cols == member) & (src % cols == snake(part, parts) * per + col)
    return jnp.where(hit, 1.0, 0.0).astype(BF)


def gather_matrix(parts, cells, members):
    out = np.zeros((cells, parts, members, parts, cells, members), np.float32)
    for s in range(parts):
        for c in range(cells):
            for m in range(members):
                out[c, s, m, s, c, m] = 1
    return out.reshape(cells * parts * members, -1)


def pack_kernel(fields, cot, send, held, sems):
    members, rows, cols, width = fields.shape
    parts = send.shape[0]
    per = cols // parts * members
    copies = []
    for k, source in enumerate((fields, cot)):
        for r in range(rows):
            copies.append(pltpu.make_async_copy(source.at[:, r], held.at[k, r], sems.at[k, r]))
    for copy in copies:
        copy.start()
    split = split_matrix(parts, members, cols)
    for k in range(2):
        for r in range(rows):
            copies[k * rows + r].wait()
            tokens = held[k, r].reshape(members * cols, width)
            moved = dot(split, tokens).astype(BF).reshape(parts, per, width)
            start = (k * rows + r) * per
            send[:, start : start + per, :] = moved


def order_kernel(members, recv, gather8, x_out, cot_out):
    rows, per, all_members, width = cot_out.shape
    cells = rows * per
    for g in range(cells // 8):
        x_out[g * 8 * all_members : (g + 1) * 8 * all_members, :] = regroup(recv, g * 8 * members, 8, members, gather8).astype(BF)
        block = regroup(recv, (cells + g * 8) * members, 8, members, gather8).astype(BF)
        cot_out[g * 8 // per : (g + 1) * 8 // per] = block.reshape(8 // per, per, all_members, width)


def regroup(recv, start, count, members, matrix):
    parts, _, width = recv.shape
    rows = count * members
    return dot(matrix[...], recv[:, start : start + rows, :].reshape(parts * rows, width))


def norm(x):
    inv = lax.rsqrt(jnp.mean(x * x, axis=-1, keepdims=True) + EPS)
    return inv, x * inv


def head_sums(v, headsum):
    hi = v.astype(BF)
    lo = (v - hi.astype(F32)).astype(BF)
    return dot(hi, headsum[...]) + dot(lo, headsum[...])


def expand_all(blocks, mats):
    cells, width, _ = mats.shape
    size = blocks.shape[0] // cells
    head_dim = width // HEADS
    row_head = lax.broadcasted_iota(jnp.int32, (width, width), 0) // head_dim
    col_head = lax.broadcasted_iota(jnp.int32, (width, width), 1) // head_dim
    same = row_head == col_head
    for c in range(cells):
        tiled = jnp.concatenate([blocks[c * size : (c + 1) * size]] * HEADS, axis=0)
        mats[c] = jnp.where(same, tiled, jnp.zeros_like(tiled))


def forward_kernel(
    cells,
    x_in,
    gain,
    wq,
    wk,
    wv,
    wo,
    headsum,
    q_out,
    prob_out,
    att_out,
    mixed_out,
    mat_k,
    mat_v,
    sums,
):
    tokens, width = x_in.shape
    scale = 1.0 / math.sqrt(width // HEADS)
    all_members = tokens // cells
    x = x_in[...].astype(F32)
    _, normed = norm(x)
    inputs = (normed * gain[...]).astype(BF)
    queries = dot(inputs, wq[...]).astype(BF)
    keys = dot(inputs, wk[...]).astype(BF)
    values = dot(inputs, wv[...]).astype(BF)
    q_out[...] = queries
    expand_all(keys, mat_k)
    expand_all(values, mat_v)
    for c in range(cells):
        rows = slice(c * all_members, (c + 1) * all_members)
        sums[rows, :] = dot(queries[rows], mat_k[c], NT)
    scores = sums[...] * scale
    lane = lax.broadcasted_iota(jnp.int32, (tokens, 128), 1)
    halves = []
    for h in range(width // 128):
        top = scores[:, h * 128 : (h + 1) * 128]
        step = 1
        while step < all_members:
            up = pltpu.roll(top, step, 1)
            down = pltpu.roll(top, 128 - step, 1)
            top = jnp.maximum(top, jnp.where((lane & step) != 0, up, down))
            step *= 2
        halves.append(top)
    lifted = jnp.exp(scores - jnp.concatenate(halves, axis=1))
    prob = lifted / head_sums(lifted, headsum)
    prob_out[...] = prob
    prob_b = prob.astype(BF)
    for c in range(cells):
        rows = slice(c * all_members, (c + 1) * all_members)
        att_out[rows, :] = dot(prob_b[rows], mat_v[c]).astype(BF)
    mixed_out[...] = dot(att_out[...], wo[...]).astype(BF)


def backward_kernel(picked, sizes, outer, place, cot, above, below, *refs):
    if outer:
        left, right, part_in, grads_in, extra_in = refs[:5]
        refs = refs[5:]
    x_in, q_in, prob_in, att_in, mixed_in, mat_k, mat_v, gain, mix, wq, wk, wv, wo, gather8, headsum = refs[:15]
    outs, (padded, sums) = refs[15:-2], refs[-2:]
    tile_rows, tile_cols, all_members, width = cot.shape
    head_dim = width // HEADS
    scale = 1.0 / math.sqrt(head_dim)
    pad_cols = tile_cols + 2
    spots = [(r, c) for r in range(tile_rows) for c in picked]
    cells = [r * tile_cols + c for r, c in spots]
    tokens = len(cells) * all_members
    row, block = place[0], place[1]

    def pick(ref):
        return jnp.concatenate([ref[c * all_members : (c + 1) * all_members, :] for c in cells], axis=0)

    def side(inside, x):
        x = x.astype(F32)
        return jnp.where(inside, x, jnp.zeros_like(x))

    in_left, in_right = block > 0, block < sizes[1] - 1
    in_above, in_below = row > 0, row < sizes[0] - 1
    padded[1 : 1 + tile_cols] = side(in_above, above[...])
    padded[(tile_rows + 1) * pad_cols + 1 : (tile_rows + 1) * pad_cols + 1 + tile_cols] = side(in_below, below[...])
    for r in range(tile_rows):
        padded[(r + 1) * pad_cols + 1 : (r + 1) * pad_cols + 1 + tile_cols] = cot[r].astype(F32)
    if outer:
        for r in range(tile_rows + 2):
            near_l, near_r = in_left, in_right
            if r == 0:
                near_l, near_r = in_left & in_above, in_right & in_above
            elif r == tile_rows + 1:
                near_l, near_r = in_left & in_below, in_right & in_below
            padded[r * pad_cols] = side(near_l, left[r])
            padded[r * pad_cols + 1 + tile_cols] = side(near_r, right[r])

    def shifted(i, j):
        moved = [padded[(r + 2 - i) * pad_cols + c + 2 - j] for r, c in spots]
        return jnp.concatenate(moved, axis=0)

    inv, normed = norm(pick(x_in).astype(F32))
    inputs = (normed * gain[...]).astype(BF)
    queries = pick(q_in)
    attended = pick(att_in)
    mixed = pick(mixed_in).astype(F32)
    extra = []
    conv = jnp.zeros((tokens, width), F32)
    for i in range(3):
        for j in range(3):
            moved = shifted(i, j)
            conv = conv + mix[i, j : j + 1, :] * moved
            extra.append(jnp.sum(mixed * moved, axis=0, keepdims=True))
    grad_mixed = conv.astype(BF)
    grad_att = dot(grad_mixed, wo[...], NT).astype(BF)
    for k, c in enumerate(cells):
        rows = slice(k * all_members, (k + 1) * all_members)
        sums[rows, :] = dot(grad_att[rows], mat_v[c], NT)

    prob = pick(prob_in)
    prob_b = prob.astype(BF)
    grad_prob = sums[...]
    inner = head_sums(prob * grad_prob, headsum)
    grad_score = (prob * (grad_prob - inner) * scale).astype(BF)
    lane_head = lax.broadcasted_iota(jnp.int32, (all_members, width), 1) // head_dim

    def diagonal(full):
        out = jnp.zeros((all_members, width), F32)
        for h in range(HEADS):
            out = jnp.where(lane_head == h, full[h * all_members : (h + 1) * all_members], out)
        return out

    gq_l, gk_l, gv_l = [], [], []
    for k, c in enumerate(cells):
        rows = slice(k * all_members, (k + 1) * all_members)
        gq_l.append(dot(grad_score[rows], mat_k[c]).astype(BF))
        gk_l.append(diagonal(dot(grad_score[rows], queries[rows], TN)).astype(BF))
        gv_l.append(diagonal(dot(prob_b[rows], grad_att[rows], TN)).astype(BF))
    grad_q = jnp.concatenate(gq_l, axis=0)
    grad_k = jnp.concatenate(gk_l, axis=0)
    grad_v = jnp.concatenate(gv_l, axis=0)

    grad_in = dot(grad_q, wq[...], NT) + dot(grad_k, wk[...], NT) + dot(grad_v, wv[...], NT)
    extra.append(jnp.sum(grad_in * normed, axis=0, keepdims=True))
    grad_normed = grad_in * gain[...]
    mean = jnp.mean(grad_normed * normed, axis=-1, keepdims=True)
    grad = (shifted(1, 1) + inv * (grad_normed - normed * mean)).astype(BF)
    weights = [
        dot(inputs, grad_q, TN),
        dot(inputs, grad_k, TN),
        dot(inputs, grad_v, TN),
        dot(attended, grad_mixed, TN),
    ]
    extras = jnp.concatenate(extra + [jnp.zeros((16 - len(extra), width), F32)], axis=0)
    if not outer:
        part_out, grads_out, extra_out = outs
        part_out[...] = grad
        for k in range(4):
            grads_out[k] = weights[k]
        extra_out[...] = extras
        return
    (send,) = outs
    parts = send.shape[0]
    members = all_members // parts
    base = tile_rows * tile_cols * members
    shard = 4 * width // parts
    done = {c: grad[k * all_members : (k + 1) * all_members] for k, c in enumerate(cells)}
    others = [c for c in range(tile_rows * tile_cols) if c not in done]
    for k, c in enumerate(others):
        done[c] = part_in[k * all_members : (k + 1) * all_members, :]
    for g in range(len(done) // 8):
        group = jnp.concatenate([done[c] for c in range(g * 8, (g + 1) * 8)], axis=0)
        back = dot(gather8[...], group, TN).astype(BF)
        send[:, g * 8 * members : (g + 1) * 8 * members, :] = back.reshape(parts, 8 * members, width)
    for j in range(parts):
        which, start = divmod(j * shard, width)
        total = weights[which][start : start + shard] + grads_in[which, start : start + shard, :]
        send[j, base : base + shard, :] = total.astype(BF)
        send[j, base + shard : base + shard + 16, :] = (extras + extra_in[...]).astype(BF)


def unpack_kernel(recv, out):
    members, rows, cols, width = out.shape
    parts = recv.shape[0]
    per = cols // parts * members
    split = split_matrix(parts, members, cols)
    for r in range(rows):
        tokens = recv[:, r * per : (r + 1) * per, :].reshape(parts * per, width)
        out[:, r] = dot(split, tokens, TN).astype(BF).reshape(members, cols, width)


def finish_kernel(scale, place, same_core, other_core, total, g_q, g_k, g_v, g_o, g_mix, g_gain):
    count, shard, width = same_core.shape
    per = width // shard
    outs = (g_q, g_k, g_v, g_o)
    for p in range(2 * count):
        code = lax.bitwise_xor(place[0], p)
        spot = lax.shift_right_logical(code, 1)
        got = jnp.where(code == 2 * spot, same_core[spot], other_core[spot]).astype(F32)
        outs[p // per][p % per * shard : (p % per + 1) * shard, :] = got * scale
    rest = total[shard:, :].astype(F32) * scale
    for i in range(3):
        g_mix[i] = rest[3 * i : 3 * i + 3]
    g_gain[...] = rest[9:10]


def partner(axis, code):
    return [(i, i ^ code) for i in range(lax.axis_size(axis))]


def meet(values, axis, codes):
    got = [values] + [lax.ppermute(values, axis, partner(axis, k)) for k in codes]
    got = [x.astype(F32) for x in got]
    while len(got) > 1:
        got = [a + b for a, b in zip(got[::2], got[1::2])]
    return lax.optimization_barrier(got[0].astype(BF))


def near(x):
    return pltpu.with_memory_space_constraint(x, pltpu.VMEM)


def swap(last, first, spot, axis, where, wrap):
    size = len(where)
    got = {}
    for odd in (1, 0):
        pairs = []
        for a in range(odd, size if wrap else size - 1, 2):
            b = (a + 1) % size
            pairs += [(where[a], where[b]), (where[b], where[a])]
        got[odd] = lax.ppermute(jnp.where(spot % 2 == odd, last, first), axis, pairs)
    odd = spot % 2 == 1
    before = jnp.where(odd, got[0], got[1])
    after = jnp.where(odd, got[1], got[0])
    return after, before


def local(fields, norm_gain, w_query, w_key, w_value, w_out, mix_kernel, cotangent):
    members, rows, cols, width = fields.shape
    parts = lax.axis_size("mem")
    per = cols // parts
    cells = rows * per
    tokens = cells * members * parts
    base = cells * members
    shard = 4 * width // parts
    grid = (lax.axis_size("row"), lax.axis_size("col"))
    params = pltpu.CompilerParams(vmem_limit_bytes=40 * 1024 * 1024)
    smem = pl.BlockSpec(memory_space=pltpu.SMEM)
    vmem = pl.BlockSpec(memory_space=pltpu.VMEM)
    gather8 = jnp.asarray(gather_matrix(parts, 8, members), BF)
    headsum = jnp.asarray(np.kron(np.eye(HEADS), np.ones((width // HEADS, width // HEADS))), BF)
    gain = norm_gain.reshape(1, width)
    blocks = parts * grid[1]
    block = lax.axis_index("col") * parts + snake(lax.axis_index("mem"), parts)
    place = jnp.stack([lax.axis_index("row"), block]).astype(jnp.int32)

    with jax.named_scope("pack"):
        send = pl.pallas_call(
            pack_kernel,
            in_specs=[pl.BlockSpec(memory_space=pltpu.MemorySpace.HBM)] * 2,
            scratch_shapes=[pltpu.VMEM((2, rows, members, cols, width), BF), pltpu.SemaphoreType.DMA((2, rows))],
            out_shape=pltpu.VMEM((parts, 2 * base, width), BF),
            compiler_params=params,
        )(*[pltpu.with_memory_space_constraint(a, pltpu.MemorySpace.HBM) for a in (fields, cotangent)])
    with jax.named_scope("to_cells"):
        recv = lax.all_to_all(send, "mem", 0, 0)
    with jax.named_scope("order"):
        x, cot = pl.pallas_call(
            functools.partial(order_kernel, members),
            out_shape=(pltpu.VMEM((tokens, width), BF), pltpu.VMEM((rows, per, parts * members, width), BF)),
            compiler_params=params,
        )(near(recv), gather8)
        x, w_query, w_key, w_value, w_out = lax.optimization_barrier((x, w_query, w_key, w_value, w_out))
    with jax.named_scope("halo_rows"):
        rows_at = {r: r for r in range(grid[0])}
        below, above = swap(cot[rows - 1], cot[0], lax.axis_index("row"), "row", rows_at, False)
    with jax.named_scope("forward"):
        token = pltpu.VMEM((tokens, width), BF)
        token_f = pltpu.VMEM((tokens, width), F32)
        mat = pltpu.VMEM((cells, width, width), BF)
        kept = pl.pallas_call(
            functools.partial(forward_kernel, cells),
            out_shape=(token, token_f, token, token, mat, mat),
            scratch_shapes=[pltpu.VMEM((tokens, width), F32)],
            compiler_params=params,
        )(near(x), gain, w_query, w_key, w_value, w_out, headsum)
    above, below, *kept = lax.optimization_barrier((above, below, *kept))
    with jax.named_scope("halo_cols"):
        where = {}
        for mem in range(parts):
            inner = mem // 2 if mem % 2 == 0 else parts - 1 - mem // 2
            for c in range(grid[1]):
                where[c * parts + inner] = mem * grid[1] + c
        first, last = [
            jnp.concatenate([above[c : c + 1], cot[:, c], below[c : c + 1]], axis=0) for c in (0, per - 1)
        ]
        right, left = swap(last, first, block, ("mem", "col"), where, True)

    half = tokens // 2
    scratch = [
        pltpu.VMEM(((rows + 2) * (per + 2), members * parts, width), F32),
        pltpu.VMEM((half, width), F32),
    ]
    halo = [near(a) for a in (cot, above, below)]
    rest = [near(a) for a in (x, *kept)] + [gain, mix_kernel, w_query, w_key, w_value, w_out, gather8, headsum]
    with jax.named_scope("backward_inner"):
        inner = pl.pallas_call(
            functools.partial(backward_kernel, tuple(range(1, per - 1)), (grid[0], blocks), False),
            in_specs=[smem] + [vmem] * 18,
            out_shape=(
                pltpu.VMEM((half, width), BF),
                pltpu.VMEM((4, width, width), F32),
                pltpu.VMEM((16, width), F32),
            ),
            scratch_shapes=scratch,
            compiler_params=params,
        )(place, *halo, *rest)
    with jax.named_scope("backward_outer"):
        back = pl.pallas_call(
            functools.partial(backward_kernel, (0, per - 1), (grid[0], blocks), True),
            in_specs=[smem] + [vmem] * 23,
            out_shape=pltpu.VMEM((parts, base + shard + 16, width), BF),
            scratch_shapes=scratch,
            compiler_params=params,
        )(place, *halo, *[near(a) for a in (left, right, *inner)], *rest)
    with jax.named_scope("to_members"):
        landed = lax.all_to_all(back, "mem", 0, 0)
    with jax.named_scope("unpack"):
        total = jnp.sum(landed[:, base:, :].astype(F32), axis=0)
        total = lax.optimization_barrier(total.astype(BF))
        grad_fields = pl.pallas_call(
            unpack_kernel,
            out_shape=jax.ShapeDtypeStruct(fields.shape, BF),
            compiler_params=params,
        )(near(landed))

    with jax.named_scope("reduce"):
        total = meet(total, "row", (1, 2, 3))
        total = meet(total, "col", (2, 6, 4))
        total = meet(total, "col", (1,))
        total, grad_fields = lax.optimization_barrier((total, grad_fields))
        piece = total[:shard]
        same_core = jnp.stack([piece] + [lax.ppermute(piece, "mem", partner("mem", k)) for k in (2, 4, 6)])
        same_core = lax.optimization_barrier(same_core)
        other_core = lax.ppermute(same_core, "mem", partner("mem", 1))

    scale_all = 1.0 / math.sqrt(tokens * grid[0] * grid[1] * parts)
    with jax.named_scope("finish"):
        square = jax.ShapeDtypeStruct((width, width), F32)
        own = lax.axis_index("mem").astype(jnp.int32).reshape(1)
        grads = pl.pallas_call(
            functools.partial(finish_kernel, scale_all),
            in_specs=[smem] + [vmem] * 3,
            out_shape=(square,) * 4 + (jax.ShapeDtypeStruct((3, 3, width), F32), jax.ShapeDtypeStruct((1, width), F32)),
            compiler_params=params,
        )(own, near(same_core), near(other_core), near(total))
    return (grad_fields, grads[5].reshape(width)) + tuple(grads[:5])


def solution(mesh):
    tile = P("mem", "row", "col", None)
    in_specs = (tile, P(), P(), P(), P(), P(), P(), tile)
    out_specs = (tile, P(), P(), P(), P(), P(), P())
    return jax.shard_map(local, mesh=mesh, in_specs=in_specs, out_specs=out_specs, check_vma=False)
```

```python
import functools
import math

import jax
import jax.numpy as jnp
import numpy as np
from jax import lax
from jax.experimental import pallas as pl
from jax.experimental.pallas import tpu as pltpu
from jax.sharding import PartitionSpec as P

HEADS = 8
EPS = 1e-06
BF = jnp.bfloat16
F32 = jnp.float32
NT = (((1,), (1,)), ((), ()))
TN = (((0,), (0,)), ((), ()))


def dot(a, b, dims=None):
    if dims is None:
        return jnp.dot(a, b, preferred_element_type=F32)
    return lax.dot_general(a, b, dims, preferred_element_type=F32)


def snake(place, parts):
    return jnp.where(place % 2 == 0, place // 2, parts - 1 - place // 2)


def split_matrix(parts, members, cols):
    size = members * cols
    per = cols // parts
    out = lax.broadcasted_iota(jnp.int32, (size, size), 0)
    src = lax.broadcasted_iota(jnp.int32, (size, size), 1)
    part, col, member = out // (per * members), out // members % per, out % members
    hit = (src // cols == member) & (src % cols == snake(part, parts) * per + col)
    return jnp.where(hit, 1.0, 0.0).astype(BF)


def gather_matrix(parts, cells, members):
    out = np.zeros((cells, parts, members, parts, cells, members), np.float32)
    for s in range(parts):
        for c in range(cells):
            for m in range(members):
                out[c, s, m, s, c, m] = 1
    return out.reshape(cells * parts * members, -1)


def pack_kernel(fields, cot, send):
    members, rows, cols, width = fields.shape
    parts = send.shape[0]
    per = cols // parts * members
    split = split_matrix(parts, members, cols)
    for k, source in enumerate((fields, cot)):
        for r in range(rows):
            tokens = source[:, r].reshape(members * cols, width)
            moved = dot(split, tokens).astype(BF).reshape(parts, per, width)
            start = (k * rows + r) * per
            send[:, start : start + per, :] = moved


def order_kernel(members, recv, gather8, x_out, cot_out):
    rows, per, all_members, width = cot_out.shape
    cells = rows * per
    for g in range(cells // 8):
        x_out[g * 8 * all_members : (g + 1) * 8 * all_members, :] = regroup(recv, g * 8 * members, 8, members, gather8).astype(BF)
        block = regroup(recv, (cells + g * 8) * members, 8, members, gather8).astype(BF)
        cot_out[g * 8 // per : (g + 1) * 8 // per] = block.reshape(8 // per, per, all_members, width)


def regroup(recv, start, count, members, matrix):
    parts, _, width = recv.shape
    rows = count * members
    return dot(matrix[...], recv[:, start : start + rows, :].reshape(parts * rows, width))


def norm(x):
    inv = lax.rsqrt(jnp.mean(x * x, axis=-1, keepdims=True) + EPS)
    return inv, x * inv


def head_sums(v, headsum):
    hi = v.astype(BF)
    lo = (v - hi.astype(F32)).astype(BF)
    return dot(hi, headsum[...]) + dot(lo, headsum[...])


def expand_all(blocks, mats):
    cells, width, _ = mats.shape
    size = blocks.shape[0] // cells
    head_dim = width // HEADS
    row_head = lax.broadcasted_iota(jnp.int32, (width, width), 0) // head_dim
    col_head = lax.broadcasted_iota(jnp.int32, (width, width), 1) // head_dim
    same = row_head == col_head
    for c in range(cells):
        tiled = jnp.concatenate([blocks[c * size : (c + 1) * size]] * HEADS, axis=0)
        mats[c] = jnp.where(same, tiled, jnp.zeros_like(tiled))


def forward_kernel(
    cells,
    x_in,
    gain,
    wq,
    wk,
    wv,
    wo,
    headsum,
    q_out,
    prob_out,
    att_out,
    mixed_out,
    mat_k,
    mat_v,
    sums,
):
    tokens, width = x_in.shape
    scale = 1.0 / math.sqrt(width // HEADS)
    all_members = tokens // cells
    x = x_in[...].astype(F32)
    _, normed = norm(x)
    inputs = (normed * gain[...]).astype(BF)
    queries = dot(inputs, wq[...]).astype(BF)
    keys = dot(inputs, wk[...]).astype(BF)
    values = dot(inputs, wv[...]).astype(BF)
    q_out[...] = queries
    expand_all(keys, mat_k)
    expand_all(values, mat_v)
    for c in range(cells):
        rows = slice(c * all_members, (c + 1) * all_members)
        sums[rows, :] = dot(queries[rows], mat_k[c], NT)
    scores = sums[...] * scale
    lane = lax.broadcasted_iota(jnp.int32, (tokens, 128), 1)
    halves = []
    for h in range(width // 128):
        top = scores[:, h * 128 : (h + 1) * 128]
        step = 1
        while step < all_members:
            up = pltpu.roll(top, step, 1)
            down = pltpu.roll(top, 128 - step, 1)
            top = jnp.maximum(top, jnp.where((lane & step) != 0, up, down))
            step *= 2
        halves.append(top)
    lifted = jnp.exp(scores - jnp.concatenate(halves, axis=1))
    prob = lifted / head_sums(lifted, headsum)
    prob_out[...] = prob
    prob_b = prob.astype(BF)
    for c in range(cells):
        rows = slice(c * all_members, (c + 1) * all_members)
        att_out[rows, :] = dot(prob_b[rows], mat_v[c]).astype(BF)
    mixed_out[...] = dot(att_out[...], wo[...]).astype(BF)


def backward_kernel(
    sizes,
    place,
    cot,
    left,
    right,
    above,
    below,
    x_in,
    q_in,
    prob_in,
    att_in,
    mixed_in,
    mat_k,
    mat_v,
    gain,
    mix,
    wq,
    wk,
    wv,
    wo,
    gather8,
    headsum,
    send,
    padded,
    sums,
):
    parts = send.shape[0]
    tile_rows, tile_cols, all_members, width = cot.shape
    members = all_members // parts
    head_dim = width // HEADS
    scale = 1.0 / math.sqrt(head_dim)
    cells = tile_rows * tile_cols
    tokens = cells * all_members
    pad_cols = tile_cols + 2
    base = cells * members
    row, block = place[0], place[1]

    def side(inside, x):
        x = x.astype(F32)
        return jnp.where(inside, x, jnp.zeros_like(x))

    in_left, in_right = block > 0, block < sizes[1] - 1
    edges = {0: (above, row > 0), tile_rows + 1: (below, row < sizes[0] - 1)}
    for r in range(tile_rows + 2):
        start = r * pad_cols
        if r in edges:
            source, inside = edges[r]
            padded[start] = side(inside & in_left, source[0])
            padded[start + 1 : start + 1 + tile_cols] = side(inside, source[1 : 1 + tile_cols])
            padded[start + 1 + tile_cols] = side(inside & in_right, source[1 + tile_cols])
        else:
            padded[start] = side(in_left, left[r - 1])
            padded[start + 1 : start + 1 + tile_cols] = cot[r - 1].astype(F32)
            padded[start + 1 + tile_cols] = side(in_right, right[r - 1])

    def shifted(i, j):
        picked = [
            padded[(r + 2 - i) * pad_cols + 2 - j : (r + 2 - i) * pad_cols + 2 - j + tile_cols]
            for r in range(tile_rows)
        ]
        return jnp.concatenate(picked, axis=0).reshape(tokens, width)

    inv, normed = norm(x_in[...].astype(F32))
    inputs = (normed * gain[...]).astype(BF)
    mixed = mixed_in[...].astype(F32)
    extra = []
    conv = jnp.zeros((tokens, width), F32)
    for i in range(3):
        for j in range(3):
            moved = shifted(i, j)
            conv = conv + mix[i, j : j + 1, :] * moved
            extra.append(jnp.sum(mixed * moved, axis=0, keepdims=True))
    grad_mixed = conv.astype(BF)
    grad_att = dot(grad_mixed, wo[...], NT).astype(BF)
    for c in range(cells):
        rows = slice(c * all_members, (c + 1) * all_members)
        sums[rows, :] = dot(grad_att[rows], mat_v[c], NT)

    prob = prob_in[...]
    prob_b = prob.astype(BF)
    grad_prob = sums[...]
    inner = head_sums(prob * grad_prob, headsum)
    grad_score = (prob * (grad_prob - inner) * scale).astype(BF)
    lane_head = lax.broadcasted_iota(jnp.int32, (all_members, width), 1) // head_dim

    def diagonal(full):
        out = jnp.zeros((all_members, width), F32)
        for h in range(HEADS):
            out = jnp.where(lane_head == h, full[h * all_members : (h + 1) * all_members], out)
        return out

    gq_l, gk_l, gv_l = [], [], []
    for c in range(cells):
        rows = slice(c * all_members, (c + 1) * all_members)
        gq_l.append(dot(grad_score[rows], mat_k[c]).astype(BF))
        gk_l.append(diagonal(dot(grad_score[rows], q_in[rows, :], TN)).astype(BF))
        gv_l.append(diagonal(dot(prob_b[rows], grad_att[rows], TN)).astype(BF))
    grad_q = jnp.concatenate(gq_l, axis=0)
    grad_k = jnp.concatenate(gk_l, axis=0)
    grad_v = jnp.concatenate(gv_l, axis=0)

    grad_in = dot(grad_q, wq[...], NT) + dot(grad_k, wk[...], NT) + dot(grad_v, wv[...], NT)
    extra.append(jnp.sum(grad_in * normed, axis=0, keepdims=True))
    grad_normed = grad_in * gain[...]
    mean = jnp.mean(grad_normed * normed, axis=-1, keepdims=True)
    grad = (shifted(1, 1) + inv * (grad_normed - normed * mean)).astype(BF)
    for g in range(cells // 8):
        back = dot(gather8[...], grad[g * 256 : (g + 1) * 256], TN).astype(BF)
        send[:, g * 32 : (g + 1) * 32, :] = back.reshape(parts, 32, width)

    weights = [
        dot(inputs, grad_q, TN),
        dot(inputs, grad_k, TN),
        dot(inputs, grad_v, TN),
        dot(att_in[...], grad_mixed, TN),
    ]
    shard = 4 * width // parts
    for j in range(parts):
        which, start = divmod(j * shard, width)
        send[j, base : base + shard, :] = weights[which][start : start + shard].astype(BF)
    extras = jnp.concatenate(extra + [jnp.zeros((16 - len(extra), width), F32)], axis=0).astype(BF)
    for j in range(parts):
        send[j, base + shard : base + shard + 16, :] = extras


def unpack_kernel(recv, out):
    members, rows, cols, width = out.shape
    parts = recv.shape[0]
    per = cols // parts * members
    split = split_matrix(parts, members, cols)
    for r in range(rows):
        tokens = recv[:, r * per : (r + 1) * per, :].reshape(parts * per, width)
        out[:, r] = dot(split, tokens, TN).astype(BF).reshape(members, cols, width)


def finish_kernel(scale, place, same_core, other_core, total, g_q, g_k, g_v, g_o, g_mix, g_gain):
    count, shard, width = same_core.shape
    per = width // shard
    outs = (g_q, g_k, g_v, g_o)
    for p in range(2 * count):
        code = lax.bitwise_xor(place[0], p)
        spot = lax.shift_right_logical(code, 1)
        got = jnp.where(code == 2 * spot, same_core[spot], other_core[spot]).astype(F32)
        outs[p // per][p % per * shard : (p % per + 1) * shard, :] = got * scale
    rest = total[shard:, :].astype(F32) * scale
    for i in range(3):
        g_mix[i] = rest[3 * i : 3 * i + 3]
    g_gain[...] = rest[9:10]


def partner(axis, code):
    return [(i, i ^ code) for i in range(lax.axis_size(axis))]


def meet(values, axis, codes):
    got = [values] + [lax.ppermute(values, axis, partner(axis, k)) for k in codes]
    got = [x.astype(F32) for x in got]
    while len(got) > 1:
        got = [a + b for a, b in zip(got[::2], got[1::2])]
    return lax.optimization_barrier(got[0].astype(BF))


def near(x):
    return pltpu.with_memory_space_constraint(x, pltpu.VMEM)


def swap(last, first, spot, axis, where, wrap):
    size = len(where)
    got = []
    for odd in (0, 1):
        pairs = []
        for a in range(odd, size if wrap else size - 1, 2):
            b = (a + 1) % size
            pairs += [(where[a], where[b]), (where[b], where[a])]
        got.append(lax.ppermute(jnp.where(spot % 2 == odd, last, first), axis, pairs))
    even = spot % 2 == 0
    return jnp.where(even, got[0], got[1]), jnp.where(even, got[1], got[0])


def local(fields, norm_gain, w_query, w_key, w_value, w_out, mix_kernel, cotangent):
    members, rows, cols, width = fields.shape
    parts = lax.axis_size("mem")
    per = cols // parts
    cells = rows * per
    tokens = cells * members * parts
    base = cells * members
    shard = 4 * width // parts
    grid = (lax.axis_size("row"), lax.axis_size("col"))
    params = pltpu.CompilerParams(vmem_limit_bytes=40 * 1024 * 1024)
    smem = pl.BlockSpec(memory_space=pltpu.SMEM)
    vmem = pl.BlockSpec(memory_space=pltpu.VMEM)
    gather8 = jnp.asarray(gather_matrix(parts, 8, members), BF)
    headsum = jnp.asarray(np.kron(np.eye(HEADS), np.ones((width // HEADS, width // HEADS))), BF)
    gain = norm_gain.reshape(1, width)
    blocks = parts * grid[1]
    block = lax.axis_index("col") * parts + snake(lax.axis_index("mem"), parts)
    place = jnp.stack([lax.axis_index("row"), block]).astype(jnp.int32)

    with jax.named_scope("pack"):
        send = pl.pallas_call(
            pack_kernel,
            out_shape=pltpu.VMEM((parts, 2 * base, width), BF),
            compiler_params=params,
        )(fields, cotangent)
    with jax.named_scope("to_cells"):
        recv = lax.all_to_all(send, "mem", 0, 0)
    with jax.named_scope("order"):
        x, cot = pl.pallas_call(
            functools.partial(order_kernel, members),
            out_shape=(pltpu.VMEM((tokens, width), BF), pltpu.VMEM((rows, per, parts * members, width), BF)),
            compiler_params=params,
        )(near(recv), gather8)
        x, w_query, w_key, w_value, w_out = lax.optimization_barrier((x, w_query, w_key, w_value, w_out))
    with jax.named_scope("halo_cols"):
        where = {}
        for mem in range(parts):
            inner = mem // 2 if mem % 2 == 0 else parts - 1 - mem // 2
            for c in range(grid[1]):
                where[c * parts + inner] = mem * grid[1] + c
        right, left = swap(cot[:, per - 1], cot[:, 0], block, ("mem", "col"), where, True)
    with jax.named_scope("forward"):
        token = pltpu.VMEM((tokens, width), BF)
        token_f = pltpu.VMEM((tokens, width), F32)
        mat = pltpu.VMEM((cells, width, width), BF)
        kept = pl.pallas_call(
            functools.partial(forward_kernel, cells),
            out_shape=(token, token_f, token, token, mat, mat),
            scratch_shapes=[pltpu.VMEM((tokens, width), F32)],
            compiler_params=params,
        )(near(x), gain, w_query, w_key, w_value, w_out, headsum)
    left, right, *kept = lax.optimization_barrier((left, right, *kept))
    with jax.named_scope("halo_rows"):
        top, bottom = [jnp.concatenate([left[r : r + 1], cot[r], right[r : r + 1]], axis=0) for r in (0, rows - 1)]
        rows_at = {r: r for r in range(grid[0])}
        below, above = swap(bottom, top, lax.axis_index("row"), "row", rows_at, False)
    with jax.named_scope("backward"):
        back = pl.pallas_call(
            functools.partial(backward_kernel, (grid[0], blocks)),
            in_specs=[smem] + [vmem] * 20,
            out_shape=pltpu.VMEM((parts, base + shard + 16, width), BF),
            scratch_shapes=[
                pltpu.VMEM(((rows + 2) * (per + 2), members * parts, width), F32),
                pltpu.VMEM((tokens, width), F32),
            ],
            compiler_params=params,
        )(
            place,
            *[near(a) for a in (cot, left, right, above, below, x, *kept)],
            gain,
            mix_kernel,
            w_query,
            w_key,
            w_value,
            w_out,
            gather8,
            headsum,
        )
    with jax.named_scope("to_members"):
        landed = lax.all_to_all(back, "mem", 0, 0)
    with jax.named_scope("unpack"):
        total = jnp.sum(landed[:, base:, :].astype(F32), axis=0)
        total = lax.optimization_barrier(total.astype(BF))
        grad_fields = pl.pallas_call(
            unpack_kernel,
            out_shape=jax.ShapeDtypeStruct(fields.shape, BF),
            compiler_params=params,
        )(near(landed))

    with jax.named_scope("reduce"):
        total = meet(total, "row", (1, 2, 3))
        total = meet(total, "col", (2, 6, 4))
        total = meet(total, "col", (1,))
        total, grad_fields = lax.optimization_barrier((total, grad_fields))
        piece = total[:shard]
        same_core = jnp.stack([piece] + [lax.ppermute(piece, "mem", partner("mem", k)) for k in (2, 4, 6)])
        same_core = lax.optimization_barrier(same_core)
        other_core = lax.ppermute(same_core, "mem", partner("mem", 1))

    scale_all = 1.0 / math.sqrt(tokens * grid[0] * grid[1] * parts)
    with jax.named_scope("finish"):
        square = jax.ShapeDtypeStruct((width, width), F32)
        own = lax.axis_index("mem").astype(jnp.int32).reshape(1)
        grads = pl.pallas_call(
            functools.partial(finish_kernel, scale_all),
            in_specs=[smem] + [vmem] * 3,
            out_shape=(square,) * 4 + (jax.ShapeDtypeStruct((3, 3, width), F32), jax.ShapeDtypeStruct((1, width), F32)),
            compiler_params=params,
        )(own, near(same_core), near(other_core), near(total))
    return (grad_fields, grads[5].reshape(width)) + tuple(grads[:5])


def solution(mesh):
    tile = P("mem", "row", "col", None)
    in_specs = (tile, P(), P(), P(), P(), P(), P(), tile)
    out_specs = (tile, P(), P(), P(), P(), P(), P())
    return jax.shard_map(local, mesh=mesh, in_specs=in_specs, out_specs=out_specs, check_vma=False)
```
